32 devices in a mesh: slab: 4 (over y, x), dom: 8 (over z, core).
Axes of the slice: x: 2, y: 2, z: 4, core: 2. Of those that a mesh axis runs over, the one named last changes fastest.
Arguments:
- positions: float32 [3, 32768], P(None, ('slab', 'dom')), may hold values from 0 to 8, as said below
- velocities: float32 [3, 32768], P(None, ('slab', 'dom')), may hold values from -3 to 3
- mass: float32 [32768], P(('slab', 'dom')), may hold values from 0.005 to 0.012
- smoothing: float32 [32768], P(('slab', 'dom')), may hold values from 0.25 to 0.4
- energy: float32 [32768], P(('slab', 'dom')), may hold values from 0.5 to 32, as said below
- send_offsets: int32 [4, 32], P(None, ('slab', 'dom')), may hold values from 0 to 7, as said below
- send_counts: int32 [4, 32], P(None, ('slab', 'dom')), may hold values from 1 to 8, as said below
- pair_blocks: int32 [8, 256], P(None, ('slab', 'dom')), may hold values from 0 to 40, as said below
Outputs:
- density: float32 [32768], P(('slab', 'dom'))
- acceleration: float32 [3, 32768], P(None, ('slab', 'dom'))
- heating: float32 [32768], P(('slab', 'dom'))
- step_share: float32 [32768], P(('slab', 'dom'))
The draws below stay inside these ranges and needn't reach their ends.
Inputs may be any that keep to these rules, and one draw needn't show every extreme that they name: `positions`: particle i of block g lies in the unit cube whose lowest corner is (slab index, domain index, local block index) of g. `energy`: largest near the middle of the box. `send_offsets`: offset plus count never passes 8. `send_counts`: some window holds all 8 blocks in every draw. `pair_blocks`: the first entry of each list is the block itself; an entry 8 (1 + r) + t names only a slot t below the count of the window received from direction r; 40 names no block; no other entry repeats within a list.
All inputs are finite; a program needn't handle non-finite values.
Results may differ from the reference program's by a relative error of at most 0.0003.
Values sent between devices are 32-bit elements; how exact they have to be, the bound alone decides.
No kernel may reach another device: no remote copies, remote signals or barrier semaphores. Data moves between devices by JAX's collectives and lax.ppermute only.
A program may use at most 64 MiB of HBM per device.

```python
import math
import jax
import jax.numpy as jnp
from jax import lax

BLOCKS = 8
BLOCK_PTS = 128
NEIGH_BLOCKS = 8
SLABS = 4
DOMAINS = 8
DEVCOUNT = 32
PARTICLES = 32768


def cell_corner():
    index = jnp.arange(PARTICLES, dtype=jnp.int32)
    block = index // BLOCK_PTS
    device = block // BLOCKS
    local_block = block % BLOCKS
    return jnp.stack([device // DOMAINS, device % DOMAINS, local_block]).astype(jnp.float32)


def window_plan(key):
    base = jax.random.fold_in(key, 4242)
    key_count, key_offset = jax.random.split(base)
    counts = jax.random.randint(key_count, (4, DEVCOUNT), 1, BLOCKS + 1)
    counts = counts.at[1, 0].set(BLOCKS)
    offsets = jax.random.randint(key_offset, (4, DEVCOUNT), 0, BLOCKS - counts + 1)
    return (offsets.astype(jnp.int32), counts.astype(jnp.int32))


def draw_send_offsets(key, part):
    return window_plan(key)[0]


def draw_send_counts(key, part):
    return window_plan(key)[1]


def draw_pair_blocks(key, part):
    offsets, counts = window_plan(key)
    devices = jnp.arange(DEVCOUNT, dtype=jnp.int32)
    slab_index = devices // DOMAINS
    dom_index = devices % DOMAINS
    local = jnp.arange(BLOCKS, dtype=jnp.int32)
    peers = ((slab_index - 1, dom_index, 1, slab_index > 0), (slab_index + 1, dom_index, 0, slab_index < SLABS - 1), (slab_index, dom_index - 1, 3, dom_index > 0), (slab_index, dom_index + 1, 2, dom_index < DOMAINS - 1))
    shape = (DEVCOUNT, BLOCKS)
    own_ids = jnp.broadcast_to(local[None, :], shape)
    candidates = [(own_ids, jnp.ones(shape, bool))]
    faces = []
    edges = []
    for rank, (peer_slab, peer_dom, direction, exists) in enumerate(peers):
        peer = jnp.clip(peer_slab, 0, SLABS - 1) * DOMAINS + jnp.clip(peer_dom, 0, DOMAINS - 1)
        start = offsets[direction][peer][:, None]
        filled = counts[direction][peer][:, None]
        for shift in (0, -1, 1):
            slot = own_ids + shift - start
            valid = exists[:, None] & (slot >= 0) & (slot < filled)
            entry = (BLOCKS * (1 + rank) + slot, valid)
            if shift == 0:
                faces.append(entry)
            else:
                edges.append(entry)
    candidates = candidates + faces
    candidates.append((own_ids - 1, own_ids >= 1))
    candidates.append((own_ids + 1, own_ids < BLOCKS - 1))
    candidates = candidates + edges
    ids = jnp.stack([entry[0] for entry in candidates], axis=-1)
    valid = jnp.stack([entry[1] for entry in candidates], axis=-1)
    priority = jnp.arange(ids.shape[-1], dtype=jnp.int32)
    score = jnp.where(valid, priority, priority + 100)
    order = jnp.argsort(score, axis=-1, stable=True)[:, :, :NEIGH_BLOCKS]
    chosen = jnp.take_along_axis(ids, order, axis=-1)
    chosen_valid = jnp.take_along_axis(valid, order, axis=-1)
    result = jnp.where(chosen_valid, chosen, 5 * BLOCKS).astype(jnp.int32)
    return result.reshape(DEVCOUNT * BLOCKS, NEIGH_BLOCKS).T


def draw_positions(key, part):
    corner = cell_corner()
    base = jax.random.fold_in(key, 17)
    offset = jax.random.uniform(base, corner.shape, jnp.float32)
    return corner + offset


def draw_energy(key, part):
    corner = cell_corner()
    centre = jnp.array([SLABS / 2.0, DOMAINS / 2.0, BLOCKS / 2.0], jnp.float32)
    dist_sq = jnp.sum((corner + 0.5 - centre[:, None]) ** 2, axis=0)
    base_key = jax.random.fold_in(key, 29)
    base = jnp.exp(jax.random.uniform(base_key, (PARTICLES,), jnp.float32, jnp.log(0.5), jnp.log(2.0)))
    strength = 9.0
    return base * (1.0 + strength * jnp.exp(-dist_sq / 18.0))


def steps_of(key, dims, cuts, smallest, top_value):
    level = 1.0
    for position, blocks in cuts:
        steps = jax.random.uniform(jax.random.fold_in(jax.random.fold_in(key, 6), position), (blocks,), jnp.float32, smallest / len(cuts), top_value / len(cuts))
        level = level * jnp.repeat(jnp.exp(steps), dims[position] // blocks).reshape((-1,) + (1,) * (len(dims) - 1 - position))
    return level


def noise(key, dims, width, reach, cuts=(), kind=jnp.bfloat16):
    gain = steps_of(key, dims, cuts, -0.22, 0.18) if cuts else 1.0
    values = jax.random.normal(key, dims, jnp.float32) * width * gain
    return jnp.minimum(jnp.maximum(values, -reach), reach).astype(kind)


def setup_inputs(seed: int = 0) -> dict:
    key_of = jax.random.split(jax.random.key(seed), 9)
    positions = draw_positions(jax.random.fold_in(key_of[8], 71), 0)
    velocities = noise(key_of[1], (3, PARTICLES), 0.5, 3.0, ((1, 32),), jnp.float32)
    mass = jnp.clip(jnp.exp(math.log(0.012) - 0.8754688 * jax.random.uniform(key_of[2], (PARTICLES,), jnp.float32) ** steps_of(key_of[2], (PARTICLES,), ((0, 32),), -0.2, 0.2)), 0.005, 0.012)
    smoothing = jnp.clip(jnp.exp(math.log(0.4) - 0.47000364 * jax.random.uniform(key_of[3], (PARTICLES,), jnp.float32) ** steps_of(key_of[3], (PARTICLES,), ((0, 32),), -0.2, 0.2)), 0.25, 0.4)
    energy = draw_energy(jax.random.fold_in(key_of[8], 71), 0)
    send_offsets = draw_send_offsets(jax.random.fold_in(key_of[8], 71), 0)
    send_counts = draw_send_counts(jax.random.fold_in(key_of[8], 71), 0)
    pair_blocks = draw_pair_blocks(jax.random.fold_in(key_of[8], 71), 0)
    return {"positions": positions, "velocities": velocities, "mass": mass, "smoothing": smoothing, "energy": energy, "send_offsets": send_offsets, "send_counts": send_counts, "pair_blocks": pair_blocks}


gas_gamma = 5.0 / 3.0
visc_alpha = 1.0
visc_beta = 2.0
courant = 0.4
index_pairs = ((0, 0), (1, 1), (2, 2), (0, 1), (0, 2), (1, 2))

def kernel(distance, length):
    ratio = distance / length
    shape = 0.25 * jnp.maximum(2.0 - ratio, 0.0) ** 3 - jnp.maximum(1.0 - ratio, 0.0) ** 3
    return shape / (math.pi * length ** 3)

def apply_matrix(matrix, vector):
    return jnp.stack([matrix[0] * vector[0] + matrix[3] * vector[1] + matrix[4] * vector[2], matrix[3] * vector[0] + matrix[1] * vector[1] + matrix[5] * vector[2], matrix[4] * vector[0] + matrix[5] * vector[1] + matrix[2] * vector[2]])

def block_density(pos_own, len_own, pos_near, mass_near):
    separation = pos_near[:, :, None] - pos_own[:, None, :]
    dist_sq = lax.optimization_barrier(jnp.sum(separation * separation, axis=0))
    weight = mass_near[:, None] * kernel(jnp.sqrt(dist_sq), len_own[None, :])
    dens = lax.optimization_barrier(jnp.sum(weight, axis=0))
    moments = [lax.optimization_barrier(jnp.sum(weight * separation[first] * separation[second], axis=0)) / dens for first, second in index_pairs]
    floor = 0.05 * len_own * len_own
    axx = moments[0] + floor
    ayy = moments[1] + floor
    azz = moments[2] + floor
    axy, axz, ayz = (moments[3], moments[4], moments[5])
    cof_xx = ayy * azz - ayz * ayz
    cof_yy = axx * azz - axz * axz
    cof_zz = axx * ayy - axy * axy
    cof_xy = axz * ayz - axy * azz
    cof_xz = axy * ayz - ayy * axz
    cof_yz = axy * axz - axx * ayz
    determinant = axx * cof_xx + axy * cof_xy + axz * cof_xz
    matrix = jnp.stack([cof_xx, cof_yy, cof_zz, cof_xy, cof_xz, cof_yz]) / determinant
    return (dens, matrix)

def block_momentum(own_fields, near_fields):
    separation = near_fields[0:3, :, None] - own_fields[0:3, None, :]
    dist_sq = lax.optimization_barrier(jnp.sum(separation * separation, axis=0))
    mean_len = 0.5 * (near_fields[7][:, None] + own_fields[7][None, :])
    kernel_val = kernel(jnp.sqrt(dist_sq), mean_len)
    grad_own = apply_matrix(own_fields[11:17, None, :], separation) * kernel_val
    grad_near = apply_matrix(near_fields[11:17, :, None], separation) * kernel_val
    grad_sum = grad_own + grad_near
    rel_vel = own_fields[4:7, None, :] - near_fields[4:7, :, None]
    closing = jnp.minimum(-lax.optimization_barrier(jnp.sum(rel_vel * separation, axis=0)), 0.0)
    closing_rate = mean_len * closing / (dist_sq + 0.01 * mean_len * mean_len)
    mean_sound = 0.5 * (own_fields[8][None, :] + near_fields[8][:, None])
    mean_dens = 0.5 * (own_fields[10][None, :] + near_fields[10][:, None])
    viscous = (-visc_alpha * mean_sound * closing_rate + visc_beta * closing_rate * closing_rate) / mean_dens
    near_mass = near_fields[3][:, None]
    press_own = own_fields[9][None, :]
    press_near = near_fields[9][:, None]
    acceleration = -lax.optimization_barrier(jnp.sum(near_mass * (press_own * grad_own + press_near * grad_near + 0.5 * viscous * grad_sum), axis=1))
    heating = own_fields[9] * lax.optimization_barrier(jnp.sum(near_mass * lax.optimization_barrier(jnp.sum(rel_vel * grad_own, axis=0)), axis=0))
    heating = heating + 0.25 * lax.optimization_barrier(jnp.sum(near_mass * viscous * lax.optimization_barrier(jnp.sum(rel_vel * grad_sum, axis=0)), axis=0))
    signal = lax.optimization_barrier(jnp.max(own_fields[8][None, :] + near_fields[8][:, None] - 3.0 * closing_rate, axis=0))
    return (acceleration, heating, signal)

def reference(positions, velocities, mass, smoothing, energy, send_offsets, send_counts, pair_blocks):
    total_blocks = DEVCOUNT * BLOCKS
    devices = jnp.arange(DEVCOUNT, dtype=jnp.int32)
    slab_index = devices // DOMAINS
    dom_index = devices % DOMAINS
    slots = jnp.arange(BLOCKS, dtype=jnp.int32)
    peers = ((slab_index - 1, dom_index, 1, slab_index > 0), (slab_index + 1, dom_index, 0, slab_index < SLABS - 1), (slab_index, dom_index - 1, 3, dom_index > 0), (slab_index, dom_index + 1, 2, dom_index < DOMAINS - 1))
    columns = [devices[:, None] * BLOCKS + slots[None, :]]
    for peer_slab, peer_dom, direction, exists in peers:
        peer = (jnp.clip(peer_slab, 0, SLABS - 1) * DOMAINS + jnp.clip(peer_dom, 0, DOMAINS - 1)).astype(jnp.int32)
        start = send_offsets[direction][peer]
        filled = send_counts[direction][peer]
        valid = exists[:, None] & (slots[None, :] < filled[:, None])
        columns.append(jnp.where(valid, peer[:, None] * BLOCKS + start[:, None] + slots[None, :], total_blocks).astype(jnp.int32))
    columns.append(jnp.full((DEVCOUNT, 1), total_blocks, jnp.int32))
    table_ids = jnp.concatenate(columns, axis=1)
    owner = jnp.arange(total_blocks, dtype=jnp.int32) // BLOCKS
    global_ids = table_ids[owner[None, :], pair_blocks]
    device_ids = global_ids.T.reshape(DEVCOUNT, BLOCKS, -1).astype(jnp.int32)

    def padded(fields):
        shaped = fields.reshape(fields.shape[0], total_blocks, BLOCK_PTS)
        empty = jnp.zeros((fields.shape[0], 1, BLOCK_PTS), jnp.float32)
        return jnp.concatenate([shaped, empty], axis=1)

    def per_device(fields):
        return fields.reshape(fields.shape[0], DEVCOUNT, BLOCKS, BLOCK_PTS).transpose(1, 2, 0, 3)

    def gather_near(table, ids):
        picked = table[:, ids]
        return picked.transpose(1, 0, 2, 3).reshape(ids.shape[0], table.shape[0], -1)
    table_first = padded(jnp.concatenate([positions, mass[None]], axis=0))

    def density_device(item):
        own_fields, ids = item
        near = gather_near(table_first, ids)
        return jax.vmap(block_density)(own_fields[:, 0:3], own_fields[:, 3], near[:, 0:3], near[:, 3])
    dens_parts, matrix_parts = lax.map(density_device, (per_device(jnp.concatenate([positions, smoothing[None]], axis=0)), device_ids))
    density = dens_parts.reshape(-1)
    matrices = matrix_parts.transpose(2, 0, 1, 3).reshape(6, -1)
    pressure = (gas_gamma - 1.0) * energy / density
    sound = jnp.sqrt(gas_gamma * (gas_gamma - 1.0) * energy)
    all_fields = jnp.concatenate([positions, mass[None], velocities, smoothing[None], sound[None], pressure[None], density[None], matrices], axis=0)
    table_all = padded(all_fields)

    def momentum_device(item):
        own_fields, ids = item
        near = gather_near(table_all, ids)
        return jax.vmap(block_momentum)(own_fields, near)
    accel_parts, heat_parts, signal_parts = lax.map(momentum_device, (per_device(all_fields), device_ids))
    acceleration = accel_parts.transpose(2, 0, 1, 3).reshape(3, -1)
    heating = heat_parts.reshape(-1)
    allowed = courant * smoothing / signal_parts.reshape(-1)
    step = jnp.min(allowed)
    return (density, acceleration, heating, step / allowed)
```

```python
import functools
import math

import jax
import jax.numpy as jnp
from jax import lax
from jax.experimental import pallas as pl
from jax.experimental.pallas import tpu as pltpu
from jax.sharding import PartitionSpec as P

gas_gamma = 5.0 / 3.0
courant = 0.4
f32 = jnp.float32
bf16 = jnp.bfloat16
rows = 8
lanes = 128
tiny = 1e-12
swaps = (("dom", 0, 2), ("slab", 0, 0), ("dom", 1, 2), ("slab", 1, 0))
vmem_spec = pl.BlockSpec(memory_space=pltpu.VMEM)
smem_spec = pl.BlockSpec(memory_space=pltpu.SMEM)


def partner(axis, odd, base):
    place = lax.axis_index(axis)
    size = lax.axis_size(axis)
    upward = lax.rem(place + odd, 2) == 0
    direction = base + jnp.where(upward, 1, 0)
    exists = jnp.where(upward, place < size - 1, place > 0)
    return direction, exists


def swap(value, axis, odd):
    size = lax.axis_size(axis)
    pairs = [
        (i, (i + 1) % size if (i - odd) % 2 == 0 else (i - 1) % size) for i in range(size)
    ]
    return lax.ppermute(value, axis, pairs)


def split2(value):
    high = value.astype(bf16)
    low = (value - high.astype(f32)).astype(bf16)
    return high, low


def split3(value):
    first = value.astype(bf16).astype(f32)
    rest = value - first
    second = rest.astype(bf16).astype(f32)
    return first, second, rest - second


def row_ids():
    return lax.broadcasted_iota(jnp.int32, (rows, lanes), 0)


def centre_of(tile):
    corner = jnp.floor(tile[:, 0:1]) + 0.5
    return jnp.where(row_ids() < 3, jnp.broadcast_to(corner, tile.shape), 0.0)


def sum_xyz(tile, start):
    return tile[start : start + 1] + tile[start + 1 : start + 2] + tile[start + 2 : start + 3]


def placed(tile, at, row):
    return jnp.where(row_ids() == at, jnp.broadcast_to(row, tile.shape), tile)


def near_operand(tile):
    norm = sum_xyz(tile * tile, 0)
    drift = (
        tile[0:1] * tile[4:5] + tile[1:2] * tile[5:6] + tile[2:3] * tile[6:7]
    )
    first, second, third = split3(placed(placed(tile, 3, norm), 7, drift))
    ones = jnp.where(row_ids() < 3, 1.0, 0.0)
    stacked = [first, second, third, first, second, first, ones, jnp.zeros_like(ones)]
    return jnp.concatenate(stacked, axis=0).astype(bf16)


def own_operand(tile, own_term):
    first, second, third = split3(tile)
    parts = split3(own_term)
    ones = jnp.zeros((rows, lanes), f32)
    for at in range(3):
        ones = placed(ones, at, parts[at])
    stacked = [first, first, first, second, second, third, ones, jnp.zeros_like(ones)]
    return jnp.concatenate(stacked, axis=0).T.astype(bf16)


def own_distance(tile, scale):
    norm = sum_xyz(tile * tile, 0)
    ids = row_ids()
    left = jnp.where(ids < 3, -2.0 * tile, jnp.where(ids == 3, 1.0, 0.0))
    if scale is None:
        return own_operand(left, norm)
    return own_operand(left * scale, norm * scale)


def own_closing(tile, scale):
    drift = (
        tile[0:1] * tile[4:5] + tile[1:2] * tile[5:6] + tile[2:3] * tile[6:7]
    )
    ids = row_ids()
    left = jnp.concatenate([-tile[4:8], -tile[0:4]], axis=0)
    left = jnp.where(ids == 3, 0.0, jnp.where(ids == 7, 1.0, left))
    return own_operand(left * scale, drift * scale)


def fill_table(own, received, table, width):
    table[0 : 8 * width, :] = own[0 : 8 * width, :]
    for message, (axis, odd, base) in zip(received, swaps):
        direction, _ = partner(axis, odd, base)
        start = pl.multiple_of((direction + 1) * (8 * width), 8 * width)
        table[pl.ds(start, 8 * width), :] = message[0 : 8 * width, :]
    table[40 * width : 40 * width + 8, :] = jnp.zeros((8, lanes), f32)


def fill_mass(own, received, masses):
    masses[0:8, :] = own[64:72, :]
    for message, (axis, odd, base) in zip(received, swaps):
        direction, _ = partner(axis, odd, base)
        start = pl.multiple_of((direction + 1) * 8, 8)
        masses[pl.ds(start, 8), :] = message[64:72, :]
    masses[40:48, :] = jnp.zeros((8, lanes), f32)


def tile_at(table, entry):
    return table[pl.ds(pl.multiple_of(entry * rows, rows), rows), :]


def cut_windows(offsets, counts, source, outgoing, masses):
    for target, (axis, odd, base) in zip(outgoing, swaps):
        direction, exists = partner(axis, odd, base)
        offset = offsets[direction, 0]
        count = jnp.where(exists, counts[direction, 0], 0)
        for slot in range(8):
            block = jnp.minimum(offset + slot, 7)
            keep = slot < count
            tile = tile_at(source, block)
            target[slot * rows : (slot + 1) * rows, :] = jnp.where(keep, tile, 0.0)
            if masses:
                row = source[pl.ds(64 + block, 1), :]
                target[64 + slot : 65 + slot, :] = jnp.where(keep, row, 0.0)


def pack_kernel(positions, velocities, mass, smoothing, energy, offsets, counts, own, *outgoing):
    sound = jnp.sqrt(gas_gamma * (gas_gamma - 1.0) * energy[...])
    for block in range(8):
        part = slice(block * lanes, (block + 1) * lanes)
        at = block * rows
        own[at : at + 3, :] = positions[:, part]
        own[at + 3 : at + 4, :] = smoothing[block : block + 1, :]
        own[at + 4 : at + 7, :] = velocities[:, part]
        own[at + 7 : at + 8, :] = sound[block : block + 1, :]
    own[64:72, :] = mass[...]
    cut_windows(offsets, counts, own, outgoing, True)


def signal_kernel(pairs, own, m0, m1, m2, m3, allowed, smallest, table, near, dots, best):
    fill_table(own, (m0, m1, m2, m3), table, rows)

    def block_step(block, _):
        own_tile = tile_at(table, block)
        centre = centre_of(own_tile)
        centred = own_tile - centre
        left = jnp.concatenate([own_distance(centred, None), own_closing(centred, 30.0)], axis=0)
        columns = own_tile.T
        len_own = jnp.broadcast_to(columns[:, 3:4] * 0.05, (lanes, lanes))
        sound_own = jnp.broadcast_to(columns[:, 7:8], (lanes, lanes))
        for k in range(8):
            tile = tile_at(table, pairs[k, block]) - centre
            near[:, k * lanes : (k + 1) * lanes] = near_operand(tile)
        dots[...] = jnp.dot(left, near[...], preferred_element_type=f32)
        for k in range(8):
            tile = tile_at(table, pairs[k, block])
            part = slice(k * lanes, (k + 1) * lanes)
            mean_len = len_own + tile[3:4] * 0.05
            closing = jnp.minimum(dots[lanes:, part], 0.0)
            rate = closing * mean_len / (dots[0:lanes, part] + mean_len * mean_len)
            signal = sound_own + tile[7:8] - rate
            best[...] = signal if k == 0 else jnp.maximum(best[...], signal)
        top = jnp.max(best[...].T, axis=0, keepdims=True)
        allowed[pl.ds(block, 1), :] = courant * own_tile[3:4] / top
        return 0

    lax.fori_loop(0, 8, block_step, 0)
    least = jnp.min(allowed[...], axis=(0, 1), keepdims=True)
    smallest[...] = jnp.broadcast_to(least, (rows, lanes))


def density_kernel(
    pairs, offsets, counts, energy, own, m0, m1, m2, m3, density, second, *rest
):
    outgoing = rest[0:4]
    table, masses, near, feats, dots, weights, sums = rest[4:]
    fill_table(own, (m0, m1, m2, m3), table, rows)
    fill_mass(own, (m0, m1, m2, m3), masses)

    def block_step(block, _):
        own_tile = tile_at(table, block)
        centre = centre_of(own_tile)
        centred = own_tile - centre
        scale = 0.25 / (own_tile[3:4] * own_tile[3:4])
        left = own_distance(centred, scale)
        ids = row_ids()
        for k in range(8):
            entry = pairs[k, block]
            part = slice(k * lanes, (k + 1) * lanes)
            tile = tile_at(table, entry) - centre
            near[:, part] = near_operand(tile)
            weighed = jnp.where(ids == 3, 1.0, tile) * masses[pl.ds(entry, 1), :]
            stacked = jnp.concatenate(
                [weighed, weighed * tile[0:1], weighed * tile[1:2], weighed * tile[2:3]], axis=0
            )
            high, low = split2(stacked)
            feats[0:32, part] = high
            feats[32:64, part] = low
        dots[...] = jnp.dot(left, near[...], preferred_element_type=f32)
        for k in range(8):
            part = slice(k * lanes, (k + 1) * lanes)
            dist_sq = jnp.maximum(dots[:, part], tiny)
            ratio = dist_sq * lax.rsqrt(dist_sq)
            wide = jnp.maximum(1.0 - ratio, 0.0)
            narrow = jnp.maximum(0.5 - ratio, 0.0)
            twice = narrow + narrow
            high, low = split2(wide * wide * wide - twice * twice * narrow)
            weights[0:lanes, part] = high
            weights[lanes:, part] = low
        out = lax.dot_general(
            weights[...], feats[...], (((1,), (1,)), ((), ())), preferred_element_type=f32
        )
        out = (out[0:lanes] + out[lanes:]).T
        sums[pl.ds(pl.multiple_of(block * 32, 32), 32), :] = out[0:32] + out[32:64]
        return 0

    lax.fori_loop(0, 8, block_step, 0)

    def total(field):
        return sums[pl.ds(field, 8, stride=32), :]

    def mine(field):
        return own[pl.ds(field, 8, stride=rows), :]

    length = mine(3)
    place = [mine(a) for a in range(3)]
    place = [value - (jnp.floor(value[:, 0:1]) + 0.5) for value in place]
    whole = total(3)
    dens = whole * (2.0 / math.pi) / (length * length * length)
    first = [total(a) for a in range(3)]
    inverse = 1.0 / whole
    floor = 0.05 * length * length

    def moment(a, b):
        raw = total(8 + 8 * a + b) - place[a] * first[b] - place[b] * first[a]
        return (raw + place[a] * place[b] * whole) * inverse

    axx = moment(0, 0) + floor
    ayy = moment(1, 1) + floor
    azz = moment(2, 2) + floor
    axy, axz, ayz = moment(0, 1), moment(0, 2), moment(1, 2)
    cof_xx = ayy * azz - ayz * ayz
    cof_yy = axx * azz - axz * axz
    cof_zz = axx * ayy - axy * axy
    cof_xy = axz * ayz - axy * azz
    cof_xz = axy * ayz - ayy * axz
    cof_yz = axy * axz - axx * ayz
    inv_det = 1.0 / (axx * cof_xx + axy * cof_xy + axz * cof_xz)
    density[...] = dens
    pressure = (gas_gamma - 1.0) * energy[...] / dens
    fields = [dens, pressure, cof_xx * inv_det, cof_yy * inv_det, cof_zz * inv_det]
    fields += [cof_xy * inv_det, cof_xz * inv_det, cof_yz * inv_det]
    for field in range(8):
        for block in range(8):
            at = block * rows + field
            second[at : at + 1, :] = fields[field][block : block + 1, :]
    cut_windows(offsets, counts, second, outgoing, False)


def momentum_kernel(pairs, own, m0, m1, m2, m3, second, s0, s1, s2, s3, accel, heating, *scratch):
    table, masses, table2, near, feats, dots, weights, sums = scratch
    fill_table(own, (m0, m1, m2, m3), table, rows)
    fill_mass(own, (m0, m1, m2, m3), masses)
    fill_table(second, (s0, s1, s2, s3), table2, rows)
    ids = row_ids()

    def features(tile, extra, mass):
        cols = [
            jnp.concatenate([extra[i : i + 1] for i in picked], axis=0)
            for picked in ((2, 5, 6, 2, 2, 5, 6, 2), (5, 3, 7, 3, 5, 3, 7, 3), (6, 7, 4, 4, 6, 7, 4, 4))
        ]
        heavy = tile * mass
        applied = None
        for axis in range(3):
            operand = jnp.where(ids < 4, tile[axis : axis + 1], tile[4 + axis : 5 + axis])
            term = cols[axis] * operand
            applied = term if applied is None else applied + term
        swirl = (
            applied[0:1] * tile[4:5] + applied[1:2] * tile[5:6] + applied[2:3] * tile[6:7]
        )
        applied = placed(applied, 3, swirl)
        press = extra[1:2] * mass
        parts = [jnp.where(ids == 3, mass, heavy)]
        parts += [heavy * tile[4 + axis : 5 + axis] for axis in range(3)]
        parts += [extra * mass, extra * press, applied * mass, applied * press]
        return jnp.concatenate(parts, axis=0)

    def block_step(block, _):
        own_tile = tile_at(table, block)
        centre = centre_of(own_tile)
        centred = own_tile - centre
        left = jnp.concatenate([own_distance(centred, None), own_closing(centred, 40.0)], axis=0)
        columns = own_tile.T
        columns2 = tile_at(table2, block).T
        len_own = jnp.broadcast_to(columns[:, 3:4] * 0.05, (lanes, lanes))
        sound_own = jnp.broadcast_to(columns[:, 7:8], (lanes, lanes))
        dens_own = jnp.broadcast_to(columns2[:, 0:1], (lanes, lanes))
        for k in range(8):
            entry = pairs[k, block]
            part = slice(k * lanes, (k + 1) * lanes)
            tile = tile_at(table, entry) - centre
            near[:, part] = near_operand(tile)
            high, low = split2(
                features(tile, tile_at(table2, entry), masses[pl.ds(entry, 1), :])
            )
            feats[0:64, part] = high
            feats[64:128, part] = low
        dots[...] = jnp.dot(left, near[...], preferred_element_type=f32)
        for k in range(8):
            entry = pairs[k, block]
            part = slice(k * lanes, (k + 1) * lanes)
            tile = tile_at(table, entry)
            extra = tile_at(table2, entry)
            len_row = tile[3:4] * 0.05
            for start in range(0, lanes, 32):
                chunk = slice(start, start + 32)
                dist_sq = jnp.maximum(dots[chunk, part], tiny)
                dist = dist_sq * lax.rsqrt(dist_sq)
                mean_len = len_own[chunk] + len_row
                inv_len = 1.0 / mean_len
                ratio = dist * inv_len
                wide = jnp.maximum(20.0 - ratio, 0.0) * inv_len
                narrow = jnp.maximum(10.0 - ratio, 0.0) * inv_len
                twice = narrow + narrow
                weight = wide * wide * wide - twice * twice * narrow
                closing = jnp.minimum(dots[lanes + start : lanes + start + 32, part], 0.0)
                rate = closing * mean_len / (dist_sq + mean_len * mean_len)
                viscous = rate * (rate - (sound_own[chunk] + tile[7:8]))
                viscous = viscous / (dens_own[chunk] + extra[0:1])
                high, low = split2(weight)
                weights[start : start + 32, part] = high
                weights[lanes + start : lanes + start + 32, part] = low
                high, low = split2(weight * viscous)
                weights[2 * lanes + start : 2 * lanes + start + 32, part] = high
                weights[3 * lanes + start : 3 * lanes + start + 32, part] = low
        out = lax.dot_general(
            weights[...], feats[...], (((1,), (1,)), ((), ())), preferred_element_type=f32
        )
        plain = (out[0:lanes] + out[lanes : 2 * lanes]).T
        damped = (out[2 * lanes : 3 * lanes] + out[3 * lanes :]).T
        at = pl.multiple_of(block * lanes, lanes)
        sums[pl.ds(at, 64), :] = plain[0:64] + plain[64:]
        sums[pl.ds(at + 64, 64), :] = damped[0:64] + damped[64:]
        return 0

    lax.fori_loop(0, 8, block_step, 0)

    def mine(ref, field):
        return ref[pl.ds(field, 8, stride=rows), :]

    place = [mine(own, a) for a in range(3)]
    place = [value - (jnp.floor(value[:, 0:1]) + 0.5) for value in place]
    speed = [mine(own, 4 + a) for a in range(3)]
    pressure = mine(second, 1)
    order = ((2, 5, 6), (5, 3, 7), (6, 7, 4))
    matrix = [[mine(second, order[a][b]) for b in range(3)] for a in range(3)]

    def pieces(base):
        def total(field):
            return sums[pl.ds(base + field, 8, stride=lanes), :]

        mass = total(3)
        offset = [total(a) - place[a] * mass for a in range(3)]
        mass_v = [total(4 + a) for a in range(3)]
        applied = [
            matrix[a][0] * offset[0] + matrix[a][1] * offset[1] + matrix[a][2] * offset[2]
            for a in range(3)
        ]
        work = None
        for a in range(3):
            for b in range(3):
                cross = speed[a] * offset[b] - total(8 + 8 * a + b) + mass_v[a] * place[b]
                term = matrix[a][b] * cross
                work = term if work is None else work + term
        return total, applied, work

    def near_force(total, matrices, vectors):
        return [
            total(vectors + a)
            - total(matrices + order[a][0]) * place[0]
            - total(matrices + order[a][1]) * place[1]
            - total(matrices + order[a][2]) * place[2]
            for a in range(3)
        ]

    norm = 16.0 / math.pi / 20.0**6
    total, applied, work = pieces(0)
    pushed = near_force(total, 40, 56)
    total2, applied2, work2 = pieces(64)
    pushed2 = near_force(total2, 32, 48)
    for a in range(3):
        value = -norm * (
            pressure * applied[a] + pushed[a] + 0.125 * (applied2[a] + pushed2[a])
        )
        for block in range(8):
            part = slice(block * lanes, (block + 1) * lanes)
            accel[a : a + 1, part] = value[block : block + 1, :]
    near_work = (
        speed[0] * pushed2[0]
        + speed[1] * pushed2[1]
        + speed[2] * pushed2[2]
        - total2(51)
        + place[0] * total2(52)
        + place[1] * total2(53)
        + place[2] * total2(54)
    )
    heating[...] = norm * (pressure * work + 0.0625 * (work2 + near_work))


def call(kernel, outs, scratch, smem, args, flops):
    return pl.pallas_call(
        kernel,
        out_shape=[jax.ShapeDtypeStruct(shape, f32) for shape in outs],
        in_specs=[smem_spec] * smem + [vmem_spec] * (len(args) - smem),
        out_specs=[vmem_spec] * len(outs),
        scratch_shapes=[pltpu.VMEM(shape, kind) for shape, kind in scratch],
        compiler_params=pltpu.CompilerParams(vmem_limit_bytes=24 * 1024 * 1024),
        cost_estimate=pl.CostEstimate(flops=flops, bytes_accessed=200000, transcendentals=0),
    )(*args)


def body(positions, velocities, mass, smoothing, energy, send_offsets, send_counts, pair_blocks):
    points = positions.shape[1]
    packed = (72, lanes)
    energy = energy.reshape(8, lanes)
    own, *outgoing = pl.pallas_call(
        pack_kernel,
        out_shape=[jax.ShapeDtypeStruct(packed, f32)] * 5,
        in_specs=[vmem_spec] * 5 + [smem_spec] * 2,
        out_specs=[vmem_spec] * 5,
    )(
        positions,
        velocities,
        mass.reshape(8, lanes),
        smoothing.reshape(8, lanes),
        energy,
        send_offsets,
        send_counts,
    )
    received = [swap(value, axis, odd) for value, (axis, odd, _) in zip(outgoing, swaps)]
    table = ((328, lanes), f32)
    masses = ((48, lanes), f32)
    near = ((64, 8 * lanes), bf16)
    allowed, smallest = call(
        signal_kernel,
        [(8, lanes), (rows, lanes)],
        [table, near, ((2 * lanes, 8 * lanes), f32), ((lanes, lanes), f32)],
        1,
        (pair_blocks, own, *received),
        4 * 10**9,
    )
    density, second, *outgoing2 = call(
        density_kernel,
        [(8, lanes), (64, lanes)] + [(64, lanes)] * 4,
        [
            table,
            masses,
            near,
            ((64, 8 * lanes), bf16),
            ((lanes, 8 * lanes), f32),
            ((2 * lanes, 8 * lanes), bf16),
            ((8 * 32, lanes), f32),
        ],
        3,
        (pair_blocks, send_offsets, send_counts, energy, own, *received),
        4 * 10**9,
    )
    received2 = [swap(value, axis, odd) for value, (axis, odd, _) in zip(outgoing2, swaps)]
    accel, heating = call(
        momentum_kernel,
        [(3, points), (8, lanes)],
        [
            table,
            masses,
            table,
            near,
            ((lanes, 8 * lanes), bf16),
            ((2 * lanes, 8 * lanes), f32),
            ((4 * lanes, 8 * lanes), bf16),
            ((8 * lanes, lanes), f32),
        ],
        1,
        (pair_blocks, own, *received, second, *received2),
        8 * 10**9,
    )
    for axis in ("dom", "slab"):
        size = lax.axis_size(axis)
        step = 1
        while step < size:
            moved = lax.ppermute(smallest, axis, [(i, i ^ step) for i in range(size)])
            smallest = jnp.minimum(smallest, moved)
            step *= 2
    share = smallest / allowed
    return (density.reshape(points), accel, heating.reshape(points), share.reshape(points))


def solution(mesh):
    both = ("slab", "dom")
    wide, flat = P(None, both), P(both)
    in_specs = (wide, wide, flat, flat, flat, wide, wide, wide)
    out_specs = (flat, wide, flat, flat)
    return jax.shard_map(body, mesh=mesh, in_specs=in_specs, out_specs=out_specs, check_vma=False)
```

```python
import functools
import math

import jax
import jax.numpy as jnp
from jax import lax
from jax.experimental import pallas as pl
from jax.experimental.pallas import tpu as pltpu
from jax.sharding import PartitionSpec as P

gas_gamma = 5.0 / 3.0
courant = 0.4
f32 = jnp.float32
bf16 = jnp.bfloat16
rows = 8
lanes = 128
tiny = 1e-12
chunk = 32
swaps = (("dom", 0, 2), ("slab", 0, 0), ("dom", 1, 2), ("slab", 1, 0))
vmem_spec = pl.BlockSpec(memory_space=pltpu.VMEM)
smem_spec = pl.BlockSpec(memory_space=pltpu.SMEM)


def partner(axis, odd, base):
    place = lax.axis_index(axis)
    size = lax.axis_size(axis)
    upward = lax.rem(place + odd, 2) == 0
    direction = base + jnp.where(upward, 1, 0)
    exists = jnp.where(upward, place < size - 1, place > 0)
    return direction, exists


def swap(value, axis, odd):
    size = lax.axis_size(axis)
    pairs = [
        (i, (i + 1) % size if (i - odd) % 2 == 0 else (i - 1) % size) for i in range(size)
    ]
    return lax.ppermute(value, axis, pairs)


def split2(value):
    high = value.astype(bf16)
    low = (value - high.astype(f32)).astype(bf16)
    return high, low


def split3(value):
    first = value.astype(bf16).astype(f32)
    rest = value - first
    second = rest.astype(bf16).astype(f32)
    return first, second, rest - second


def row_ids():
    return lax.broadcasted_iota(jnp.int32, (rows, lanes), 0)


def centre_of(tile):
    corner = jnp.floor(tile[:, 0:1]) + 0.5
    return jnp.where(row_ids() < 3, jnp.broadcast_to(corner, tile.shape), 0.0)


def sum_xyz(tile, start):
    return tile[start : start + 1] + tile[start + 1 : start + 2] + tile[start + 2 : start + 3]


def placed(tile, at, row):
    return jnp.where(row_ids() == at, jnp.broadcast_to(row, tile.shape), tile)


def near_operand(tile):
    norm = sum_xyz(tile * tile, 0)
    drift = (
        tile[0:1] * tile[4:5] + tile[1:2] * tile[5:6] + tile[2:3] * tile[6:7]
    )
    first, second, third = split3(placed(placed(tile, 3, norm), 7, drift))
    ones = jnp.where(row_ids() < 3, 1.0, 0.0)
    stacked = [first, second, third, first, second, first, ones, jnp.zeros_like(ones)]
    return jnp.concatenate(stacked, axis=0).astype(bf16)


def own_operand(tile, own_term):
    first, second, third = split3(tile)
    parts = split3(own_term)
    ones = jnp.zeros((rows, lanes), f32)
    for at in range(3):
        ones = placed(ones, at, parts[at])
    stacked = [first, first, first, second, second, third, ones, jnp.zeros_like(ones)]
    return jnp.concatenate(stacked, axis=0)


def own_distance(tile):
    norm = sum_xyz(tile * tile, 0)
    ids = row_ids()
    left = jnp.where(ids < 3, -2.0 * tile, jnp.where(ids == 3, 1.0, 0.0))
    return own_operand(left, norm)


def own_closing(tile, scale):
    drift = (
        tile[0:1] * tile[4:5] + tile[1:2] * tile[5:6] + tile[2:3] * tile[6:7]
    )
    ids = row_ids()
    left = jnp.concatenate([-tile[4:8], -tile[0:4]], axis=0)
    left = jnp.where(ids == 3, 0.0, jnp.where(ids == 7, 1.0, left))
    return own_operand(left * scale, drift * scale)


def fill_table(own, received, table, width):
    table[0 : 8 * width, :] = own[0 : 8 * width, :]
    for message, (axis, odd, base) in zip(received, swaps):
        direction, _ = partner(axis, odd, base)
        start = pl.multiple_of((direction + 1) * (8 * width), 8 * width)
        table[pl.ds(start, 8 * width), :] = message[0 : 8 * width, :]
    table[40 * width : 40 * width + 8, :] = jnp.zeros((8, lanes), f32)


def fill_mass(own, received, masses):
    masses[0:8, :] = own[64:72, :]
    for message, (axis, odd, base) in zip(received, swaps):
        direction, _ = partner(axis, odd, base)
        start = pl.multiple_of((direction + 1) * 8, 8)
        masses[pl.ds(start, 8), :] = message[64:72, :]
    masses[40:48, :] = jnp.zeros((8, lanes), f32)


def tile_at(table, entry):
    return table[pl.ds(pl.multiple_of(entry * rows, rows), rows), :]


def cut_windows(offset_of, count_of, source, outgoing, masses):
    for target, (axis, odd, base) in zip(outgoing, swaps):
        direction, exists = partner(axis, odd, base)
        offset = offset_of(direction)
        count = jnp.where(exists, count_of(direction), 0)
        for slot in range(8):
            block = jnp.minimum(offset + slot, 7)
            keep = slot < count
            tile = tile_at(source, block)
            target[slot * rows : (slot + 1) * rows, :] = jnp.where(keep, tile, 0.0)
            if masses:
                row = source[pl.ds(64 + block, 1), :]
                target[64 + slot : 65 + slot, :] = jnp.where(keep, row, 0.0)


def pack_kernel(positions, velocities, mass, smoothing, energy, offsets, counts, own, *outgoing):
    sound = jnp.sqrt(gas_gamma * (gas_gamma - 1.0) * energy[...])
    for block in range(8):
        part = slice(block * lanes, (block + 1) * lanes)
        at = block * rows
        own[at : at + 3, :] = positions[:, part]
        own[at + 3 : at + 4, :] = smoothing[block : block + 1, :]
        own[at + 4 : at + 7, :] = velocities[:, part]
        own[at + 7 : at + 8, :] = sound[block : block + 1, :]
    own[64:72, :] = mass[...]
    own[72:80, :] = energy[...]
    cut_windows(lambda r: offsets[0, r], lambda r: counts[0, r], own, outgoing, True)


def two_deep(prepare, finish, first=0, last=8):
    prepare(first, 0)

    def step(half, _):
        block = first + half * 2
        prepare(block + 1, 1)
        finish(block, 0)
        prepare(jnp.minimum(block + 2, last - 1), 0)
        finish(block + 1, 1)
        return 0

    lax.fori_loop(0, (last - first) // 2, step, 0)


def own_kernel(own, left, columns, table):
    table[...] = own[...]

    def step(block, _):
        tile = tile_at(own, block)
        centred = tile - centre_of(tile)
        stacked = jnp.concatenate([own_distance(centred), own_closing(centred, 30.0)], axis=0)
        at = pl.ds(pl.multiple_of(block * lanes, lanes), lanes)
        left[at, :] = stacked.T.astype(bf16)
        turned = tile.T
        length = turned[:, 3:4]
        columns[at, 0:lanes] = jnp.broadcast_to(length * 0.05, (lanes, lanes))
        columns[at, lanes : 2 * lanes] = jnp.broadcast_to(turned[:, 7:8] * 0.75, (lanes, lanes))
        columns[at, 2 * lanes :] = jnp.broadcast_to(0.5 / length, (lanes, lanes))
        return 0

    lax.fori_loop(0, 8, step, 0)


def put_near(near, k, tile):
    operand = near_operand(tile)
    at = 2 * k * lanes
    near[0:64, at : at + lanes] = operand
    near[64:128, at + lanes : at + 2 * lanes] = operand


def clear_near(buffers):
    for near in buffers:
        near[...] = jnp.zeros(near.shape, bf16)


def pair_dots(left, near, block, start, k):
    at = pl.ds(pl.multiple_of(block * lanes + start, chunk), chunk)
    part = slice(2 * k * lanes, 2 * (k + 1) * lanes)
    both = jnp.dot(left[at, :], near[:, part], preferred_element_type=f32)
    return both[:, 0:lanes], both[:, lanes:]


def signal_kernel(
    plan, left, columns, own, m0, m1, m2, m3, allowed, smallest, distance, rates, table, *near
):
    clear_near(near)
    fill_table(own, (m0, m1, m2, m3), table, rows)

    def prepare(block, buf):
        centre = centre_of(tile_at(table, block))
        for k in range(8):
            put_near(near[buf], k, tile_at(table, plan[k, block]) - centre)

    def finish(block, buf):
        tops = [None] * (lanes // chunk)
        sounds = None
        for k in range(8):
            tile = tile_at(table, plan[k, block])
            len_row, sound_row = tile[3:4] * 0.05, tile[7:8]
            sounds = sound_row if k == 0 else jnp.maximum(sounds, sound_row)
            part = slice(k * lanes, (k + 1) * lanes)
            for c in range(lanes // chunk):
                start = c * chunk
                at = pl.ds(pl.multiple_of(block * lanes + start, chunk), chunk)
                dist_sq, closing = pair_dots(left, near[buf], block, start, k)
                dist_sq = jnp.maximum(dist_sq, tiny)
                distance[at, part] = dist_sq * lax.rsqrt(dist_sq)
                mean_len = columns[at, 0:lanes] + len_row
                rate = closing * mean_len / (dist_sq + mean_len * mean_len)
                rates[at, part] = rate
                signal = sound_row - rate
                tops[c] = signal if k == 0 else jnp.maximum(tops[c], signal)
        top = jnp.max(jnp.concatenate(tops, axis=0).T, axis=0, keepdims=True)
        top = jnp.maximum(top, jnp.max(sounds, axis=1, keepdims=True))
        own_tile = tile_at(table, block)
        allowed[pl.ds(block, 1), :] = courant * own_tile[3:4] / (own_tile[7:8] + top)

    two_deep(prepare, finish)
    least = jnp.min(allowed[...], axis=(0, 1), keepdims=True)
    smallest[...] = jnp.broadcast_to(least, (rows, lanes))


def density_kernel(
    plan, offsets, counts, columns, distance, own, m0, m1, m2, m3, density, second, *rest
):
    outgoing = rest[0:4]
    table, masses, sums, *scratch = rest[4:]
    feats, weights = scratch[0:2], scratch[2:4]
    fill_table(own, (m0, m1, m2, m3), table, rows)
    fill_mass(own, (m0, m1, m2, m3), masses)

    def prepare(block, buf):
        centre = centre_of(tile_at(table, block))
        ids = row_ids()
        for k in range(8):
            entry = plan[k, block]
            part = slice(k * lanes, (k + 1) * lanes)
            tile = tile_at(table, entry) - centre
            weighed = jnp.where(ids == 3, 1.0, tile) * masses[pl.ds(entry, 1), :]
            stacked = jnp.concatenate(
                [weighed, weighed * tile[0:1], weighed * tile[1:2], weighed * tile[2:3]], axis=0
            )
            high, low = split2(stacked)
            feats[buf][0:32, part] = high
            feats[buf][32:64, part] = low

    def finish(block, buf):
        for start in range(0, lanes, chunk):
            at = pl.ds(pl.multiple_of(block * lanes + start, chunk), chunk)
            scale = columns[at, 2 * lanes :]
            for k in range(8):
                part = slice(k * lanes, (k + 1) * lanes)
                ratio = distance[at, part] * scale
                wide = jnp.maximum(1.0 - ratio, 0.0)
                narrow = jnp.maximum(0.5 - ratio, 0.0)
                twice = narrow + narrow
                high, low = split2(wide * wide * wide - twice * twice * narrow)
                weights[buf][start : start + chunk, part] = high
                weights[buf][lanes + start : lanes + start + chunk, part] = low
        out = lax.dot_general(
            feats[buf][...], weights[buf][...], (((1,), (1,)), ((), ())), preferred_element_type=f32
        )
        out = out[0:32] + out[32:64]
        at = pl.ds(pl.multiple_of(block * 32, 32), 32)
        sums[at, :] = out[:, 0:lanes] + out[:, lanes:]

    two_deep(prepare, finish)

    def total(field):
        return sums[pl.ds(field, 8, stride=32), :]

    def mine(field):
        return own[pl.ds(field, 8, stride=rows), :]

    length = mine(3)
    place = [mine(a) for a in range(3)]
    place = [value - (jnp.floor(value[:, 0:1]) + 0.5) for value in place]
    whole = total(3)
    dens = whole * (2.0 / math.pi) / (length * length * length)
    first = [total(a) for a in range(3)]
    inverse = 1.0 / whole
    floor = 0.05 * length * length

    def moment(a, b):
        raw = total(8 + 8 * a + b) - place[a] * first[b] - place[b] * first[a]
        return (raw + place[a] * place[b] * whole) * inverse

    axx = moment(0, 0) + floor
    ayy = moment(1, 1) + floor
    azz = moment(2, 2) + floor
    axy, axz, ayz = moment(0, 1), moment(0, 2), moment(1, 2)
    cof_xx = ayy * azz - ayz * ayz
    cof_yy = axx * azz - axz * axz
    cof_zz = axx * ayy - axy * axy
    cof_xy = axz * ayz - axy * azz
    cof_xz = axy * ayz - ayy * axz
    cof_yz = axy * axz - axx * ayz
    inv_det = 1.0 / (axx * cof_xx + axy * cof_xy + axz * cof_xz)
    density[...] = dens
    pressure = (gas_gamma - 1.0) * own[72:80, :] / dens
    fields = [dens, pressure, cof_xx * inv_det, cof_yy * inv_det, cof_zz * inv_det]
    fields += [cof_xy * inv_det, cof_xz * inv_det, cof_yz * inv_det]
    for field in range(8):
        for block in range(8):
            at = block * rows + field
            second[at : at + 1, :] = fields[field][block : block + 1, :]
    cut_windows(lambda r: offsets[0, r], lambda r: counts[0, r], second, outgoing, False)


def weight_kernel(
    first, plan, columns, distance, rates, density, own, m0, m1, m2, m3,
    weights, damping, dens_col, table
):
    fill_table(own, (m0, m1, m2, m3), table, rows)

    def step(place, _):
        block = first + place
        turned = jnp.broadcast_to(density[pl.ds(block, 1), :], (lanes, lanes)).T
        dens_col[pl.ds(pl.multiple_of(place * lanes, lanes), lanes), :] = turned
        tiles = [tile_at(table, plan[k, block]) for k in range(8)]
        for start in range(0, lanes, chunk):
            at = pl.ds(pl.multiple_of(block * lanes + start, chunk), chunk)
            to = pl.ds(pl.multiple_of(place * lanes + start, chunk), chunk)
            len_own = columns[at, 0:lanes]
            sound_own = columns[at, lanes : 2 * lanes]
            for k in range(8):
                part = slice(k * lanes, (k + 1) * lanes)
                inv_len = 1.0 / (len_own + tiles[k][3:4] * 0.05)
                ratio = distance[at, part] * inv_len
                wide = jnp.maximum(20.0 - ratio, 0.0) * inv_len
                narrow = jnp.maximum(10.0 - ratio, 0.0) * inv_len
                twice = narrow + narrow
                weight = wide * wide * wide - twice * twice * narrow
                rate = jnp.minimum(rates[at, part], 0.0)
                sounds = sound_own + tiles[k][7:8] * 0.75
                damping[to, part] = weight * rate * (rate - sounds)
                high, low = split2(weight)
                base = pl.multiple_of(place * 2 * lanes + start, chunk)
                weights[pl.ds(base, chunk), part] = high
                weights[pl.ds(base + lanes, chunk), part] = low
        return 0

    lax.fori_loop(0, 4, step, 0, unroll=2)


def momentum_kernel(
    plan, weights_a, damping_a, dens_col_a, weights_b, damping_b, dens_col_b,
    own, m0, m1, m2, m3, second, s0, s1, s2, s3, accel, heating, *scratch
):
    table, masses, table2, sums, *scratch = scratch
    feats, damped = scratch[0:2], scratch[2:4]
    fill_table(own, (m0, m1, m2, m3), table, rows)
    fill_mass(own, (m0, m1, m2, m3), masses)
    fill_table(second, (s0, s1, s2, s3), table2, rows)
    ids = row_ids()

    def features(tile, extra, mass):
        cols = [
            jnp.concatenate([extra[i : i + 1] for i in picked], axis=0)
            for picked in ((2, 5, 6, 2, 2, 5, 6, 2), (5, 3, 7, 3, 5, 3, 7, 3), (6, 7, 4, 4, 6, 7, 4, 4))
        ]
        heavy = tile * mass
        applied = None
        for axis in range(3):
            operand = jnp.where(ids < 4, tile[axis : axis + 1], tile[4 + axis : 5 + axis])
            term = cols[axis] * operand
            applied = term if applied is None else applied + term
        swirl = (
            applied[0:1] * tile[4:5] + applied[1:2] * tile[5:6] + applied[2:3] * tile[6:7]
        )
        applied = placed(applied, 3, swirl)
        press = extra[1:2] * mass
        parts = [jnp.where(ids == 3, mass, heavy)]
        parts += [heavy * tile[4 + axis : 5 + axis] for axis in range(3)]
        parts += [extra * mass, extra * press, applied * mass, applied * press]
        return jnp.concatenate(parts, axis=0)

    def prepare(block, buf):
        centre = centre_of(tile_at(table, block))
        for k in range(8):
            entry = plan[k, block]
            part = slice(k * lanes, (k + 1) * lanes)
            tile = tile_at(table, entry) - centre
            high, low = split2(
                features(tile, tile_at(table2, entry), masses[pl.ds(entry, 1), :])
            )
            feats[buf][0:64, part] = high
            feats[buf][64:128, part] = low

    def finish_part(weights, damping, dens_col, first, block, buf):
        place = block - first
        for start in range(0, lanes, chunk):
            at = pl.ds(pl.multiple_of(place * lanes + start, chunk), chunk)
            for k in range(8):
                dens_row = tile_at(table2, plan[k, block])[0:1]
                part = slice(k * lanes, (k + 1) * lanes)
                high, low = split2(damping[at, part] / (dens_col[at, :] + dens_row))
                damped[buf][start : start + chunk, part] = high
                damped[buf][lanes + start : lanes + start + chunk, part] = low
        own_weights = weights[pl.ds(pl.multiple_of(place * 2 * lanes, lanes), 2 * lanes), :]
        for base, value in ((0, own_weights), (64, damped[buf][...])):
            out = lax.dot_general(
                feats[buf][...], value, (((1,), (1,)), ((), ())), preferred_element_type=f32
            )
            out = out[0:64] + out[64:128]
            at = pl.ds(pl.multiple_of(block * lanes + base, 64), 64)
            sums[at, :] = out[:, 0:lanes] + out[:, lanes:]

    two_deep(prepare, functools.partial(finish_part, weights_a, damping_a, dens_col_a, 0), 0, 4)
    two_deep(prepare, functools.partial(finish_part, weights_b, damping_b, dens_col_b, 4), 4, 8)

    def mine(ref, field):
        return ref[pl.ds(field, 8, stride=rows), :]

    place = [mine(own, a) for a in range(3)]
    place = [value - (jnp.floor(value[:, 0:1]) + 0.5) for value in place]
    speed = [mine(own, 4 + a) for a in range(3)]
    pressure = mine(second, 1)
    order = ((2, 5, 6), (5, 3, 7), (6, 7, 4))
    matrix = [[mine(second, order[a][b]) for b in range(3)] for a in range(3)]

    def pieces(base):
        def total(field):
            return sums[pl.ds(base + field, 8, stride=lanes), :]

        mass = total(3)
        offset = [total(a) - place[a] * mass for a in range(3)]
        mass_v = [total(4 + a) for a in range(3)]
        applied = [
            matrix[a][0] * offset[0] + matrix[a][1] * offset[1] + matrix[a][2] * offset[2]
            for a in range(3)
        ]
        work = None
        for a in range(3):
            for b in range(3):
                cross = speed[a] * offset[b] - total(8 + 8 * a + b) + mass_v[a] * place[b]
                term = matrix[a][b] * cross
                work = term if work is None else work + term
        return total, applied, work

    def near_force(total, matrices, vectors):
        return [
            total(vectors + a)
            - total(matrices + order[a][0]) * place[0]
            - total(matrices + order[a][1]) * place[1]
            - total(matrices + order[a][2]) * place[2]
            for a in range(3)
        ]

    norm = 16.0 / math.pi / 20.0**6
    total, applied, work = pieces(0)
    pushed = near_force(total, 40, 56)
    total2, applied2, work2 = pieces(64)
    pushed2 = near_force(total2, 32, 48)
    for a in range(3):
        value = -norm * (
            pressure * applied[a] + pushed[a] + (2.0 / 9.0) * (applied2[a] + pushed2[a])
        )
        for block in range(8):
            part = slice(block * lanes, (block + 1) * lanes)
            accel[a : a + 1, part] = value[block : block + 1, :]
    near_work = (
        speed[0] * pushed2[0]
        + speed[1] * pushed2[1]
        + speed[2] * pushed2[2]
        - total2(51)
        + place[0] * total2(52)
        + place[1] * total2(53)
        + place[2] * total2(54)
    )
    heating[...] = norm * (pressure * work + (1.0 / 9.0) * (work2 + near_work))


def call(kernel, outs, scratch, smem, args, flops, limit):
    return pl.pallas_call(
        kernel,
        out_shape=[jax.ShapeDtypeStruct(shape, kind) for shape, kind in outs],
        in_specs=[smem_spec] * smem + [vmem_spec] * (len(args) - smem),
        out_specs=[vmem_spec] * len(outs),
        scratch_shapes=[pltpu.VMEM(shape, kind) for shape, kind in scratch],
        compiler_params=pltpu.CompilerParams(vmem_limit_bytes=limit * 1024 * 1024),
        cost_estimate=pl.CostEstimate(flops=flops, bytes_accessed=200000, transcendentals=0),
    )(*args)


def fold(value, axis, step):
    size = lax.axis_size(axis)
    return jnp.minimum(value, lax.ppermute(value, axis, [(i, i ^ step) for i in range(size)]))


def body(positions, velocities, mass, smoothing, energy, send_offsets, send_counts, pair_blocks):
    points = positions.shape[1]
    send_offsets, send_counts = send_offsets.reshape(1, 4), send_counts.reshape(1, 4)
    tile = ((rows, lanes), f32)
    packed = ((72, lanes), f32)
    own, *outgoing = pl.pallas_call(
        pack_kernel,
        out_shape=[jax.ShapeDtypeStruct((80, lanes), f32)] + [jax.ShapeDtypeStruct(*packed)] * 4,
        in_specs=[vmem_spec] * 5 + [smem_spec] * 2,
        out_specs=[vmem_spec] * 5,
    )(
        positions,
        velocities,
        mass.reshape(8, lanes),
        smoothing.reshape(8, lanes),
        energy.reshape(8, lanes),
        send_offsets,
        send_counts,
    )
    received = [swap(value, axis, odd) for value, (axis, odd, _) in zip(outgoing, swaps)]
    steps = [
        (axis, 1 << bit)
        for axis in ("slab", "dom")
        for bit in reversed(range(lax.axis_size(axis).bit_length() - 1))
    ]
    left, columns, own = pl.pallas_call(
        own_kernel,
        out_shape=[
            jax.ShapeDtypeStruct((8 * lanes, lanes), bf16),
            jax.ShapeDtypeStruct((8 * lanes, 3 * lanes), f32),
            jax.ShapeDtypeStruct((80, lanes), f32),
        ],
        in_specs=[vmem_spec],
        out_specs=[vmem_spec] * 3,
        compiler_params=pltpu.CompilerParams(vmem_limit_bytes=8 * 1024 * 1024),
    )(own)
    table = ((328, lanes), f32)
    masses = ((48, lanes), f32)
    near = ((lanes, 16 * lanes), bf16)
    feats = ((64, 8 * lanes), bf16)
    halves = ((2 * lanes, 8 * lanes), bf16)
    square = ((8 * lanes, 8 * lanes), f32)
    allowed, smallest, distance, rates = call(
        signal_kernel,
        [tile, tile, square, square],
        [table, near, near],
        1,
        (pair_blocks, left, columns, own, *received),
        3 * 10**9,
        20,
    )
    smallest = fold(smallest, *steps[0])
    density, second, *outgoing2 = call(
        density_kernel,
        [tile] + [((64, lanes), f32)] * 5,
        [table, masses, ((8 * 32, lanes), f32)] + [feats] * 2 + [halves] * 2,
        3,
        (pair_blocks, send_offsets, send_counts, columns, distance, own, *received),
        5 * 10**9,
        20,
    )
    smallest, outgoing2 = lax.optimization_barrier((smallest, outgoing2))
    received2 = [swap(value, axis, odd) for value, (axis, odd, _) in zip(outgoing2, swaps)]
    parts = []
    for first in (0, 4):
        step, steps_left = steps[1], steps[2:]
        smallest = fold(smallest, *step)
        steps = steps[:1] + steps_left
        weights, damping, dens_col = call(
            functools.partial(weight_kernel, first),
            [((8 * lanes, 8 * lanes), bf16), ((4 * lanes, 8 * lanes), f32), ((4 * lanes, lanes), f32)],
            [table],
            1,
            (pair_blocks, columns, distance, rates, density, own, *received),
            10**8,
            20,
        )
        smallest, distance, weights = lax.optimization_barrier((smallest, distance, weights))
        parts += [weights, damping, dens_col]
    for step in steps[1:-2]:
        smallest = fold(smallest, *step)
    smallest, received2 = lax.optimization_barrier((smallest, received2))
    accel, heating = call(
        momentum_kernel,
        [((3, points), f32), tile],
        [table, masses, table, ((8 * lanes, lanes), f32)]
        + [((lanes, 8 * lanes), bf16)] * 2
        + [halves] * 2,
        1,
        (pair_blocks, *parts, own, *received, second, *received2),
        5 * 10**9,
        20,
    )
    smallest = fold(smallest, *steps[-2])
    smallest, accel = lax.optimization_barrier((smallest, accel))
    smallest = fold(smallest, *steps[-1])
    share = smallest / allowed
    return (density.reshape(points), accel, heating.reshape(points), share.reshape(points))


def solution(mesh):
    both = ("slab", "dom")
    wide, flat = P(None, both), P(both)
    in_specs = (wide, wide, flat, flat, flat, wide, wide, wide)
    out_specs = (flat, wide, flat, flat)
    return jax.shard_map(body, mesh=mesh, in_specs=in_specs, out_specs=out_specs, check_vma=False)
```

```python
import functools
import math

import jax
import jax.numpy as jnp
from jax import lax
from jax.experimental import pallas as pl
from jax.experimental.pallas import tpu as pltpu
from jax.sharding import PartitionSpec as P

gas_gamma = 5.0 / 3.0
courant = 0.4
f32 = jnp.float32
bf16 = jnp.bfloat16
rows = 8
lanes = 128
tiny = 1e-12
chunk = 32
swaps = (("dom", 0, 2), ("slab", 0, 0), ("dom", 1, 2), ("slab", 1, 0))
vmem_spec = pl.BlockSpec(memory_space=pltpu.VMEM)
smem_spec = pl.BlockSpec(memory_space=pltpu.SMEM)


def partner(axis, odd, base):
    place = lax.axis_index(axis)
    size = lax.axis_size(axis)
    upward = lax.rem(place + odd, 2) == 0
    direction = base + jnp.where(upward, 1, 0)
    exists = jnp.where(upward, place < size - 1, place > 0)
    return direction, exists


def swap(value, axis, odd):
    size = lax.axis_size(axis)
    pairs = [
        (i, (i + 1) % size if (i - odd) % 2 == 0 else (i - 1) % size) for i in range(size)
    ]
    return lax.ppermute(value, axis, pairs)


def split2(value):
    high = value.astype(bf16)
    low = (value - high.astype(f32)).astype(bf16)
    return high, low


def split3(value):
    first = value.astype(bf16).astype(f32)
    rest = value - first
    second = rest.astype(bf16).astype(f32)
    return first, second, rest - second


def row_ids():
    return lax.broadcasted_iota(jnp.int32, (rows, lanes), 0)


def centre_of(tile):
    corner = jnp.floor(tile[:, 0:1]) + 0.5
    return jnp.where(row_ids() < 3, jnp.broadcast_to(corner, tile.shape), 0.0)


def sum_xyz(tile, start):
    return tile[start : start + 1] + tile[start + 1 : start + 2] + tile[start + 2 : start + 3]


def placed(tile, at, row):
    return jnp.where(row_ids() == at, jnp.broadcast_to(row, tile.shape), tile)


def near_operand(tile):
    norm = sum_xyz(tile * tile, 0)
    drift = (
        tile[0:1] * tile[4:5] + tile[1:2] * tile[5:6] + tile[2:3] * tile[6:7]
    )
    first, second, third = split3(placed(placed(tile, 3, norm), 7, drift))
    ones = jnp.where(row_ids() < 3, 1.0, 0.0)
    stacked = [first, second, third, first, second, first, ones, jnp.zeros_like(ones)]
    return jnp.concatenate(stacked, axis=0).astype(bf16)


def own_operand(tile, own_term):
    first, second, third = split3(tile)
    parts = split3(own_term)
    ones = jnp.zeros((rows, lanes), f32)
    for at in range(3):
        ones = placed(ones, at, parts[at])
    stacked = [first, first, first, second, second, third, ones, jnp.zeros_like(ones)]
    return jnp.concatenate(stacked, axis=0)


def own_distance(tile):
    norm = sum_xyz(tile * tile, 0)
    ids = row_ids()
    left = jnp.where(ids < 3, -2.0 * tile, jnp.where(ids == 3, 1.0, 0.0))
    return own_operand(left, norm)


def own_closing(tile, scale):
    drift = (
        tile[0:1] * tile[4:5] + tile[1:2] * tile[5:6] + tile[2:3] * tile[6:7]
    )
    ids = row_ids()
    left = jnp.concatenate([-tile[4:8], -tile[0:4]], axis=0)
    left = jnp.where(ids == 3, 0.0, jnp.where(ids == 7, 1.0, left))
    return own_operand(left * scale, drift * scale)


def fill_table(own, received, table, width):
    table[0 : 8 * width, :] = own[0 : 8 * width, :]
    for message, (axis, odd, base) in zip(received, swaps):
        direction, _ = partner(axis, odd, base)
        start = pl.multiple_of((direction + 1) * (8 * width), 8 * width)
        table[pl.ds(start, 8 * width), :] = message[0 : 8 * width, :]
    table[40 * width : 40 * width + 8, :] = jnp.zeros((8, lanes), f32)


def fill_mass(own, received, masses):
    masses[0:8, :] = own[64:72, :]
    for message, (axis, odd, base) in zip(received, swaps):
        direction, _ = partner(axis, odd, base)
        start = pl.multiple_of((direction + 1) * 8, 8)
        masses[pl.ds(start, 8), :] = message[64:72, :]
    masses[40:48, :] = jnp.zeros((8, lanes), f32)


def tile_at(table, entry):
    return table[pl.ds(pl.multiple_of(entry * rows, rows), rows), :]


def cut_windows(offset_of, count_of, source, outgoing, masses):
    for target, (axis, odd, base) in zip(outgoing, swaps):
        direction, exists = partner(axis, odd, base)
        offset = offset_of(direction)
        count = jnp.where(exists, count_of(direction), 0)
        for slot in range(8):
            block = jnp.minimum(offset + slot, 7)
            keep = slot < count
            tile = tile_at(source, block)
            target[slot * rows : (slot + 1) * rows, :] = jnp.where(keep, tile, 0.0)
            if masses:
                row = source[pl.ds(64 + block, 1), :]
                target[64 + slot : 65 + slot, :] = jnp.where(keep, row, 0.0)


def pack_kernel(positions, velocities, mass, smoothing, energy, offsets, counts, own, *outgoing):
    sound = jnp.sqrt(gas_gamma * (gas_gamma - 1.0) * energy[...])
    for block in range(8):
        part = slice(block * lanes, (block + 1) * lanes)
        at = block * rows
        own[at : at + 3, :] = positions[:, part]
        own[at + 3 : at + 4, :] = smoothing[block : block + 1, :]
        own[at + 4 : at + 7, :] = velocities[:, part]
        own[at + 7 : at + 8, :] = sound[block : block + 1, :]
    own[64:72, :] = mass[...]
    own[72:80, :] = energy[...]
    cut_windows(lambda r: offsets[0, r], lambda r: counts[0, r], own, outgoing, True)


def two_deep(prepare, finish, first=0, last=8):
    prepare(first, 0)

    def step(half, _):
        block = first + half * 2
        prepare(block + 1, 1)
        finish(block, 0)
        prepare(jnp.minimum(block + 2, last - 1), 0)
        finish(block + 1, 1)
        return 0

    lax.fori_loop(0, (last - first) // 2, step, 0, unroll=True)


def own_kernel(pairs, own, left, columns, table, plan):
    table[...] = own[...]
    plan[...] = pairs[...]

    def step(block, _):
        tile = tile_at(own, block)
        centred = tile - centre_of(tile)
        stacked = jnp.concatenate([own_distance(centred), own_closing(centred, 30.0)], axis=0)
        at = pl.ds(pl.multiple_of(block * lanes, lanes), lanes)
        left[at, :] = stacked.T.astype(bf16)
        turned = tile.T
        length = turned[:, 3:4]
        columns[at, 0:lanes] = jnp.broadcast_to(length * 0.05, (lanes, lanes))
        columns[at, lanes : 2 * lanes] = jnp.broadcast_to(turned[:, 7:8] * 0.75, (lanes, lanes))
        columns[at, 2 * lanes :] = jnp.broadcast_to(0.5 / length, (lanes, lanes))
        return 0

    lax.fori_loop(0, 8, step, 0)


def put_near(near, k, tile):
    operand = near_operand(tile)
    at = 2 * k * lanes
    near[0:64, at : at + lanes] = operand
    near[64:128, at + lanes : at + 2 * lanes] = operand


def clear_near(buffers):
    for near in buffers:
        near[...] = jnp.zeros(near.shape, bf16)


def pair_dots(left, near, block, start, k):
    at = pl.ds(pl.multiple_of(block * lanes + start, chunk), chunk)
    part = slice(2 * k * lanes, 2 * (k + 1) * lanes)
    both = jnp.dot(left[at, :], near[:, part], preferred_element_type=f32)
    return both[:, 0:lanes], both[:, lanes:]


def signal_kernel(
    plan, left, columns, own, m0, m1, m2, m3, allowed, smallest, distance, rates, table, *near
):
    clear_near(near)
    fill_table(own, (m0, m1, m2, m3), table, rows)

    def prepare(block, buf):
        centre = centre_of(tile_at(table, block))
        for k in range(8):
            put_near(near[buf], k, tile_at(table, plan[k, block]) - centre)

    def finish(block, buf):
        tops = [None] * (lanes // chunk)
        sounds = None
        for k in range(8):
            tile = tile_at(table, plan[k, block])
            len_row, sound_row = tile[3:4] * 0.05, tile[7:8]
            sounds = sound_row if k == 0 else jnp.maximum(sounds, sound_row)
            part = slice(k * lanes, (k + 1) * lanes)
            for c in range(lanes // chunk):
                start = c * chunk
                at = pl.ds(pl.multiple_of(block * lanes + start, chunk), chunk)
                dist_sq, closing = pair_dots(left, near[buf], block, start, k)
                dist_sq = jnp.maximum(dist_sq, tiny)
                distance[at, part] = dist_sq * lax.rsqrt(dist_sq)
                mean_len = columns[at, 0:lanes] + len_row
                rate = closing * mean_len / (dist_sq + mean_len * mean_len)
                rates[at, part] = rate
                signal = sound_row - rate
                tops[c] = signal if k == 0 else jnp.maximum(tops[c], signal)
        top = jnp.max(jnp.concatenate(tops, axis=0).T, axis=0, keepdims=True)
        top = jnp.maximum(top, jnp.max(sounds, axis=1, keepdims=True))
        own_tile = tile_at(table, block)
        allowed[pl.ds(block, 1), :] = courant * own_tile[3:4] / (own_tile[7:8] + top)

    two_deep(prepare, finish)
    least = jnp.min(allowed[...], axis=(0, 1), keepdims=True)
    smallest[...] = jnp.broadcast_to(least, (rows, lanes))


def density_kernel(
    plan, offsets, counts, columns, distance, own, m0, m1, m2, m3, density, second, *rest
):
    outgoing = rest[0:4]
    table, masses, sums, *scratch = rest[4:]
    feats, weights = scratch[0:2], scratch[2:4]
    fill_table(own, (m0, m1, m2, m3), table, rows)
    fill_mass(own, (m0, m1, m2, m3), masses)

    def prepare(block, buf):
        centre = centre_of(tile_at(table, block))
        ids = row_ids()
        for k in range(8):
            entry = plan[k, block]
            part = slice(k * lanes, (k + 1) * lanes)
            tile = tile_at(table, entry) - centre
            weighed = jnp.where(ids == 3, 1.0, tile) * masses[pl.ds(entry, 1), :]
            stacked = jnp.concatenate(
                [weighed, weighed * tile[0:1], weighed * tile[1:2], weighed * tile[2:3]], axis=0
            )
            high, low = split2(stacked)
            feats[buf][0:32, part] = high
            feats[buf][32:64, part] = low

    def finish(block, buf):
        for start in range(0, lanes, chunk):
            at = pl.ds(pl.multiple_of(block * lanes + start, chunk), chunk)
            scale = columns[at, 2 * lanes :]
            for k in range(8):
                part = slice(k * lanes, (k + 1) * lanes)
                ratio = distance[at, part] * scale
                wide = jnp.maximum(1.0 - ratio, 0.0)
                narrow = jnp.maximum(0.5 - ratio, 0.0)
                twice = narrow + narrow
                high, low = split2(wide * wide * wide - twice * twice * narrow)
                weights[buf][start : start + chunk, part] = high
                weights[buf][lanes + start : lanes + start + chunk, part] = low
        out = lax.dot_general(
            weights[buf][...], feats[buf][...], (((1,), (1,)), ((), ())), preferred_element_type=f32
        )
        out = (out[0:lanes] + out[lanes:]).T
        at = pl.ds(pl.multiple_of(block * 32, 32), 32)
        sums[at, :] = out[0:32] + out[32:64]

    two_deep(prepare, finish)

    def total(field):
        return sums[pl.ds(field, 8, stride=32), :]

    def mine(field):
        return own[pl.ds(field, 8, stride=rows), :]

    length = mine(3)
    place = [mine(a) for a in range(3)]
    place = [value - (jnp.floor(value[:, 0:1]) + 0.5) for value in place]
    whole = total(3)
    dens = whole * (2.0 / math.pi) / (length * length * length)
    first = [total(a) for a in range(3)]
    inverse = 1.0 / whole
    floor = 0.05 * length * length

    def moment(a, b):
        raw = total(8 + 8 * a + b) - place[a] * first[b] - place[b] * first[a]
        return (raw + place[a] * place[b] * whole) * inverse

    axx = moment(0, 0) + floor
    ayy = moment(1, 1) + floor
    azz = moment(2, 2) + floor
    axy, axz, ayz = moment(0, 1), moment(0, 2), moment(1, 2)
    cof_xx = ayy * azz - ayz * ayz
    cof_yy = axx * azz - axz * axz
    cof_zz = axx * ayy - axy * axy
    cof_xy = axz * ayz - axy * azz
    cof_xz = axy * ayz - ayy * axz
    cof_yz = axy * axz - axx * ayz
    inv_det = 1.0 / (axx * cof_xx + axy * cof_xy + axz * cof_xz)
    density[...] = dens
    pressure = (gas_gamma - 1.0) * own[72:80, :] / dens
    fields = [dens, pressure, cof_xx * inv_det, cof_yy * inv_det, cof_zz * inv_det]
    fields += [cof_xy * inv_det, cof_xz * inv_det, cof_yz * inv_det]
    for field in range(8):
        for block in range(8):
            at = block * rows + field
            second[at : at + 1, :] = fields[field][block : block + 1, :]
    cut_windows(lambda r: offsets[0, r], lambda r: counts[0, r], second, outgoing, False)


def weight_kernel(
    first, plan, columns, distance, rates, second, own, m0, m1, m2, m3,
    weights, damping, dens_col, table
):
    fill_table(own, (m0, m1, m2, m3), table, rows)

    def step(place, _):
        block = first + place
        turned = jnp.broadcast_to(second[pl.ds(block * rows, 1), :], (lanes, lanes)).T
        dens_col[pl.ds(pl.multiple_of(place * lanes, lanes), lanes), :] = turned
        tiles = [tile_at(table, plan[k, block]) for k in range(8)]
        for start in range(0, lanes, chunk):
            at = pl.ds(pl.multiple_of(block * lanes + start, chunk), chunk)
            to = pl.ds(pl.multiple_of(place * lanes + start, chunk), chunk)
            len_own = columns[at, 0:lanes]
            sound_own = columns[at, lanes : 2 * lanes]
            for k in range(8):
                part = slice(k * lanes, (k + 1) * lanes)
                inv_len = 1.0 / (len_own + tiles[k][3:4] * 0.05)
                ratio = distance[at, part] * inv_len
                wide = jnp.maximum(20.0 - ratio, 0.0) * inv_len
                narrow = jnp.maximum(10.0 - ratio, 0.0) * inv_len
                twice = narrow + narrow
                weight = wide * wide * wide - twice * twice * narrow
                rate = jnp.minimum(rates[at, part], 0.0)
                sounds = sound_own + tiles[k][7:8] * 0.75
                damping[to, part] = weight * rate * (rate - sounds)
                high, low = split2(weight)
                base = pl.multiple_of(place * 2 * lanes + start, chunk)
                weights[pl.ds(base, chunk), part] = high
                weights[pl.ds(base + lanes, chunk), part] = low
        return 0

    lax.fori_loop(0, 4, step, 0, unroll=2)


def momentum_kernel(
    plan, weights_a, damping_a, dens_col_a, weights_b, damping_b, dens_col_b,
    own, m0, m1, m2, m3, second, s0, s1, s2, s3, accel, heating, *scratch
):
    table, masses, table2, sums, *scratch = scratch
    feats, damped = scratch[0:2], scratch[2:4]
    fill_table(own, (m0, m1, m2, m3), table, rows)
    fill_mass(own, (m0, m1, m2, m3), masses)
    fill_table(second, (s0, s1, s2, s3), table2, rows)
    ids = row_ids()

    def features(tile, extra, mass):
        cols = [
            jnp.concatenate([extra[i : i + 1] for i in picked], axis=0)
            for picked in ((2, 5, 6, 2, 2, 5, 6, 2), (5, 3, 7, 3, 5, 3, 7, 3), (6, 7, 4, 4, 6, 7, 4, 4))
        ]
        heavy = tile * mass
        applied = None
        for axis in range(3):
            operand = jnp.where(ids < 4, tile[axis : axis + 1], tile[4 + axis : 5 + axis])
            term = cols[axis] * operand
            applied = term if applied is None else applied + term
        swirl = (
            applied[0:1] * tile[4:5] + applied[1:2] * tile[5:6] + applied[2:3] * tile[6:7]
        )
        applied = placed(applied, 3, swirl)
        press = extra[1:2] * mass
        parts = [jnp.where(ids == 3, mass, heavy)]
        parts += [heavy * tile[4 + axis : 5 + axis] for axis in range(3)]
        parts += [extra * mass, extra * press, applied * mass, applied * press]
        return jnp.concatenate(parts, axis=0)

    def prepare(block, buf):
        centre = centre_of(tile_at(table, block))
        for k in range(8):
            entry = plan[k, block]
            part = slice(k * lanes, (k + 1) * lanes)
            tile = tile_at(table, entry) - centre
            high, low = split2(
                features(tile, tile_at(table2, entry), masses[pl.ds(entry, 1), :])
            )
            feats[buf][0:64, part] = high
            feats[buf][64:128, part] = low

    def finish_part(weights, damping, dens_col, first, block, buf):
        place = block - first
        for start in range(0, lanes, chunk):
            at = pl.ds(pl.multiple_of(place * lanes + start, chunk), chunk)
            for k in range(8):
                dens_row = tile_at(table2, plan[k, block])[0:1]
                part = slice(k * lanes, (k + 1) * lanes)
                high, low = split2(damping[at, part] / (dens_col[at, :] + dens_row))
                damped[buf][start : start + chunk, part] = high
                damped[buf][lanes + start : lanes + start + chunk, part] = low
        own_weights = weights[pl.ds(pl.multiple_of(place * 2 * lanes, lanes), 2 * lanes), :]
        for base, value in ((0, own_weights), (64, damped[buf][...])):
            out = lax.dot_general(
                value, feats[buf][...], (((1,), (1,)), ((), ())), preferred_element_type=f32
            )
            out = (out[0:lanes] + out[lanes:]).T
            at = pl.ds(pl.multiple_of(block * lanes + base, 64), 64)
            sums[at, :] = out[0:64] + out[64:128]

    two_deep(prepare, functools.partial(finish_part, weights_a, damping_a, dens_col_a, 0), 0, 4)
    two_deep(prepare, functools.partial(finish_part, weights_b, damping_b, dens_col_b, 4), 4, 8)

    def mine(ref, field):
        return ref[pl.ds(field, 8, stride=rows), :]

    place = [mine(own, a) for a in range(3)]
    place = [value - (jnp.floor(value[:, 0:1]) + 0.5) for value in place]
    speed = [mine(own, 4 + a) for a in range(3)]
    pressure = mine(second, 1)
    order = ((2, 5, 6), (5, 3, 7), (6, 7, 4))
    matrix = [[mine(second, order[a][b]) for b in range(3)] for a in range(3)]

    def pieces(base):
        def total(field):
            return sums[pl.ds(base + field, 8, stride=lanes), :]

        mass = total(3)
        offset = [total(a) - place[a] * mass for a in range(3)]
        mass_v = [total(4 + a) for a in range(3)]
        applied = [
            matrix[a][0] * offset[0] + matrix[a][1] * offset[1] + matrix[a][2] * offset[2]
            for a in range(3)
        ]
        work = None
        for a in range(3):
            for b in range(3):
                cross = speed[a] * offset[b] - total(8 + 8 * a + b) + mass_v[a] * place[b]
                term = matrix[a][b] * cross
                work = term if work is None else work + term
        return total, applied, work

    def near_force(total, matrices, vectors):
        return [
            total(vectors + a)
            - total(matrices + order[a][0]) * place[0]
            - total(matrices + order[a][1]) * place[1]
            - total(matrices + order[a][2]) * place[2]
            for a in range(3)
        ]

    norm = 16.0 / math.pi / 20.0**6
    total, applied, work = pieces(0)
    pushed = near_force(total, 40, 56)
    total2, applied2, work2 = pieces(64)
    pushed2 = near_force(total2, 32, 48)
    for a in range(3):
        value = -norm * (
            pressure * applied[a] + pushed[a] + (2.0 / 9.0) * (applied2[a] + pushed2[a])
        )
        for block in range(8):
            part = slice(block * lanes, (block + 1) * lanes)
            accel[a : a + 1, part] = value[block : block + 1, :]
    near_work = (
        speed[0] * pushed2[0]
        + speed[1] * pushed2[1]
        + speed[2] * pushed2[2]
        - total2(51)
        + place[0] * total2(52)
        + place[1] * total2(53)
        + place[2] * total2(54)
    )
    heating[...] = norm * (pressure * work + (1.0 / 9.0) * (work2 + near_work))


def call(kernel, outs, scratch, smem, args, flops, limit):
    return pl.pallas_call(
        kernel,
        out_shape=[jax.ShapeDtypeStruct(shape, kind) for shape, kind in outs],
        in_specs=[smem_spec] * smem + [vmem_spec] * (len(args) - smem),
        out_specs=[vmem_spec] * len(outs),
        scratch_shapes=[pltpu.VMEM(shape, kind) for shape, kind in scratch],
        compiler_params=pltpu.CompilerParams(vmem_limit_bytes=limit * 1024 * 1024),
        cost_estimate=pl.CostEstimate(flops=flops, bytes_accessed=200000, transcendentals=0),
    )(*args)


def fold(value, axis, step):
    size = lax.axis_size(axis)
    return jnp.minimum(value, lax.ppermute(value, axis, [(i, i ^ step) for i in range(size)]))


def body(positions, velocities, mass, smoothing, energy, send_offsets, send_counts, pair_blocks):
    points = positions.shape[1]
    send_offsets, send_counts = send_offsets.reshape(1, 4), send_counts.reshape(1, 4)
    tile = ((rows, lanes), f32)
    packed = ((72, lanes), f32)
    own, *outgoing = pl.pallas_call(
        pack_kernel,
        out_shape=[jax.ShapeDtypeStruct((80, lanes), f32)] + [jax.ShapeDtypeStruct(*packed)] * 4,
        in_specs=[vmem_spec] * 5 + [smem_spec] * 2,
        out_specs=[vmem_spec] * 5,
    )(
        positions,
        velocities,
        mass.reshape(8, lanes),
        smoothing.reshape(8, lanes),
        energy.reshape(8, lanes),
        send_offsets,
        send_counts,
    )
    received = [swap(value, axis, odd) for value, (axis, odd, _) in zip(outgoing, swaps)]
    steps = [("dom", 1 << bit) for bit in range(lax.axis_size("dom").bit_length() - 1)]
    steps = steps[::-1][:1] + steps[:-1]
    steps += [("slab", 1 << bit) for bit in reversed(range(lax.axis_size("slab").bit_length() - 1))]
    steps = steps[:2] + steps[3:] + steps[2:3]
    left, columns, own, plan = pl.pallas_call(
        own_kernel,
        out_shape=[
            jax.ShapeDtypeStruct((8 * lanes, lanes), bf16),
            jax.ShapeDtypeStruct((8 * lanes, 3 * lanes), f32),
            jax.ShapeDtypeStruct((80, lanes), f32),
            jax.ShapeDtypeStruct(pair_blocks.shape, jnp.int32),
        ],
        in_specs=[vmem_spec] * 2,
        out_specs=[vmem_spec] * 4,
        compiler_params=pltpu.CompilerParams(vmem_limit_bytes=8 * 1024 * 1024),
    )(pair_blocks, own)
    table = ((328, lanes), f32)
    masses = ((48, lanes), f32)
    near = ((lanes, 16 * lanes), bf16)
    feats = ((64, 8 * lanes), bf16)
    halves = ((2 * lanes, 8 * lanes), bf16)
    square = ((8 * lanes, 8 * lanes), f32)
    allowed, smallest, distance, rates = call(
        signal_kernel,
        [tile, tile, square, square],
        [table, near, near],
        1,
        (plan, left, columns, own, *received),
        3 * 10**9,
        20,
    )
    smallest = fold(smallest, *steps[0])
    density, second, *outgoing2 = call(
        density_kernel,
        [tile] + [((64, lanes), f32)] * 5,
        [table, masses, ((8 * 32, lanes), f32)] + [feats] * 2 + [halves] * 2,
        3,
        (plan, send_offsets, send_counts, columns, distance, own, *received),
        5 * 10**9,
        20,
    )
    smallest, outgoing2 = lax.optimization_barrier((smallest, outgoing2))
    received2 = [swap(value, axis, odd) for value, (axis, odd, _) in zip(outgoing2, swaps)]
    smallest = fold(smallest, *steps[1])
    parts = []
    for first in (0, 4):
        smallest = fold(smallest, *steps[2 + first // 4])
        weights, damping, dens_col = call(
            functools.partial(weight_kernel, first),
            [((8 * lanes, 8 * lanes), bf16), ((4 * lanes, 8 * lanes), f32), ((4 * lanes, lanes), f32)],
            [table],
            1,
            (plan, columns, distance, rates, second, own, *received),
            10**8,
            20,
        )
        smallest, distance, weights = lax.optimization_barrier((smallest, distance, weights))
        parts += [weights, damping, dens_col]
    for step in steps[4:-1]:
        smallest = fold(smallest, *step)
    smallest, received2 = lax.optimization_barrier((smallest, received2))
    accel, heating = call(
        momentum_kernel,
        [((3, points), f32), tile],
        [table, masses, table, ((8 * lanes, lanes), f32)]
        + [((lanes, 8 * lanes), bf16)] * 2
        + [halves] * 2,
        1,
        (plan, *parts, own, *received, second, *received2),
        5 * 10**9,
        20,
    )
    smallest = fold(smallest, *steps[-1])
    share = smallest / allowed
    return (density.reshape(points), accel, heating.reshape(points), share.reshape(points))


def solution(mesh):
    both = ("slab", "dom")
    wide, flat = P(None, both), P(both)
    in_specs = (wide, wide, flat, flat, flat, wide, wide, wide)
    out_specs = (flat, wide, flat, flat)
    return jax.shard_map(body, mesh=mesh, in_specs=in_specs, out_specs=out_specs, check_vma=False)
```

```python
import functools
import math

import jax
import jax.numpy as jnp
from jax import lax
from jax.experimental import pallas as pl
from jax.experimental.pallas import tpu as pltpu
from jax.sharding import PartitionSpec as P

gas_gamma = 5.0 / 3.0
courant = 0.4
f32 = jnp.float32
bf16 = jnp.bfloat16
rows = 8
lanes = 128
tiny = 1e-12
chunk = 32
swaps = (("dom", 0, 2), ("slab", 0, 0), ("dom", 1, 2), ("slab", 1, 0))
vmem_spec = pl.BlockSpec(memory_space=pltpu.VMEM)
smem_spec = pl.BlockSpec(memory_space=pltpu.SMEM)


def partner(axis, odd, base):
    place = lax.axis_index(axis)
    size = lax.axis_size(axis)
    upward = lax.rem(place + odd, 2) == 0
    direction = base + jnp.where(upward, 1, 0)
    exists = jnp.where(upward, place < size - 1, place > 0)
    return direction, exists


def swap(value, axis, odd):
    size = lax.axis_size(axis)
    pairs = [
        (i, (i + 1) % size if (i - odd) % 2 == 0 else (i - 1) % size) for i in range(size)
    ]
    return lax.ppermute(value, axis, pairs)


def split2(value):
    high = value.astype(bf16)
    low = (value - high.astype(f32)).astype(bf16)
    return high, low


def split3(value):
    first = value.astype(bf16).astype(f32)
    rest = value - first
    second = rest.astype(bf16).astype(f32)
    return first, second, rest - second


def row_ids():
    return lax.broadcasted_iota(jnp.int32, (rows, lanes), 0)


def centre_of(tile):
    corner = jnp.floor(tile[:, 0:1]) + 0.5
    return jnp.where(row_ids() < 3, jnp.broadcast_to(corner, tile.shape), 0.0)


def sum_xyz(tile, start):
    return tile[start : start + 1] + tile[start + 1 : start + 2] + tile[start + 2 : start + 3]


def placed(tile, at, row):
    return jnp.where(row_ids() == at, jnp.broadcast_to(row, tile.shape), tile)


def near_operand(tile):
    norm = sum_xyz(tile * tile, 0)
    drift = (
        tile[0:1] * tile[4:5] + tile[1:2] * tile[5:6] + tile[2:3] * tile[6:7]
    )
    first, second, third = split3(placed(placed(tile, 3, norm), 7, drift))
    ones = jnp.where(row_ids() < 3, 1.0, 0.0)
    stacked = [first, second, third, first, second, first, ones, jnp.zeros_like(ones)]
    return jnp.concatenate(stacked, axis=0).astype(bf16)


def own_operand(tile, own_term):
    first, second, third = split3(tile)
    parts = split3(own_term)
    ones = jnp.zeros((rows, lanes), f32)
    for at in range(3):
        ones = placed(ones, at, parts[at])
    stacked = [first, first, first, second, second, third, ones, jnp.zeros_like(ones)]
    return jnp.concatenate(stacked, axis=0)


def own_distance(tile):
    norm = sum_xyz(tile * tile, 0)
    ids = row_ids()
    left = jnp.where(ids < 3, -2.0 * tile, jnp.where(ids == 3, 1.0, 0.0))
    return own_operand(left, norm)


def own_closing(tile, scale):
    drift = (
        tile[0:1] * tile[4:5] + tile[1:2] * tile[5:6] + tile[2:3] * tile[6:7]
    )
    ids = row_ids()
    left = jnp.concatenate([-tile[4:8], -tile[0:4]], axis=0)
    left = jnp.where(ids == 3, 0.0, jnp.where(ids == 7, 1.0, left))
    return own_operand(left * scale, drift * scale)


def fill_table(own, received, table, width):
    table[0 : 8 * width, :] = own[0 : 8 * width, :]
    for message, (axis, odd, base) in zip(received, swaps):
        direction, _ = partner(axis, odd, base)
        start = pl.multiple_of((direction + 1) * (8 * width), 8 * width)
        table[pl.ds(start, 8 * width), :] = message[0 : 8 * width, :]
    table[40 * width : 40 * width + 8, :] = jnp.zeros((8, lanes), f32)


def fill_mass(own, received, masses):
    masses[0:8, :] = own[64:72, :]
    for message, (axis, odd, base) in zip(received, swaps):
        direction, _ = partner(axis, odd, base)
        start = pl.multiple_of((direction + 1) * 8, 8)
        masses[pl.ds(start, 8), :] = message[64:72, :]
    masses[40:48, :] = jnp.zeros((8, lanes), f32)


def tile_at(table, entry):
    return table[pl.ds(pl.multiple_of(entry * rows, rows), rows), :]


def cut_windows(offset_of, count_of, source, outgoing, masses):
    for target, (axis, odd, base) in zip(outgoing, swaps):
        direction, exists = partner(axis, odd, base)
        offset = offset_of(direction)
        count = jnp.where(exists, count_of(direction), 0)
        for slot in range(8):
            block = jnp.minimum(offset + slot, 7)
            keep = slot < count
            tile = tile_at(source, block)
            target[slot * rows : (slot + 1) * rows, :] = jnp.where(keep, tile, 0.0)
            if masses:
                row = source[pl.ds(64 + block, 1), :]
                target[64 + slot : 65 + slot, :] = jnp.where(keep, row, 0.0)


def pack_kernel(positions, velocities, mass, smoothing, energy, offsets, counts, own, *outgoing):
    sound = jnp.sqrt(gas_gamma * (gas_gamma - 1.0) * energy[...])
    for block in range(8):
        part = slice(block * lanes, (block + 1) * lanes)
        at = block * rows
        own[at : at + 3, :] = positions[:, part]
        own[at + 4 : at + 7, :] = velocities[:, part]
    own[pl.ds(3, 8, stride=rows), :] = smoothing[...]
    own[pl.ds(7, 8, stride=rows), :] = sound
    own[64:72, :] = mass[...]
    own[72:80, :] = energy[...]
    cut_windows(lambda r: offsets[0, r], lambda r: counts[0, r], own, outgoing, True)


def two_deep(prepare, finish, first=0, last=8):
    prepare(first, 0)

    def step(half, _):
        block = first + half * 2
        prepare(block + 1, 1)
        finish(block, 0)
        prepare(jnp.minimum(block + 2, last - 1), 0)
        finish(block + 1, 1)
        return 0

    lax.fori_loop(0, (last - first) // 2, step, 0, unroll=True)


def own_kernel(pairs, own, left, columns, table, plan):
    table[...] = own[...]
    plan[...] = pairs[...]

    def step(block, _):
        tile = tile_at(own, block)
        centred = tile - centre_of(tile)
        stacked = jnp.concatenate([own_distance(centred), own_closing(centred, 30.0)], axis=0)
        at = pl.ds(pl.multiple_of(block * lanes, lanes), lanes)
        left[at, :] = stacked.T.astype(bf16)
        turned = tile.T
        length = turned[:, 3:4]
        columns[at, 0:lanes] = jnp.broadcast_to(length * 0.05, (lanes, lanes))
        columns[at, lanes : 2 * lanes] = jnp.broadcast_to(turned[:, 7:8] * 0.75, (lanes, lanes))
        columns[at, 2 * lanes :] = jnp.broadcast_to(0.5 / length, (lanes, lanes))
        return 0

    lax.fori_loop(0, 8, step, 0)


def put_near(near, k, tile):
    operand = near_operand(tile)
    at = 2 * k * lanes
    near[0:64, at : at + lanes] = operand
    near[64:128, at + lanes : at + 2 * lanes] = operand


def clear_near(buffers):
    for near in buffers:
        near[...] = jnp.zeros(near.shape, bf16)


def pair_dots(left, near, block, start, k):
    at = pl.ds(pl.multiple_of(block * lanes + start, chunk), chunk)
    part = slice(2 * k * lanes, 2 * (k + 1) * lanes)
    both = jnp.dot(left[at, :], near[:, part], preferred_element_type=f32)
    return both[:, 0:lanes], both[:, lanes:]


def signal_kernel(
    plan, left, columns, own, m0, m1, m2, m3, allowed, smallest, distance, rates, table, *near
):
    clear_near(near)
    fill_table(own, (m0, m1, m2, m3), table, rows)

    def prepare(block, buf):
        centre = centre_of(tile_at(table, block))
        for k in range(8):
            put_near(near[buf], k, tile_at(table, plan[k, block]) - centre)

    def finish(block, buf):
        tops = [None] * (lanes // chunk)
        sounds = None
        for k in range(8):
            tile = tile_at(table, plan[k, block])
            len_row, sound_row = tile[3:4] * 0.05, tile[7:8]
            sounds = sound_row if k == 0 else jnp.maximum(sounds, sound_row)
            part = slice(k * lanes, (k + 1) * lanes)
            for c in range(lanes // chunk):
                start = c * chunk
                at = pl.ds(pl.multiple_of(block * lanes + start, chunk), chunk)
                dist_sq, closing = pair_dots(left, near[buf], block, start, k)
                dist_sq = jnp.maximum(dist_sq, tiny)
                distance[at, part] = dist_sq * lax.rsqrt(dist_sq)
                mean_len = columns[at, 0:lanes] + len_row
                rate = closing * mean_len / (dist_sq + mean_len * mean_len)
                rates[at, part] = rate
                signal = sound_row - rate
                tops[c] = signal if k == 0 else jnp.maximum(tops[c], signal)
        top = jnp.max(jnp.concatenate(tops, axis=0).T, axis=0, keepdims=True)
        top = jnp.maximum(top, jnp.max(sounds, axis=1, keepdims=True))
        own_tile = tile_at(table, block)
        allowed[pl.ds(block, 1), :] = courant * own_tile[3:4] / (own_tile[7:8] + top)

    two_deep(prepare, finish)
    least = jnp.min(allowed[...], axis=(0, 1), keepdims=True)
    smallest[...] = jnp.broadcast_to(least, (rows, lanes))


def density_kernel(
    plan, offsets, counts, columns, distance, own, m0, m1, m2, m3, density, second, *rest
):
    outgoing = rest[0:4]
    table, masses, sums, *scratch = rest[4:]
    feats, weights = scratch[0:2], scratch[2:4]
    fill_table(own, (m0, m1, m2, m3), table, rows)
    fill_mass(own, (m0, m1, m2, m3), masses)

    def prepare(block, buf):
        centre = centre_of(tile_at(table, block))
        ids = row_ids()
        for k in range(8):
            entry = plan[k, block]
            part = slice(k * lanes, (k + 1) * lanes)
            tile = tile_at(table, entry) - centre
            weighed = jnp.where(ids == 3, 1.0, tile) * masses[pl.ds(entry, 1), :]
            stacked = jnp.concatenate(
                [weighed, weighed * tile[0:1], weighed * tile[1:2], weighed * tile[2:3]], axis=0
            )
            high, low = split2(stacked)
            feats[buf][0:32, part] = high
            feats[buf][32:64, part] = low

    def finish(block, buf):
        for start in range(0, lanes, chunk):
            at = pl.ds(pl.multiple_of(block * lanes + start, chunk), chunk)
            scale = columns[at, 2 * lanes :]
            for k in range(8):
                part = slice(k * lanes, (k + 1) * lanes)
                ratio = distance[at, part] * scale
                wide = jnp.maximum(1.0 - ratio, 0.0)
                narrow = jnp.maximum(0.5 - ratio, 0.0)
                twice = narrow + narrow
                high, low = split2(wide * wide * wide - twice * twice * narrow)
                weights[buf][start : start + chunk, part] = high
                weights[buf][lanes + start : lanes + start + chunk, part] = low
        out = lax.dot_general(
            weights[buf][...], feats[buf][...], (((1,), (1,)), ((), ())), preferred_element_type=f32
        )
        out = (out[0:lanes] + out[lanes:]).T
        at = pl.ds(pl.multiple_of(block * 32, 32), 32)
        sums[at, :] = out[0:32] + out[32:64]

    two_deep(prepare, finish)

    def total(field):
        return sums[pl.ds(field, 8, stride=32), :]

    def mine(field):
        return own[pl.ds(field, 8, stride=rows), :]

    length = mine(3)
    place = [mine(a) for a in range(3)]
    place = [value - (jnp.floor(value[:, 0:1]) + 0.5) for value in place]
    whole = total(3)
    dens = whole * (2.0 / math.pi) / (length * length * length)
    first = [total(a) for a in range(3)]
    inverse = 1.0 / whole
    floor = 0.05 * length * length

    def moment(a, b):
        raw = total(8 + 8 * a + b) - place[a] * first[b] - place[b] * first[a]
        return (raw + place[a] * place[b] * whole) * inverse

    axx = moment(0, 0) + floor
    ayy = moment(1, 1) + floor
    azz = moment(2, 2) + floor
    axy, axz, ayz = moment(0, 1), moment(0, 2), moment(1, 2)
    cof_xx = ayy * azz - ayz * ayz
    cof_yy = axx * azz - axz * axz
    cof_zz = axx * ayy - axy * axy
    cof_xy = axz * ayz - axy * azz
    cof_xz = axy * ayz - ayy * axz
    cof_yz = axy * axz - axx * ayz
    inv_det = 1.0 / (axx * cof_xx + axy * cof_xy + axz * cof_xz)
    density[...] = dens
    pressure = (gas_gamma - 1.0) * own[72:80, :] / dens
    fields = [dens, pressure, cof_xx * inv_det, cof_yy * inv_det, cof_zz * inv_det]
    fields += [cof_xy * inv_det, cof_xz * inv_det, cof_yz * inv_det]
    for field in range(8):
        second[pl.ds(field, 8, stride=rows), :] = fields[field]
    cut_windows(lambda r: offsets[0, r], lambda r: counts[0, r], second, outgoing, False)


def weight_kernel(
    first, plan, columns, distance, rates, second, own, m0, m1, m2, m3,
    weights, damping, dens_col, table
):
    fill_table(own, (m0, m1, m2, m3), table, rows)

    def step(place, _):
        block = first + place
        turned = jnp.broadcast_to(second[pl.ds(block * rows, 1), :], (lanes, lanes)).T
        dens_col[pl.ds(pl.multiple_of(place * lanes, lanes), lanes), :] = turned
        tiles = [tile_at(table, plan[k, block]) for k in range(8)]
        for start in range(0, lanes, chunk):
            at = pl.ds(pl.multiple_of(block * lanes + start, chunk), chunk)
            to = pl.ds(pl.multiple_of(place * lanes + start, chunk), chunk)
            len_own = columns[at, 0:lanes]
            sound_own = columns[at, lanes : 2 * lanes]
            for k in range(8):
                part = slice(k * lanes, (k + 1) * lanes)
                inv_len = 1.0 / (len_own + tiles[k][3:4] * 0.05)
                ratio = distance[at, part] * inv_len
                wide = jnp.maximum(20.0 - ratio, 0.0) * inv_len
                narrow = jnp.maximum(10.0 - ratio, 0.0) * inv_len
                twice = narrow + narrow
                weight = wide * wide * wide - twice * twice * narrow
                rate = jnp.minimum(rates[at, part], 0.0)
                sounds = sound_own + tiles[k][7:8] * 0.75
                damping[to, part] = weight * rate * (rate - sounds)
                high, low = split2(weight)
                base = pl.multiple_of(place * 2 * lanes + start, chunk)
                weights[pl.ds(base, chunk), part] = high
                weights[pl.ds(base + lanes, chunk), part] = low
        return 0

    lax.fori_loop(0, 8, step, 0, unroll=2)


def momentum_kernel(
    plan, weights, damping, dens_col,
    own, m0, m1, m2, m3, second, s0, s1, s2, s3, accel, heating, *scratch
):
    table, masses, table2, sums, *scratch = scratch
    feats, damped = scratch[0:2], scratch[2:4]
    fill_table(own, (m0, m1, m2, m3), table, rows)
    fill_mass(own, (m0, m1, m2, m3), masses)
    fill_table(second, (s0, s1, s2, s3), table2, rows)
    ids = row_ids()
    picks = []
    for picked in ((2, 5, 6, 2), (5, 3, 7, 3), (6, 7, 4, 4)):
        places = jnp.full((rows, lanes), picked[3], jnp.int32)
        for at in range(3):
            places = jnp.where(lax.rem(ids, 4) == at, picked[at], places)
        picks.append(places)

    def features(tile, extra, mass):
        cols = [jnp.take_along_axis(extra, places, axis=0) for places in picks]
        heavy = tile * mass
        applied = None
        for axis in range(3):
            operand = jnp.where(ids < 4, tile[axis : axis + 1], tile[4 + axis : 5 + axis])
            term = cols[axis] * operand
            applied = term if applied is None else applied + term
        swirl = (
            applied[0:1] * tile[4:5] + applied[1:2] * tile[5:6] + applied[2:3] * tile[6:7]
        )
        applied = placed(applied, 3, swirl)
        press = extra[1:2] * mass
        parts = [jnp.where(ids == 3, mass, heavy)]
        parts += [heavy * tile[4 + axis : 5 + axis] for axis in range(3)]
        parts += [extra * mass, extra * press, applied * mass, applied * press]
        return jnp.concatenate(parts, axis=0)

    def prepare(block, buf):
        centre = centre_of(tile_at(table, block))
        for k in range(8):
            entry = plan[k, block]
            part = slice(k * lanes, (k + 1) * lanes)
            tile = tile_at(table, entry) - centre
            high, low = split2(
                features(tile, tile_at(table2, entry), masses[pl.ds(entry, 1), :])
            )
            feats[buf][0:64, part] = high
            feats[buf][64:128, part] = low

    def finish_part(weights, damping, dens_col, first, block, buf):
        place = block - first
        for start in range(0, lanes, chunk):
            at = pl.ds(pl.multiple_of(place * lanes + start, chunk), chunk)
            for k in range(8):
                dens_row = tile_at(table2, plan[k, block])[0:1]
                part = slice(k * lanes, (k + 1) * lanes)
                high, low = split2(damping[at, part] / (dens_col[at, :] + dens_row))
                damped[buf][start : start + chunk, part] = high
                damped[buf][lanes + start : lanes + start + chunk, part] = low
        own_weights = weights[pl.ds(pl.multiple_of(place * 2 * lanes, lanes), 2 * lanes), :]
        for base, value in ((0, own_weights), (64, damped[buf][...])):
            out = lax.dot_general(
                value, feats[buf][...], (((1,), (1,)), ((), ())), preferred_element_type=f32
            )
            out = (out[0:lanes] + out[lanes:]).T
            at = pl.ds(pl.multiple_of(block * lanes + base, 64), 64)
            sums[at, :] = out[0:64] + out[64:128]

    two_deep(prepare, functools.partial(finish_part, weights, damping, dens_col, 0))

    def mine(ref, field):
        return ref[pl.ds(field, 8, stride=rows), :]

    place = [mine(own, a) for a in range(3)]
    place = [value - (jnp.floor(value[:, 0:1]) + 0.5) for value in place]
    speed = [mine(own, 4 + a) for a in range(3)]
    pressure = mine(second, 1)
    order = ((2, 5, 6), (5, 3, 7), (6, 7, 4))
    matrix = [[mine(second, order[a][b]) for b in range(3)] for a in range(3)]

    def pieces(base):
        def total(field):
            return sums[pl.ds(base + field, 8, stride=lanes), :]

        mass = total(3)
        offset = [total(a) - place[a] * mass for a in range(3)]
        mass_v = [total(4 + a) for a in range(3)]
        applied = [
            matrix[a][0] * offset[0] + matrix[a][1] * offset[1] + matrix[a][2] * offset[2]
            for a in range(3)
        ]
        work = None
        for a in range(3):
            for b in range(3):
                cross = speed[a] * offset[b] - total(8 + 8 * a + b) + mass_v[a] * place[b]
                term = matrix[a][b] * cross
                work = term if work is None else work + term
        return total, applied, work

    def near_force(total, matrices, vectors):
        return [
            total(vectors + a)
            - total(matrices + order[a][0]) * place[0]
            - total(matrices + order[a][1]) * place[1]
            - total(matrices + order[a][2]) * place[2]
            for a in range(3)
        ]

    norm = 16.0 / math.pi / 20.0**6
    total, applied, work = pieces(0)
    pushed = near_force(total, 40, 56)
    total2, applied2, work2 = pieces(64)
    pushed2 = near_force(total2, 32, 48)
    for a in range(3):
        value = -norm * (
            pressure * applied[a] + pushed[a] + (2.0 / 9.0) * (applied2[a] + pushed2[a])
        )
        for block in range(8):
            part = slice(block * lanes, (block + 1) * lanes)
            accel[a : a + 1, part] = value[block : block + 1, :]
    near_work = (
        speed[0] * pushed2[0]
        + speed[1] * pushed2[1]
        + speed[2] * pushed2[2]
        - total2(51)
        + place[0] * total2(52)
        + place[1] * total2(53)
        + place[2] * total2(54)
    )
    heating[...] = norm * (pressure * work + (1.0 / 9.0) * (work2 + near_work))


def call(kernel, outs, scratch, smem, args, flops, limit):
    return pl.pallas_call(
        kernel,
        out_shape=[jax.ShapeDtypeStruct(shape, kind) for shape, kind in outs],
        in_specs=[smem_spec] * smem + [vmem_spec] * (len(args) - smem),
        out_specs=[vmem_spec] * len(outs),
        scratch_shapes=[pltpu.VMEM(shape, kind) for shape, kind in scratch],
        compiler_params=pltpu.CompilerParams(vmem_limit_bytes=limit * 1024 * 1024),
        cost_estimate=pl.CostEstimate(flops=flops, bytes_accessed=200000, transcendentals=0),
    )(*args)


def fold(value, axis, step):
    size = lax.axis_size(axis)
    return jnp.minimum(value, lax.ppermute(value, axis, [(i, i ^ step) for i in range(size)]))


def body(positions, velocities, mass, smoothing, energy, send_offsets, send_counts, pair_blocks):
    points = positions.shape[1]
    send_offsets, send_counts = send_offsets.reshape(1, 4), send_counts.reshape(1, 4)
    tile = ((rows, lanes), f32)
    packed = ((72, lanes), f32)
    own, *outgoing = pl.pallas_call(
        pack_kernel,
        out_shape=[jax.ShapeDtypeStruct((80, lanes), f32)] + [jax.ShapeDtypeStruct(*packed)] * 4,
        in_specs=[vmem_spec] * 5 + [smem_spec] * 2,
        out_specs=[vmem_spec] * 5,
    )(
        positions,
        velocities,
        mass.reshape(8, lanes),
        smoothing.reshape(8, lanes),
        energy.reshape(8, lanes),
        send_offsets,
        send_counts,
    )
    received = [swap(value, axis, odd) for value, (axis, odd, _) in zip(outgoing, swaps)]
    steps = [("dom", 1 << bit) for bit in range(lax.axis_size("dom").bit_length() - 1)]
    steps = steps[::-1][:1] + steps[:-1]
    steps += [("slab", 1 << bit) for bit in reversed(range(lax.axis_size("slab").bit_length() - 1))]
    steps = steps[:2] + steps[3:] + steps[2:3]
    left, columns, own, plan = pl.pallas_call(
        own_kernel,
        out_shape=[
            jax.ShapeDtypeStruct((8 * lanes, lanes), bf16),
            jax.ShapeDtypeStruct((8 * lanes, 3 * lanes), f32),
            jax.ShapeDtypeStruct((80, lanes), f32),
            jax.ShapeDtypeStruct(pair_blocks.shape, jnp.int32),
        ],
        in_specs=[vmem_spec] * 2,
        out_specs=[vmem_spec] * 4,
        compiler_params=pltpu.CompilerParams(vmem_limit_bytes=8 * 1024 * 1024),
    )(pair_blocks, own)
    table = ((328, lanes), f32)
    masses = ((48, lanes), f32)
    near = ((lanes, 16 * lanes), bf16)
    feats = ((64, 8 * lanes), bf16)
    halves = ((2 * lanes, 8 * lanes), bf16)
    square = ((8 * lanes, 8 * lanes), f32)
    allowed, smallest, distance, rates = call(
        signal_kernel,
        [tile, tile, square, square],
        [table, near, near],
        1,
        (plan, left, columns, own, *received),
        3 * 10**9,
        20,
    )
    smallest = fold(smallest, *steps[0])
    density, second, *outgoing2 = call(
        density_kernel,
        [tile] + [((64, lanes), f32)] * 5,
        [table, masses, ((8 * 32, lanes), f32)] + [feats] * 2 + [halves] * 2,
        3,
        (plan, send_offsets, send_counts, columns, distance, own, *received),
        5 * 10**9,
        20,
    )
    smallest, outgoing2 = lax.optimization_barrier((smallest, outgoing2))
    received2 = [swap(value, axis, odd) for value, (axis, odd, _) in zip(outgoing2, swaps)]
    parts = []
    smallest = fold(smallest, *steps[2])
    for first in (0,):
        smallest = fold(smallest, *steps[3])
        weights, damping, dens_col = call(
            functools.partial(weight_kernel, first),
            [((16 * lanes, 8 * lanes), bf16), ((8 * lanes, 8 * lanes), f32), ((8 * lanes, lanes), f32)],
            [table],
            1,
            (plan, columns, distance, rates, second, own, *received),
            10**9,
            20,
        )
        smallest, distance, weights = lax.optimization_barrier((smallest, distance, weights))
        parts += [weights, damping, dens_col]
    for step in steps[4:-1]:
        smallest = fold(smallest, *step)
    smallest, received2 = lax.optimization_barrier((smallest, received2))
    accel, heating = call(
        momentum_kernel,
        [((3, points), f32), tile],
        [table, masses, table, ((8 * lanes, lanes), f32)]
        + [((lanes, 8 * lanes), bf16)] * 2
        + [halves] * 2,
        1,
        (plan, *parts, own, *received, second, *received2),
        5 * 10**9,
        20,
    )
    smallest = fold(smallest, *steps[-1])
    smallest, accel = lax.optimization_barrier((smallest, accel))
    smallest = fold(smallest, *steps[1])
    share = smallest / allowed
    return (density.reshape(points), accel, heating.reshape(points), share.reshape(points))


def solution(mesh):
    both = ("slab", "dom")
    wide, flat = P(None, both), P(both)
    in_specs = (wide, wide, flat, flat, flat, wide, wide, wide)
    out_specs = (flat, wide, flat, flat)
    return jax.shard_map(body, mesh=mesh, in_specs=in_specs, out_specs=out_specs, check_vma=False)
```

```python
import functools
import math

import jax
import jax.numpy as jnp
from jax import lax
from jax.experimental import pallas as pl
from jax.experimental.pallas import tpu as pltpu
from jax.sharding import PartitionSpec as P

gas_gamma = 5.0 / 3.0
courant = 0.4
f32 = jnp.float32
bf16 = jnp.bfloat16
rows = 8
lanes = 128
tiny = 1e-12
chunk = 32
swaps = (("dom", 0, 2), ("slab", 0, 0), ("dom", 1, 2), ("slab", 1, 0))
vmem_spec = pl.BlockSpec(memory_space=pltpu.VMEM)
smem_spec = pl.BlockSpec(memory_space=pltpu.SMEM)


def partner(axis, odd, base):
    place = lax.axis_index(axis)
    size = lax.axis_size(axis)
    upward = lax.rem(place + odd, 2) == 0
    direction = base + jnp.where(upward, 1, 0)
    exists = jnp.where(upward, place < size - 1, place > 0)
    return direction, exists


def swap(value, axis, odd):
    size = lax.axis_size(axis)
    pairs = [
        (i, (i + 1) % size if (i - odd) % 2 == 0 else (i - 1) % size) for i in range(size)
    ]
    return lax.ppermute(value, axis, pairs)


def split2(value):
    high = value.astype(bf16)
    low = (value - high.astype(f32)).astype(bf16)
    return high, low


def split3(value):
    first = value.astype(bf16).astype(f32)
    rest = value - first
    second = rest.astype(bf16).astype(f32)
    return first, second, rest - second


def row_ids():
    return lax.broadcasted_iota(jnp.int32, (rows, lanes), 0)


def centre_of(tile):
    corner = jnp.floor(tile[:, 0:1]) + 0.5
    return jnp.where(row_ids() < 3, jnp.broadcast_to(corner, tile.shape), 0.0)


def sum_xyz(tile, start):
    return tile[start : start + 1] + tile[start + 1 : start + 2] + tile[start + 2 : start + 3]


def placed(tile, at, row):
    return jnp.where(row_ids() == at, jnp.broadcast_to(row, tile.shape), tile)


def near_operand(tile):
    norm = sum_xyz(tile * tile, 0)
    drift = (
        tile[0:1] * tile[4:5] + tile[1:2] * tile[5:6] + tile[2:3] * tile[6:7]
    )
    first, second, third = split3(placed(placed(tile, 3, norm), 7, drift))
    ones = jnp.where(row_ids() < 3, 1.0, 0.0)
    stacked = [first, second, third, first, second, first, ones, jnp.zeros_like(ones)]
    return jnp.concatenate(stacked, axis=0).astype(bf16)


def own_operand(tile, own_term):
    first, second, third = split3(tile)
    parts = split3(own_term)
    ones = jnp.zeros((rows, lanes), f32)
    for at in range(3):
        ones = placed(ones, at, parts[at])
    stacked = [first, first, first, second, second, third, ones, jnp.zeros_like(ones)]
    return jnp.concatenate(stacked, axis=0)


def own_distance(tile):
    norm = sum_xyz(tile * tile, 0)
    ids = row_ids()
    left = jnp.where(ids < 3, -2.0 * tile, jnp.where(ids == 3, 1.0, 0.0))
    return own_operand(left, norm)


def own_closing(tile, scale):
    drift = (
        tile[0:1] * tile[4:5] + tile[1:2] * tile[5:6] + tile[2:3] * tile[6:7]
    )
    ids = row_ids()
    left = jnp.concatenate([-tile[4:8], -tile[0:4]], axis=0)
    left = jnp.where(ids == 3, 0.0, jnp.where(ids == 7, 1.0, left))
    return own_operand(left * scale, drift * scale)


def fill_table(own, received, table, width):
    table[0 : 8 * width, :] = own[0 : 8 * width, :]
    for message, (axis, odd, base) in zip(received, swaps):
        direction, _ = partner(axis, odd, base)
        start = pl.multiple_of((direction + 1) * (8 * width), 8 * width)
        table[pl.ds(start, 8 * width), :] = message[0 : 8 * width, :]
    table[40 * width : 40 * width + 8, :] = jnp.zeros((8, lanes), f32)


def fill_mass(own, received, masses):
    masses[0:8, :] = own[64:72, :]
    for message, (axis, odd, base) in zip(received, swaps):
        direction, _ = partner(axis, odd, base)
        start = pl.multiple_of((direction + 1) * 8, 8)
        masses[pl.ds(start, 8), :] = message[64:72, :]
    masses[40:48, :] = jnp.zeros((8, lanes), f32)


def tile_at(table, entry):
    return table[pl.ds(pl.multiple_of(entry * rows, rows), rows), :]


def cut_windows(offset_of, count_of, source, outgoing, masses):
    for target, (axis, odd, base) in zip(outgoing, swaps):
        direction, exists = partner(axis, odd, base)
        offset = offset_of(direction)
        count = jnp.where(exists, count_of(direction), 0)
        for slot in range(8):
            block = jnp.minimum(offset + slot, 7)
            keep = slot < count
            tile = tile_at(source, block)
            target[slot * rows : (slot + 1) * rows, :] = jnp.where(keep, tile, 0.0)
            if masses:
                row = source[pl.ds(64 + block, 1), :]
                target[64 + slot : 65 + slot, :] = jnp.where(keep, row, 0.0)


def pack_kernel(positions, velocities, mass, smoothing, energy, offsets, counts, own, *outgoing):
    sound = jnp.sqrt(gas_gamma * (gas_gamma - 1.0) * energy[...])
    for block in range(8):
        part = slice(block * lanes, (block + 1) * lanes)
        at = block * rows
        own[at : at + 3, :] = positions[:, part]
        own[at + 4 : at + 7, :] = velocities[:, part]
    own[pl.ds(3, 8, stride=rows), :] = smoothing[...]
    own[pl.ds(7, 8, stride=rows), :] = sound
    own[64:72, :] = mass[...]
    own[72:80, :] = energy[...]
    cut_windows(lambda r: offsets[0, r], lambda r: counts[0, r], own, outgoing, True)


def two_deep(prepare, finish, first=0, last=8):
    prepare(first, 0)

    def step(half, _):
        block = first + half * 2
        prepare(block + 1, 1)
        finish(block, 0)
        prepare(jnp.minimum(block + 2, last - 1), 0)
        finish(block + 1, 1)
        return 0

    lax.fori_loop(0, (last - first) // 2, step, 0, unroll=True)


def own_kernel(pairs, own, left, columns, table, plan):
    table[...] = own[...]
    plan[...] = pairs[...]

    def step(block, _):
        tile = tile_at(own, block)
        centred = tile - centre_of(tile)
        stacked = jnp.concatenate([own_distance(centred), own_closing(centred, 30.0)], axis=0)
        at = pl.ds(pl.multiple_of(block * lanes, lanes), lanes)
        left[at, :] = stacked.T.astype(bf16)
        turned = tile.T
        length = turned[:, 3:4]
        columns[at, 0:lanes] = jnp.broadcast_to(length * 0.05, (lanes, lanes))
        columns[at, lanes : 2 * lanes] = jnp.broadcast_to(turned[:, 7:8] * 0.75, (lanes, lanes))
        columns[at, 2 * lanes :] = jnp.broadcast_to(0.5 / length, (lanes, lanes))
        return 0

    lax.fori_loop(0, 8, step, 0, unroll=True)


def put_near(near, k, tile):
    operand = near_operand(tile)
    at = 2 * k * lanes
    near[0:64, at : at + lanes] = operand
    near[64:128, at + lanes : at + 2 * lanes] = operand


def clear_near(buffers):
    for near in buffers:
        near[...] = jnp.zeros(near.shape, bf16)


def pair_dots(left, near, block, k):
    at = pl.ds(pl.multiple_of(block * lanes, lanes), lanes)
    part = slice(2 * k * lanes, 2 * (k + 1) * lanes)
    both = jnp.dot(left[at, :], near[:, part], preferred_element_type=f32)
    return both[:, 0:lanes], both[:, lanes:]


def signal_kernel(
    plan, left, columns, own, m0, m1, m2, m3, allowed, smallest, distance, rates, table, *near
):
    clear_near(near)
    fill_table(own, (m0, m1, m2, m3), table, rows)

    def prepare(block, buf):
        centre = centre_of(tile_at(table, block))
        for k in range(8):
            put_near(near[buf], k, tile_at(table, plan[k, block]) - centre)

    def finish(block, buf):
        best = None
        sounds = None
        for k in range(8):
            tile = tile_at(table, plan[k, block])
            len_row, sound_row = tile[3:4] * 0.05, tile[7:8]
            sounds = sound_row if k == 0 else jnp.maximum(sounds, sound_row)
            part = slice(k * lanes, (k + 1) * lanes)
            at = pl.ds(pl.multiple_of(block * lanes, lanes), lanes)
            dist_sq, closing = pair_dots(left, near[buf], block, k)
            dist_sq = jnp.maximum(dist_sq, tiny)
            distance[at, part] = dist_sq * lax.rsqrt(dist_sq)
            mean_len = columns[at, 0:lanes] + len_row
            rate = closing * mean_len / (dist_sq + mean_len * mean_len)
            rates[at, part] = rate
            signal = sound_row - rate
            best = signal if k == 0 else jnp.maximum(best, signal)
        top = jnp.max(best.T, axis=0, keepdims=True)
        top = jnp.maximum(top, jnp.max(sounds, axis=1, keepdims=True))
        own_tile = tile_at(table, block)
        allowed[pl.ds(block, 1), :] = courant * own_tile[3:4] / (own_tile[7:8] + top)

    two_deep(prepare, finish)
    least = jnp.min(allowed[...], axis=(0, 1), keepdims=True)
    smallest[...] = jnp.broadcast_to(least, (rows, lanes))


def density_kernel(
    plan, offsets, counts, columns, distance, own, m0, m1, m2, m3, density, second, *rest
):
    outgoing = rest[0:4]
    table, masses, sums, *scratch = rest[4:]
    feats, weights = scratch[0:2], scratch[2:4]
    fill_table(own, (m0, m1, m2, m3), table, rows)
    fill_mass(own, (m0, m1, m2, m3), masses)

    def prepare(block, buf):
        centre = centre_of(tile_at(table, block))
        ids = row_ids()
        for k in range(8):
            entry = plan[k, block]
            part = slice(k * lanes, (k + 1) * lanes)
            tile = tile_at(table, entry) - centre
            weighed = jnp.where(ids == 3, 1.0, tile) * masses[pl.ds(entry, 1), :]
            stacked = jnp.concatenate(
                [weighed, weighed * tile[0:1], weighed * tile[1:2], weighed * tile[2:3]], axis=0
            )
            high, low = split2(stacked)
            feats[buf][0:32, part] = high
            feats[buf][32:64, part] = low

    def finish(block, buf):
        for start in range(0, lanes, 2 * chunk):
            at = pl.ds(pl.multiple_of(block * lanes + start, 2 * chunk), 2 * chunk)
            scale = columns[at, 2 * lanes :]
            for k in range(8):
                part = slice(k * lanes, (k + 1) * lanes)
                ratio = distance[at, part] * scale
                wide = jnp.maximum(1.0 - ratio, 0.0)
                narrow = jnp.maximum(0.5 - ratio, 0.0)
                twice = narrow + narrow
                high, low = split2(wide * wide * wide - twice * twice * narrow)
                weights[buf][start : start + 2 * chunk, part] = high
                weights[buf][lanes + start : lanes + start + 2 * chunk, part] = low
        out = lax.dot_general(
            weights[buf][...], feats[buf][...], (((1,), (1,)), ((), ())), preferred_element_type=f32
        )
        out = (out[0:lanes] + out[lanes:]).T
        at = pl.ds(pl.multiple_of(block * 32, 32), 32)
        sums[at, :] = out[0:32] + out[32:64]

    two_deep(prepare, finish)

    def total(field):
        return sums[pl.ds(field, 8, stride=32), :]

    def mine(field):
        return own[pl.ds(field, 8, stride=rows), :]

    length = mine(3)
    place = [mine(a) for a in range(3)]
    place = [value - (jnp.floor(value[:, 0:1]) + 0.5) for value in place]
    whole = total(3)
    dens = whole * (2.0 / math.pi) / (length * length * length)
    first = [total(a) for a in range(3)]
    inverse = 1.0 / whole
    floor = 0.05 * length * length

    def moment(a, b):
        raw = total(8 + 8 * a + b) - place[a] * first[b] - place[b] * first[a]
        return (raw + place[a] * place[b] * whole) * inverse

    axx = moment(0, 0) + floor
    ayy = moment(1, 1) + floor
    azz = moment(2, 2) + floor
    axy, axz, ayz = moment(0, 1), moment(0, 2), moment(1, 2)
    cof_xx = ayy * azz - ayz * ayz
    cof_yy = axx * azz - axz * axz
    cof_zz = axx * ayy - axy * axy
    cof_xy = axz * ayz - axy * azz
    cof_xz = axy * ayz - ayy * axz
    cof_yz = axy * axz - axx * ayz
    inv_det = 1.0 / (axx * cof_xx + axy * cof_xy + axz * cof_xz)
    density[...] = dens
    pressure = (gas_gamma - 1.0) * own[72:80, :] / dens
    fields = [dens, pressure, cof_xx * inv_det, cof_yy * inv_det, cof_zz * inv_det]
    fields += [cof_xy * inv_det, cof_xz * inv_det, cof_yz * inv_det]
    for field in range(8):
        second[pl.ds(field, 8, stride=rows), :] = fields[field]
    cut_windows(lambda r: offsets[0, r], lambda r: counts[0, r], second, outgoing, False)


def weight_kernel(
    first, plan, columns, distance, rates, second, own, m0, m1, m2, m3,
    weights, damping, dens_col, table
):
    fill_table(own, (m0, m1, m2, m3), table, rows)

    def step(place, _):
        block = first + place
        turned = jnp.broadcast_to(second[pl.ds(block * rows, 1), :], (lanes, lanes)).T
        dens_col[pl.ds(pl.multiple_of(place * lanes, lanes), lanes), :] = turned
        tiles = [tile_at(table, plan[k, block]) for k in range(8)]
        for start in range(0, lanes, chunk):
            at = pl.ds(pl.multiple_of(block * lanes + start, chunk), chunk)
            to = pl.ds(pl.multiple_of(place * lanes + start, chunk), chunk)
            len_own = columns[at, 0:lanes]
            sound_own = columns[at, lanes : 2 * lanes]
            for k in range(8):
                part = slice(k * lanes, (k + 1) * lanes)
                inv_len = 1.0 / (len_own + tiles[k][3:4] * 0.05)
                ratio = distance[at, part] * inv_len
                wide = jnp.maximum(20.0 - ratio, 0.0) * inv_len
                narrow = jnp.maximum(10.0 - ratio, 0.0) * inv_len
                twice = narrow + narrow
                weight = wide * wide * wide - twice * twice * narrow
                rate = jnp.minimum(rates[at, part], 0.0)
                sounds = sound_own + tiles[k][7:8] * 0.75
                damping[to, part] = weight * rate * (rate - sounds)
                high, low = split2(weight)
                base = pl.multiple_of(place * 2 * lanes + start, chunk)
                weights[pl.ds(base, chunk), part] = high
                weights[pl.ds(base + lanes, chunk), part] = low
        return 0

    lax.fori_loop(0, 8, step, 0, unroll=2)


def momentum_kernel(
    plan, weights, damping, dens_col,
    own, m0, m1, m2, m3, second, s0, s1, s2, s3, accel, heating, *scratch
):
    table, masses, table2, sums, *scratch = scratch
    feats, damped = scratch[0:2], scratch[2:4]
    fill_table(own, (m0, m1, m2, m3), table, rows)
    fill_mass(own, (m0, m1, m2, m3), masses)
    fill_table(second, (s0, s1, s2, s3), table2, rows)
    ids = row_ids()
    picks = []
    for picked in ((2, 5, 6, 2), (5, 3, 7, 3), (6, 7, 4, 4)):
        places = jnp.full((rows, lanes), picked[3], jnp.int32)
        for at in range(3):
            places = jnp.where(lax.rem(ids, 4) == at, picked[at], places)
        picks.append(places)

    def features(tile, extra, mass):
        cols = [jnp.take_along_axis(extra, places, axis=0) for places in picks]
        heavy = tile * mass
        applied = None
        for axis in range(3):
            operand = jnp.where(ids < 4, tile[axis : axis + 1], tile[4 + axis : 5 + axis])
            term = cols[axis] * operand
            applied = term if applied is None else applied + term
        swirl = (
            applied[0:1] * tile[4:5] + applied[1:2] * tile[5:6] + applied[2:3] * tile[6:7]
        )
        applied = placed(applied, 3, swirl)
        press = extra[1:2] * mass
        parts = [jnp.where(ids == 3, mass, heavy)]
        parts += [heavy * tile[4 + axis : 5 + axis] for axis in range(3)]
        parts += [extra * mass, extra * press, applied * mass, applied * press]
        return jnp.concatenate(parts, axis=0)

    def prepare(block, buf):
        centre = centre_of(tile_at(table, block))
        for k in range(8):
            entry = plan[k, block]
            part = slice(k * lanes, (k + 1) * lanes)
            tile = tile_at(table, entry) - centre
            high, low = split2(
                features(tile, tile_at(table2, entry), masses[pl.ds(entry, 1), :])
            )
            feats[buf][0:64, part] = high
            feats[buf][64:128, part] = low

    def finish_part(weights, damping, dens_col, first, block, buf):
        place = block - first
        for start in range(0, lanes, chunk):
            at = pl.ds(pl.multiple_of(place * lanes + start, chunk), chunk)
            for k in range(8):
                dens_row = tile_at(table2, plan[k, block])[0:1]
                part = slice(k * lanes, (k + 1) * lanes)
                high, low = split2(damping[at, part] / (dens_col[at, :] + dens_row))
                damped[buf][start : start + chunk, part] = high
                damped[buf][lanes + start : lanes + start + chunk, part] = low
        own_weights = weights[pl.ds(pl.multiple_of(place * 2 * lanes, lanes), 2 * lanes), :]
        for base, value in ((0, own_weights), (64, damped[buf][...])):
            out = lax.dot_general(
                feats[buf][...], value, (((1,), (1,)), ((), ())), preferred_element_type=f32
            )
            out = out[0:64] + out[64:128]
            at = pl.ds(pl.multiple_of(block * lanes + base, 64), 64)
            sums[at, :] = out[:, 0:lanes] + out[:, lanes:]

    two_deep(prepare, functools.partial(finish_part, weights, damping, dens_col, 0))

    def mine(ref, field):
        return ref[pl.ds(field, 8, stride=rows), :]

    place = [mine(own, a) for a in range(3)]
    place = [value - (jnp.floor(value[:, 0:1]) + 0.5) for value in place]
    speed = [mine(own, 4 + a) for a in range(3)]
    pressure = mine(second, 1)
    order = ((2, 5, 6), (5, 3, 7), (6, 7, 4))
    matrix = [[mine(second, order[a][b]) for b in range(3)] for a in range(3)]

    def pieces(base):
        def total(field):
            return sums[pl.ds(base + field, 8, stride=lanes), :]

        mass = total(3)
        offset = [total(a) - place[a] * mass for a in range(3)]
        mass_v = [total(4 + a) for a in range(3)]
        applied = [
            matrix[a][0] * offset[0] + matrix[a][1] * offset[1] + matrix[a][2] * offset[2]
            for a in range(3)
        ]
        work = None
        for a in range(3):
            for b in range(3):
                cross = speed[a] * offset[b] - total(8 + 8 * a + b) + mass_v[a] * place[b]
                term = matrix[a][b] * cross
                work = term if work is None else work + term
        return total, applied, work

    def near_force(total, matrices, vectors):
        return [
            total(vectors + a)
            - total(matrices + order[a][0]) * place[0]
            - total(matrices + order[a][1]) * place[1]
            - total(matrices + order[a][2]) * place[2]
            for a in range(3)
        ]

    norm = 16.0 / math.pi / 20.0**6
    total, applied, work = pieces(0)
    pushed = near_force(total, 40, 56)
    total2, applied2, work2 = pieces(64)
    pushed2 = near_force(total2, 32, 48)
    for a in range(3):
        value = -norm * (
            pressure * applied[a] + pushed[a] + (2.0 / 9.0) * (applied2[a] + pushed2[a])
        )
        for block in range(8):
            part = slice(block * lanes, (block + 1) * lanes)
            accel[a : a + 1, part] = value[block : block + 1, :]
    near_work = (
        speed[0] * pushed2[0]
        + speed[1] * pushed2[1]
        + speed[2] * pushed2[2]
        - total2(51)
        + place[0] * total2(52)
        + place[1] * total2(53)
        + place[2] * total2(54)
    )
    heating[...] = norm * (pressure * work + (1.0 / 9.0) * (work2 + near_work))


def call(kernel, outs, scratch, smem, args, flops, limit):
    return pl.pallas_call(
        kernel,
        out_shape=[jax.ShapeDtypeStruct(shape, kind) for shape, kind in outs],
        in_specs=[smem_spec] * smem + [vmem_spec] * (len(args) - smem),
        out_specs=[vmem_spec] * len(outs),
        scratch_shapes=[pltpu.VMEM(shape, kind) for shape, kind in scratch],
        compiler_params=pltpu.CompilerParams(vmem_limit_bytes=limit * 1024 * 1024),
        cost_estimate=pl.CostEstimate(flops=flops, bytes_accessed=200000, transcendentals=0),
    )(*args)


def fold(value, axis, step):
    size = lax.axis_size(axis)
    return jnp.minimum(value, lax.ppermute(value, axis, [(i, i ^ step) for i in range(size)]))


def body(positions, velocities, mass, smoothing, energy, send_offsets, send_counts, pair_blocks):
    points = positions.shape[1]
    send_offsets, send_counts = send_offsets.reshape(1, 4), send_counts.reshape(1, 4)
    tile = ((rows, lanes), f32)
    packed = ((72, lanes), f32)
    own, *outgoing = pl.pallas_call(
        pack_kernel,
        out_shape=[jax.ShapeDtypeStruct((80, lanes), f32)] + [jax.ShapeDtypeStruct(*packed)] * 4,
        in_specs=[vmem_spec] * 5 + [smem_spec] * 2,
        out_specs=[vmem_spec] * 5,
    )(
        positions,
        velocities,
        mass.reshape(8, lanes),
        smoothing.reshape(8, lanes),
        energy.reshape(8, lanes),
        send_offsets,
        send_counts,
    )
    received = [swap(value, axis, odd) for value, (axis, odd, _) in zip(outgoing, swaps)]
    last = (1, 2, 3)
    steps = [("dom", 1 << bit) for bit in range(2, lax.axis_size("dom").bit_length() - 1)]
    steps += [("slab", 1 << bit) for bit in reversed(range(lax.axis_size("slab").bit_length() - 1))]
    left, columns, own, plan = pl.pallas_call(
        own_kernel,
        out_shape=[
            jax.ShapeDtypeStruct((8 * lanes, lanes), bf16),
            jax.ShapeDtypeStruct((8 * lanes, 3 * lanes), f32),
            jax.ShapeDtypeStruct((80, lanes), f32),
            jax.ShapeDtypeStruct(pair_blocks.shape, jnp.int32),
        ],
        in_specs=[vmem_spec] * 2,
        out_specs=[vmem_spec] * 4,
        compiler_params=pltpu.CompilerParams(vmem_limit_bytes=8 * 1024 * 1024),
    )(pair_blocks, own)
    table = ((328, lanes), f32)
    masses = ((48, lanes), f32)
    near = ((lanes, 16 * lanes), bf16)
    feats = ((64, 8 * lanes), bf16)
    halves = ((2 * lanes, 8 * lanes), bf16)
    square = ((8 * lanes, 8 * lanes), f32)
    allowed, smallest, distance, rates = call(
        signal_kernel,
        [tile, tile, square, square],
        [table, near, near],
        1,
        (plan, left, columns, own, *received),
        3 * 10**9,
        20,
    )
    smallest = fold(smallest, *steps[0])
    density, second, *outgoing2 = call(
        density_kernel,
        [tile] + [packed] + [((64, lanes), f32)] * 4,
        [table, masses, ((9 * 32, lanes), f32)] + [feats] * 2 + [halves] * 2,
        3,
        (plan, send_offsets, send_counts, columns, distance, own, *received),
        5 * 10**9,
        20,
    )
    smallest, outgoing2 = lax.optimization_barrier((smallest, outgoing2))
    received2 = [swap(value, axis, odd) for value, (axis, odd, _) in zip(outgoing2, swaps)]
    parts = []
    smallest = fold(smallest, *steps[1])
    for first in (0,):
        smallest = fold(smallest, *steps[2])
        weights, damping, dens_col = call(
            functools.partial(weight_kernel, first),
            [((16 * lanes, 8 * lanes), bf16), ((8 * lanes, 8 * lanes), f32), ((8 * lanes, lanes), f32)],
            [table],
            1,
            (plan, columns, distance, rates, second, own, *received),
            10**9,
            20,
        )
        smallest, distance, weights = lax.optimization_barrier((smallest, distance, weights))
        parts += [weights, damping, dens_col]
    for step in steps[3:]:
        smallest = fold(smallest, *step)
    smallest, received2 = lax.optimization_barrier((smallest, received2))
    accel, heating = call(
        momentum_kernel,
        [((3, points), f32), tile],
        [table, masses, table, ((9 * lanes, lanes), f32)]
        + [((lanes, 8 * lanes), bf16)] * 2
        + [halves] * 2,
        1,
        (plan, *parts, own, *received, second, *received2),
        5 * 10**9,
        20,
    )
    size = lax.axis_size("dom")
    moved = [
        lax.ppermute(smallest, "dom", [(i, i ^ step) for i in range(size)]) for step in last
    ]
    for value in moved:
        smallest = jnp.minimum(smallest, value)
    share = smallest / allowed
    return (density.reshape(points), accel, heating.reshape(points), share.reshape(points))


def solution(mesh):
    both = ("slab", "dom")
    wide, flat = P(None, both), P(both)
    in_specs = (wide, wide, flat, flat, flat, wide, wide, wide)
    out_specs = (flat, wide, flat, flat)
    return jax.shard_map(body, mesh=mesh, in_specs=in_specs, out_specs=out_specs, check_vma=False)
```

```python
import functools
import math

import jax
import jax.numpy as jnp
from jax import lax
from jax.experimental import pallas as pl
from jax.experimental.pallas import tpu as pltpu
from jax.sharding import PartitionSpec as P

gas_gamma = 5.0 / 3.0
courant = 0.4
f32 = jnp.float32
bf16 = jnp.bfloat16
rows = 8
lanes = 128
tiny = 1e-12
chunk = 32
swaps = (("dom", 0, 2), ("slab", 0, 0), ("dom", 1, 2), ("slab", 1, 0))
vmem_spec = pl.BlockSpec(memory_space=pltpu.VMEM)
smem_spec = pl.BlockSpec(memory_space=pltpu.SMEM)


def partner(axis, odd, base):
    place = lax.axis_index(axis)
    size = lax.axis_size(axis)
    upward = lax.rem(place + odd, 2) == 0
    direction = base + jnp.where(upward, 1, 0)
    exists = jnp.where(upward, place < size - 1, place > 0)
    return direction, exists


def swap(value, axis, odd):
    size = lax.axis_size(axis)
    pairs = [
        (i, (i + 1) % size if (i - odd) % 2 == 0 else (i - 1) % size) for i in range(size)
    ]
    return lax.ppermute(value, axis, pairs)


def split2(value):
    high = value.astype(bf16)
    low = (value - high.astype(f32)).astype(bf16)
    return high, low


def split3(value):
    first = value.astype(bf16).astype(f32)
    rest = value - first
    second = rest.astype(bf16).astype(f32)
    return first, second, rest - second


def row_ids():
    return lax.broadcasted_iota(jnp.int32, (rows, lanes), 0)


def centre_of(tile):
    corner = jnp.floor(tile[:, 0:1]) + 0.5
    return jnp.where(row_ids() < 3, jnp.broadcast_to(corner, tile.shape), 0.0)


def sum_xyz(tile, start):
    return tile[start : start + 1] + tile[start + 1 : start + 2] + tile[start + 2 : start + 3]


def placed(tile, at, row):
    return jnp.where(row_ids() == at, jnp.broadcast_to(row, tile.shape), tile)


def near_operand(tile):
    norm = sum_xyz(tile * tile, 0)
    drift = (
        tile[0:1] * tile[4:5] + tile[1:2] * tile[5:6] + tile[2:3] * tile[6:7]
    )
    first, second, third = split3(placed(placed(tile, 3, norm), 7, drift))
    ones = jnp.where(row_ids() < 3, 1.0, 0.0)
    stacked = [first, second, third, first, second, first, ones, jnp.zeros_like(ones)]
    return jnp.concatenate(stacked, axis=0).astype(bf16)


def own_operand(tile, own_term):
    first, second, third = split3(tile)
    parts = split3(own_term)
    ones = jnp.zeros((rows, lanes), f32)
    for at in range(3):
        ones = placed(ones, at, parts[at])
    stacked = [first, first, first, second, second, third, ones, jnp.zeros_like(ones)]
    return jnp.concatenate(stacked, axis=0)


def own_distance(tile):
    norm = sum_xyz(tile * tile, 0)
    ids = row_ids()
    left = jnp.where(ids < 3, -2.0 * tile, jnp.where(ids == 3, 1.0, 0.0))
    return own_operand(left, norm)


def own_closing(tile, scale):
    drift = (
        tile[0:1] * tile[4:5] + tile[1:2] * tile[5:6] + tile[2:3] * tile[6:7]
    )
    ids = row_ids()
    left = jnp.concatenate([-tile[4:8], -tile[0:4]], axis=0)
    left = jnp.where(ids == 3, 0.0, jnp.where(ids == 7, 1.0, left))
    return own_operand(left * scale, drift * scale)


def fill_table(own, received, table, width):
    table[0 : 8 * width, :] = own[0 : 8 * width, :]
    for message, (axis, odd, base) in zip(received, swaps):
        direction, _ = partner(axis, odd, base)
        start = pl.multiple_of((direction + 1) * (8 * width), 8 * width)
        table[pl.ds(start, 8 * width), :] = message[0 : 8 * width, :]
    table[40 * width : 40 * width + 8, :] = jnp.zeros((8, lanes), f32)


def fill_mass(own, received, masses):
    masses[0:8, :] = own[64:72, :]
    for message, (axis, odd, base) in zip(received, swaps):
        direction, _ = partner(axis, odd, base)
        start = pl.multiple_of((direction + 1) * 8, 8)
        masses[pl.ds(start, 8), :] = message[64:72, :]
    masses[40:48, :] = jnp.zeros((8, lanes), f32)


def tile_at(table, entry):
    return table[pl.ds(pl.multiple_of(entry * rows, rows), rows), :]


def cut_windows(offset_of, count_of, source, outgoing, masses):
    for target, (axis, odd, base) in zip(outgoing, swaps):
        direction, exists = partner(axis, odd, base)
        offset = offset_of(direction)
        count = jnp.where(exists, count_of(direction), 0)
        for slot in range(8):
            block = jnp.minimum(offset + slot, 7)
            keep = slot < count
            tile = tile_at(source, block)
            target[slot * rows : (slot + 1) * rows, :] = jnp.where(keep, tile, 0.0)
            if masses:
                row = source[pl.ds(64 + block, 1), :]
                target[64 + slot : 65 + slot, :] = jnp.where(keep, row, 0.0)


def pack_kernel(positions, velocities, mass, smoothing, energy, offsets, counts, own, *outgoing):
    sound = jnp.sqrt(gas_gamma * (gas_gamma - 1.0) * energy[...])
    for block in range(8):
        part = slice(block * lanes, (block + 1) * lanes)
        at = block * rows
        own[at : at + 3, :] = positions[:, part]
        own[at + 4 : at + 7, :] = velocities[:, part]
    own[pl.ds(3, 8, stride=rows), :] = smoothing[...]
    own[pl.ds(7, 8, stride=rows), :] = sound
    own[64:72, :] = mass[...]
    own[72:80, :] = energy[...]
    cut_windows(lambda r: offsets[0, r], lambda r: counts[0, r], own, outgoing, True)


def two_deep(prepare, finish, first=0, last=8):
    prepare(first, 0)

    def step(half, _):
        block = first + half * 2
        prepare(block + 1, 1)
        finish(block, 0)
        prepare(jnp.minimum(block + 2, last - 1), 0)
        finish(block + 1, 1)
        return 0

    lax.fori_loop(0, (last - first) // 2, step, 0, unroll=True)


def own_kernel(pairs, own, left, columns, table, plan):
    table[...] = own[...]
    plan[...] = pairs[...]

    def step(block, _):
        tile = tile_at(own, block)
        centred = tile - centre_of(tile)
        stacked = jnp.concatenate([own_distance(centred), own_closing(centred, 30.0)], axis=0)
        at = pl.ds(pl.multiple_of(block * lanes, lanes), lanes)
        left[at, :] = stacked.T.astype(bf16)
        turned = tile.T
        length = turned[:, 3:4]
        columns[at, 0:lanes] = jnp.broadcast_to(length * 0.05, (lanes, lanes))
        columns[at, lanes : 2 * lanes] = jnp.broadcast_to(turned[:, 7:8] * 0.75, (lanes, lanes))
        columns[at, 2 * lanes :] = jnp.broadcast_to(0.5 / length, (lanes, lanes))
        return 0

    lax.fori_loop(0, 8, step, 0, unroll=True)


def put_near(near, k, tile):
    operand = near_operand(tile)
    at = 2 * k * lanes
    near[0:64, at : at + lanes] = operand
    near[64:128, at + lanes : at + 2 * lanes] = operand


def clear_near(buffers):
    for near in buffers:
        near[...] = jnp.zeros(near.shape, bf16)


def pair_dots(left, near, block, k):
    at = pl.ds(pl.multiple_of(block * lanes, lanes), lanes)
    part = slice(2 * k * lanes, 2 * (k + 1) * lanes)
    both = jnp.dot(left[at, :], near[:, part], preferred_element_type=f32)
    return both[:, 0:lanes], both[:, lanes:]


def signal_kernel(
    plan, left, columns, own, m0, m1, m2, m3, allowed, smallest, distance, rates, table, *near
):
    clear_near(near)
    fill_table(own, (m0, m1, m2, m3), table, rows)

    def prepare(block, buf):
        centre = centre_of(tile_at(table, block))
        for k in range(8):
            put_near(near[buf], k, tile_at(table, plan[k, block]) - centre)

    def finish(block, buf):
        best = None
        sounds = None
        for k in range(8):
            tile = tile_at(table, plan[k, block])
            len_row, sound_row = tile[3:4] * 0.05, tile[7:8]
            sounds = sound_row if k == 0 else jnp.maximum(sounds, sound_row)
            part = slice(k * lanes, (k + 1) * lanes)
            at = pl.ds(pl.multiple_of(block * lanes, lanes), lanes)
            dist_sq, closing = pair_dots(left, near[buf], block, k)
            dist_sq = jnp.maximum(dist_sq, tiny)
            distance[at, part] = dist_sq * lax.rsqrt(dist_sq)
            mean_len = columns[at, 0:lanes] + len_row
            rate = closing * mean_len / (dist_sq + mean_len * mean_len)
            rates[at, part] = rate
            signal = sound_row - rate
            best = signal if k == 0 else jnp.maximum(best, signal)
        top = jnp.max(best.T, axis=0, keepdims=True)
        top = jnp.maximum(top, jnp.max(sounds, axis=1, keepdims=True))
        own_tile = tile_at(table, block)
        allowed[pl.ds(block, 1), :] = courant * own_tile[3:4] / (own_tile[7:8] + top)

    two_deep(prepare, finish)
    least = jnp.min(allowed[...], axis=(0, 1), keepdims=True)
    smallest[...] = jnp.broadcast_to(least, (rows, lanes))


def density_kernel(
    plan, offsets, counts, columns, distance, own, m0, m1, m2, m3, second, *rest
):
    outgoing = rest[0:4]
    table, masses, sums, *scratch = rest[4:]
    feats, weights = scratch[0:2], scratch[2:4]
    fill_table(own, (m0, m1, m2, m3), table, rows)
    fill_mass(own, (m0, m1, m2, m3), masses)

    def prepare(block, buf):
        centre = centre_of(tile_at(table, block))
        ids = row_ids()
        for k in range(8):
            entry = plan[k, block]
            part = slice(k * lanes, (k + 1) * lanes)
            tile = tile_at(table, entry) - centre
            weighed = jnp.where(ids == 3, 1.0, tile) * masses[pl.ds(entry, 1), :]
            stacked = jnp.concatenate(
                [weighed, weighed * tile[0:1], weighed * tile[1:2], weighed * tile[2:3]], axis=0
            )
            high, low = split2(stacked)
            feats[buf][0:32, part] = high
            feats[buf][32:64, part] = low

    def finish(block, buf):
        for start in range(0, lanes, 2 * chunk):
            at = pl.ds(pl.multiple_of(block * lanes + start, 2 * chunk), 2 * chunk)
            scale = columns[at, 2 * lanes :]
            for k in range(8):
                part = slice(k * lanes, (k + 1) * lanes)
                ratio = distance[at, part] * scale
                wide = jnp.maximum(1.0 - ratio, 0.0)
                narrow = jnp.maximum(0.5 - ratio, 0.0)
                twice = narrow + narrow
                high, low = split2(wide * wide * wide - twice * twice * narrow)
                weights[buf][start : start + 2 * chunk, part] = high
                weights[buf][lanes + start : lanes + start + 2 * chunk, part] = low
        out = lax.dot_general(
            feats[buf][...], weights[buf][...], (((1,), (1,)), ((), ())), preferred_element_type=f32
        )
        out = out[0:32] + out[32:64]
        sums[pl.ds(block, 32, stride=8), :] = out[:, 0:lanes] + out[:, lanes:]

    two_deep(prepare, finish)

    def total(field):
        return sums[field * 8 : (field + 1) * 8, :]

    def mine(field):
        return own[pl.ds(field, 8, stride=rows), :]

    length = mine(3)
    place = [mine(a) for a in range(3)]
    place = [value - (jnp.floor(value[:, 0:1]) + 0.5) for value in place]
    whole = total(3)
    dens = whole * (2.0 / math.pi) / (length * length * length)
    first = [total(a) for a in range(3)]
    inverse = 1.0 / whole
    floor = 0.05 * length * length

    def moment(a, b):
        raw = total(8 + 8 * a + b) - place[a] * first[b] - place[b] * first[a]
        return (raw + place[a] * place[b] * whole) * inverse

    axx = moment(0, 0) + floor
    ayy = moment(1, 1) + floor
    azz = moment(2, 2) + floor
    axy, axz, ayz = moment(0, 1), moment(0, 2), moment(1, 2)
    cof_xx = ayy * azz - ayz * ayz
    cof_yy = axx * azz - axz * axz
    cof_zz = axx * ayy - axy * axy
    cof_xy = axz * ayz - axy * azz
    cof_xz = axy * ayz - ayy * axz
    cof_yz = axy * axz - axx * ayz
    inv_det = 1.0 / (axx * cof_xx + axy * cof_xy + axz * cof_xz)
    pressure = (gas_gamma - 1.0) * own[72:80, :] / dens
    fields = [dens, pressure, cof_xx * inv_det, cof_yy * inv_det, cof_zz * inv_det]
    fields += [cof_xy * inv_det, cof_xz * inv_det, cof_yz * inv_det]
    for field in range(8):
        second[pl.ds(field, 8, stride=rows), :] = fields[field]
    cut_windows(lambda r: offsets[0, r], lambda r: counts[0, r], second, outgoing, False)


def weight_kernel(
    first, plan, columns, distance, rates, second, own, m0, m1, m2, m3,
    weights, damping, dens_col, table
):
    fill_table(own, (m0, m1, m2, m3), table, rows)

    def step(place, _):
        block = first + place
        turned = jnp.broadcast_to(second[pl.ds(block * rows, 1), :], (lanes, lanes)).T
        dens_col[pl.ds(pl.multiple_of(place * lanes, lanes), lanes), :] = turned
        tiles = [tile_at(table, plan[k, block]) for k in range(8)]
        for start in range(0, lanes, chunk):
            at = pl.ds(pl.multiple_of(block * lanes + start, chunk), chunk)
            to = pl.ds(pl.multiple_of(place * lanes + start, chunk), chunk)
            len_own = columns[at, 0:lanes]
            sound_own = columns[at, lanes : 2 * lanes]
            for k in range(8):
                part = slice(k * lanes, (k + 1) * lanes)
                inv_len = 1.0 / (len_own + tiles[k][3:4] * 0.05)
                ratio = distance[at, part] * inv_len
                wide = jnp.maximum(20.0 - ratio, 0.0) * inv_len
                narrow = jnp.maximum(10.0 - ratio, 0.0) * inv_len
                twice = narrow + narrow
                weight = wide * wide * wide - twice * twice * narrow
                rate = jnp.minimum(rates[at, part], 0.0)
                sounds = sound_own + tiles[k][7:8] * 0.75
                damping[to, part] = weight * rate * (rate - sounds)
                high, low = split2(weight)
                base = pl.multiple_of(place * 2 * lanes + start, chunk)
                weights[pl.ds(base, chunk), part] = high
                weights[pl.ds(base + lanes, chunk), part] = low
        return 0

    lax.fori_loop(0, 8, step, 0, unroll=2)


def momentum_kernel(
    plan, weights, damping, dens_col,
    own, m0, m1, m2, m3, second, s0, s1, s2, s3, accel, heating, density, *scratch
):
    table, masses, table2, sums, *scratch = scratch
    feats, damped = scratch[0:2], scratch[2:4]
    fill_table(own, (m0, m1, m2, m3), table, rows)
    fill_mass(own, (m0, m1, m2, m3), masses)
    fill_table(second, (s0, s1, s2, s3), table2, rows)
    ids = row_ids()
    picks = []
    for picked in ((2, 5, 6, 2), (5, 3, 7, 3), (6, 7, 4, 4)):
        places = jnp.full((rows, lanes), picked[3], jnp.int32)
        for at in range(3):
            places = jnp.where(lax.rem(ids, 4) == at, picked[at], places)
        picks.append(places)

    def features(tile, extra, mass):
        cols = [jnp.take_along_axis(extra, places, axis=0) for places in picks]
        heavy = tile * mass
        applied = None
        for axis in range(3):
            operand = jnp.where(ids < 4, tile[axis : axis + 1], tile[4 + axis : 5 + axis])
            term = cols[axis] * operand
            applied = term if applied is None else applied + term
        swirl = (
            applied[0:1] * tile[4:5] + applied[1:2] * tile[5:6] + applied[2:3] * tile[6:7]
        )
        applied = placed(applied, 3, swirl)
        press = extra[1:2] * mass
        parts = [jnp.where(ids == 3, mass, heavy)]
        parts += [heavy * tile[4 + axis : 5 + axis] for axis in range(3)]
        parts += [extra * mass, extra * press, applied * mass, applied * press]
        return jnp.concatenate(parts, axis=0)

    def prepare(block, buf):
        centre = centre_of(tile_at(table, block))
        for k in range(8):
            entry = plan[k, block]
            part = slice(k * lanes, (k + 1) * lanes)
            tile = tile_at(table, entry) - centre
            high, low = split2(
                features(tile, tile_at(table2, entry), masses[pl.ds(entry, 1), :])
            )
            feats[buf][0:64, part] = high
            feats[buf][64:128, part] = low

    def finish_part(weights, damping, dens_col, first, block, buf):
        place = block - first
        for start in range(0, lanes, chunk):
            at = pl.ds(pl.multiple_of(place * lanes + start, chunk), chunk)
            for k in range(8):
                dens_row = tile_at(table2, plan[k, block])[0:1]
                part = slice(k * lanes, (k + 1) * lanes)
                high, low = split2(damping[at, part] / (dens_col[at, :] + dens_row))
                damped[buf][start : start + chunk, part] = high
                damped[buf][lanes + start : lanes + start + chunk, part] = low
        own_weights = weights[pl.ds(pl.multiple_of(place * 2 * lanes, lanes), 2 * lanes), :]
        for base, value in ((0, own_weights), (64, damped[buf][...])):
            out = lax.dot_general(
                feats[buf][...], value, (((1,), (1,)), ((), ())), preferred_element_type=f32
            )
            out = out[0:64] + out[64:128]
            sums[pl.ds(base * 8 + block, 64, stride=8), :] = out[:, 0:lanes] + out[:, lanes:]

    two_deep(prepare, functools.partial(finish_part, weights, damping, dens_col, 0))

    def mine(ref, field):
        return ref[pl.ds(field, 8, stride=rows), :]

    place = [mine(own, a) for a in range(3)]
    place = [value - (jnp.floor(value[:, 0:1]) + 0.5) for value in place]
    speed = [mine(own, 4 + a) for a in range(3)]
    density[...] = mine(second, 0)
    pressure = mine(second, 1)
    order = ((2, 5, 6), (5, 3, 7), (6, 7, 4))
    matrix = [[mine(second, order[a][b]) for b in range(3)] for a in range(3)]

    def pieces(base):
        def total(field):
            return sums[(base + field) * 8 : (base + field + 1) * 8, :]

        mass = total(3)
        offset = [total(a) - place[a] * mass for a in range(3)]
        mass_v = [total(4 + a) for a in range(3)]
        applied = [
            matrix[a][0] * offset[0] + matrix[a][1] * offset[1] + matrix[a][2] * offset[2]
            for a in range(3)
        ]
        work = None
        for a in range(3):
            for b in range(3):
                cross = speed[a] * offset[b] - total(8 + 8 * a + b) + mass_v[a] * place[b]
                term = matrix[a][b] * cross
                work = term if work is None else work + term
        return total, applied, work

    def near_force(total, matrices, vectors):
        return [
            total(vectors + a)
            - total(matrices + order[a][0]) * place[0]
            - total(matrices + order[a][1]) * place[1]
            - total(matrices + order[a][2]) * place[2]
            for a in range(3)
        ]

    norm = 16.0 / math.pi / 20.0**6
    total, applied, work = pieces(0)
    pushed = near_force(total, 40, 56)
    total2, applied2, work2 = pieces(64)
    pushed2 = near_force(total2, 32, 48)
    for a in range(3):
        value = -norm * (
            pressure * applied[a] + pushed[a] + (2.0 / 9.0) * (applied2[a] + pushed2[a])
        )
        for block in range(8):
            part = slice(block * lanes, (block + 1) * lanes)
            accel[a : a + 1, part] = value[block : block + 1, :]
    near_work = (
        speed[0] * pushed2[0]
        + speed[1] * pushed2[1]
        + speed[2] * pushed2[2]
        - total2(51)
        + place[0] * total2(52)
        + place[1] * total2(53)
        + place[2] * total2(54)
    )
    heating[...] = norm * (pressure * work + (1.0 / 9.0) * (work2 + near_work))


def call(kernel, outs, scratch, smem, args, flops, limit):
    return pl.pallas_call(
        kernel,
        out_shape=[jax.ShapeDtypeStruct(shape, kind) for shape, kind in outs],
        in_specs=[smem_spec] * smem + [vmem_spec] * (len(args) - smem),
        out_specs=[vmem_spec] * len(outs),
        scratch_shapes=[pltpu.VMEM(shape, kind) for shape, kind in scratch],
        compiler_params=pltpu.CompilerParams(vmem_limit_bytes=limit * 1024 * 1024),
        cost_estimate=pl.CostEstimate(flops=flops, bytes_accessed=200000, transcendentals=0),
    )(*args)


def fold(value, axis, step):
    size = lax.axis_size(axis)
    return jnp.minimum(value, lax.ppermute(value, axis, [(i, i ^ step) for i in range(size)]))


def body(positions, velocities, mass, smoothing, energy, send_offsets, send_counts, pair_blocks):
    points = positions.shape[1]
    send_offsets, send_counts = send_offsets.reshape(1, 4), send_counts.reshape(1, 4)
    tile = ((rows, lanes), f32)
    packed = ((72, lanes), f32)
    own, *outgoing = pl.pallas_call(
        pack_kernel,
        out_shape=[jax.ShapeDtypeStruct((80, lanes), f32)] + [jax.ShapeDtypeStruct(*packed)] * 4,
        in_specs=[vmem_spec] * 5 + [smem_spec] * 2,
        out_specs=[vmem_spec] * 5,
    )(
        positions,
        velocities,
        mass.reshape(8, lanes),
        smoothing.reshape(8, lanes),
        energy.reshape(8, lanes),
        send_offsets,
        send_counts,
    )
    received = [swap(value, axis, odd) for value, (axis, odd, _) in zip(outgoing, swaps)]
    last = (1, 2, 3)
    steps = [("dom", 1 << bit) for bit in range(2, lax.axis_size("dom").bit_length() - 1)]
    steps += [("slab", 1 << bit) for bit in reversed(range(lax.axis_size("slab").bit_length() - 1))]
    left, columns, own, plan = pl.pallas_call(
        own_kernel,
        out_shape=[
            jax.ShapeDtypeStruct((8 * lanes, lanes), bf16),
            jax.ShapeDtypeStruct((8 * lanes, 3 * lanes), f32),
            jax.ShapeDtypeStruct((80, lanes), f32),
            jax.ShapeDtypeStruct(pair_blocks.shape, jnp.int32),
        ],
        in_specs=[vmem_spec] * 2,
        out_specs=[vmem_spec] * 4,
        compiler_params=pltpu.CompilerParams(vmem_limit_bytes=8 * 1024 * 1024),
    )(pair_blocks, own)
    table = ((328, lanes), f32)
    masses = ((48, lanes), f32)
    near = ((lanes, 16 * lanes), bf16)
    feats = ((64, 8 * lanes), bf16)
    halves = ((2 * lanes, 8 * lanes), bf16)
    square = ((8 * lanes, 8 * lanes), f32)
    allowed, smallest, distance, rates = call(
        signal_kernel,
        [tile, tile, square, square],
        [table, near, near],
        1,
        (plan, left, columns, own, *received),
        3 * 10**9,
        20,
    )
    smallest = fold(smallest, *steps[0])
    second, *outgoing2 = call(
        density_kernel,
        [packed] + [((64, lanes), f32)] * 4,
        [table, masses, ((9 * 32, lanes), f32)] + [feats] * 2 + [halves] * 2,
        3,
        (plan, send_offsets, send_counts, columns, distance, own, *received),
        5 * 10**9,
        20,
    )
    smallest, outgoing2 = lax.optimization_barrier((smallest, outgoing2))
    received2 = [swap(value, axis, odd) for value, (axis, odd, _) in zip(outgoing2, swaps)]
    parts = []
    smallest = fold(smallest, *steps[1])
    for first in (0,):
        smallest = fold(smallest, *steps[2])
        weights, damping, dens_col = call(
            functools.partial(weight_kernel, first),
            [((16 * lanes, 8 * lanes), bf16), ((8 * lanes, 8 * lanes), f32), ((8 * lanes, lanes), f32)],
            [table],
            1,
            (plan, columns, distance, rates, second, own, *received),
            10**9,
            20,
        )
        smallest, distance, weights = lax.optimization_barrier((smallest, distance, weights))
        parts += [weights, damping, dens_col]
    for step in steps[3:]:
        smallest = fold(smallest, *step)
    smallest, received2 = lax.optimization_barrier((smallest, received2))
    accel, heating, density = call(
        momentum_kernel,
        [((3, points), f32), tile, tile],
        [table, masses, table, ((9 * lanes, lanes), f32)]
        + [((lanes, 8 * lanes), bf16)] * 2
        + [halves] * 2,
        1,
        (plan, *parts, own, *received, second, *received2),
        5 * 10**9,
        20,
    )
    size = lax.axis_size("dom")
    moved = [
        lax.ppermute(smallest, "dom", [(i, i ^ step) for i in range(size)]) for step in last
    ]
    for value in moved:
        smallest = jnp.minimum(smallest, value)
    share = smallest / allowed
    return (density.reshape(points), accel, heating.reshape(points), share.reshape(points))


def solution(mesh):
    both = ("slab", "dom")
    wide, flat = P(None, both), P(both)
    in_specs = (wide, wide, flat, flat, flat, wide, wide, wide)
    out_specs = (flat, wide, flat, flat)
    return jax.shard_map(body, mesh=mesh, in_specs=in_specs, out_specs=out_specs, check_vma=False)
```

```python
import functools
import math

import jax
import jax.numpy as jnp
from jax import lax
from jax.experimental import pallas as pl
from jax.experimental.pallas import tpu as pltpu
from jax.sharding import PartitionSpec as P

gas_gamma = 5.0 / 3.0
courant = 0.4
f32 = jnp.float32
bf16 = jnp.bfloat16
rows = 8
lanes = 128
tiny = 1e-12
chunk = 32
narrow_rows = 16
swaps = (("dom", 0, 2), ("slab", 0, 0), ("dom", 1, 2), ("slab", 1, 0))
vmem_spec = pl.BlockSpec(memory_space=pltpu.VMEM)
smem_spec = pl.BlockSpec(memory_space=pltpu.SMEM)


def partner(axis, odd, base):
    place = lax.axis_index(axis)
    size = lax.axis_size(axis)
    upward = lax.rem(place + odd, 2) == 0
    direction = base + jnp.where(upward, 1, 0)
    exists = jnp.where(upward, place < size - 1, place > 0)
    return direction, exists


def swap(value, axis, odd):
    size = lax.axis_size(axis)
    pairs = [
        (i, (i + 1) % size if (i - odd) % 2 == 0 else (i - 1) % size) for i in range(size)
    ]
    return lax.ppermute(value, axis, pairs)


def split2(value):
    high = value.astype(bf16)
    low = (value - high.astype(f32)).astype(bf16)
    return high, low


def split3(value):
    first = value.astype(bf16).astype(f32)
    rest = value - first
    second = rest.astype(bf16).astype(f32)
    return first, second, rest - second


def row_ids():
    return lax.broadcasted_iota(jnp.int32, (rows, lanes), 0)


def centre_of(tile):
    corner = jnp.floor(tile[:, 0:1]) + 0.5
    return jnp.where(row_ids() < 3, jnp.broadcast_to(corner, tile.shape), 0.0)


def sum_xyz(tile, start):
    return tile[start : start + 1] + tile[start + 1 : start + 2] + tile[start + 2 : start + 3]


def placed(tile, at, row):
    return jnp.where(row_ids() == at, jnp.broadcast_to(row, tile.shape), tile)


def near_operand(tile):
    norm = sum_xyz(tile * tile, 0)
    drift = (
        tile[0:1] * tile[4:5] + tile[1:2] * tile[5:6] + tile[2:3] * tile[6:7]
    )
    first, second, third = split3(placed(placed(tile, 3, norm), 7, drift))
    ones = jnp.where(row_ids() < 3, 1.0, 0.0)
    stacked = [first, second, third, first, second, first, ones, jnp.zeros_like(ones)]
    return jnp.concatenate(stacked, axis=0).astype(bf16)


def own_operand(tile, own_term):
    first, second, third = split3(tile)
    parts = split3(own_term)
    ones = jnp.zeros((rows, lanes), f32)
    for at in range(3):
        ones = placed(ones, at, parts[at])
    stacked = [first, first, first, second, second, third, ones, jnp.zeros_like(ones)]
    return jnp.concatenate(stacked, axis=0)


def own_distance(tile):
    norm = sum_xyz(tile * tile, 0)
    ids = row_ids()
    left = jnp.where(ids < 3, -2.0 * tile, jnp.where(ids == 3, 1.0, 0.0))
    return own_operand(left, norm)


def own_closing(tile, scale):
    drift = (
        tile[0:1] * tile[4:5] + tile[1:2] * tile[5:6] + tile[2:3] * tile[6:7]
    )
    ids = row_ids()
    left = jnp.concatenate([-tile[4:8], -tile[0:4]], axis=0)
    left = jnp.where(ids == 3, 0.0, jnp.where(ids == 7, 1.0, left))
    return own_operand(left * scale, drift * scale)


def fill_table(own, received, table, width):
    table[0 : 8 * width, :] = own[0 : 8 * width, :]
    for message, (axis, odd, base) in zip(received, swaps):
        direction, _ = partner(axis, odd, base)
        start = pl.multiple_of((direction + 1) * (8 * width), 8 * width)
        table[pl.ds(start, 8 * width), :] = message[0 : 8 * width, :]
    table[40 * width : 40 * width + 8, :] = jnp.zeros((8, lanes), f32)


def fill_mass(own, received, masses):
    masses[0:8, :] = own[64:72, :]
    for message, (axis, odd, base) in zip(received, swaps):
        direction, _ = partner(axis, odd, base)
        start = pl.multiple_of((direction + 1) * 8, 8)
        masses[pl.ds(start, 8), :] = message[64:72, :]
    masses[40:48, :] = jnp.zeros((8, lanes), f32)


def tile_at(table, entry):
    return table[pl.ds(pl.multiple_of(entry * rows, rows), rows), :]


def cut_windows(offset_of, count_of, source, outgoing, masses):
    for target, (axis, odd, base) in zip(outgoing, swaps):
        direction, exists = partner(axis, odd, base)
        offset = offset_of(direction)
        count = jnp.where(exists, count_of(direction), 0)
        for slot in range(8):
            block = jnp.minimum(offset + slot, 7)
            keep = slot < count
            tile = tile_at(source, block)
            target[slot * rows : (slot + 1) * rows, :] = jnp.where(keep, tile, 0.0)
            if masses:
                row = source[pl.ds(64 + block, 1), :]
                target[64 + slot : 65 + slot, :] = jnp.where(keep, row, 0.0)


def pack_kernel(positions, velocities, mass, smoothing, energy, offsets, counts, own, *outgoing):
    sound = jnp.sqrt(gas_gamma * (gas_gamma - 1.0) * energy[...])
    for block in range(8):
        part = slice(block * lanes, (block + 1) * lanes)
        at = block * rows
        own[at : at + 3, :] = positions[:, part]
        own[at + 4 : at + 7, :] = velocities[:, part]
    own[pl.ds(3, 8, stride=rows), :] = smoothing[...]
    own[pl.ds(7, 8, stride=rows), :] = sound
    own[64:72, :] = mass[...]
    own[72:80, :] = energy[...]
    cut_windows(lambda r: offsets[0, r], lambda r: counts[0, r], own, outgoing, True)


def two_deep(prepare, finish, first=0, last=8):
    prepare(first, 0)

    def step(half, _):
        block = first + half * 2
        prepare(block + 1, 1)
        finish(block, 0)
        prepare(jnp.minimum(block + 2, last - 1), 0)
        finish(block + 1, 1)
        return 0

    lax.fori_loop(0, (last - first) // 2, step, 0, unroll=True)


def spline(ratio):
    wide = jnp.maximum(1.0 - ratio, 0.0)
    narrow = jnp.maximum(0.5 - ratio, 0.0)
    twice = narrow + narrow
    return wide * wide * wide - twice * twice * narrow


def pair_weight(dist, rate, mean_len, sounds):
    inv_len = 1.0 / mean_len
    ratio = dist * inv_len
    wide = jnp.maximum(20.0 - ratio, 0.0) * inv_len
    narrow = jnp.maximum(10.0 - ratio, 0.0) * inv_len
    twice = narrow + narrow
    weight = wide * wide * wide - twice * twice * narrow
    rate = jnp.minimum(rate, 0.0)
    return weight, weight * rate * (rate - sounds)


def own_kernel(
    pairs, own, left, columns, table, plan, self_kernel, self_signal, self_weight, self_damping
):
    table[...] = own[...]
    plan[...] = pairs[...]

    def step(block, _):
        tile = tile_at(own, block)
        centred = tile - centre_of(tile)
        stacked = jnp.concatenate([own_distance(centred), own_closing(centred, 30.0)], axis=0)
        at = pl.ds(pl.multiple_of(block * lanes, lanes), lanes)
        operand = stacked.T.astype(bf16)
        left[at, :] = operand
        turned = tile.T
        length = turned[:, 3:4]
        columns[at, 0:lanes] = jnp.broadcast_to(length * 0.05, (lanes, lanes))
        columns[at, lanes : 2 * lanes] = jnp.broadcast_to(turned[:, 7:8] * 0.75, (lanes, lanes))
        columns[at, 2 * lanes :] = jnp.broadcast_to(0.5 / length, (lanes, lanes))
        near = near_operand(centred)
        empty = jnp.zeros_like(near)
        near = jnp.concatenate(
            [jnp.concatenate([near, empty], axis=1), jnp.concatenate([empty, near], axis=1)], axis=0
        )
        both = jnp.dot(operand, near, preferred_element_type=f32)
        dist_sq = jnp.maximum(both[:, 0:lanes], tiny)
        dist = dist_sq * lax.rsqrt(dist_sq)
        mean_len = columns[at, 0:lanes] + tile[3:4] * 0.05
        rate = both[:, lanes:] * mean_len / (dist_sq + mean_len * mean_len)
        to = pl.multiple_of(block * 2 * lanes, lanes)
        high, low = split2(spline(dist * columns[at, 2 * lanes :]))
        self_kernel[pl.ds(to, lanes), :] = high
        self_kernel[pl.ds(to + lanes, lanes), :] = low
        self_signal[at, :] = tile[7:8] - rate
        weight, damping = pair_weight(
            dist, rate, mean_len, columns[at, lanes : 2 * lanes] + tile[7:8] * 0.75
        )
        self_damping[at, :] = damping
        high, low = split2(weight)
        self_weight[pl.ds(to, lanes), :] = high
        self_weight[pl.ds(to + lanes, lanes), :] = low
        return 0

    lax.fori_loop(0, 8, step, 0, unroll=True)


def put_near(near, k, tile):
    operand = near_operand(tile)
    at = 2 * k * lanes
    near[0:64, at : at + lanes] = operand
    near[64:128, at + lanes : at + 2 * lanes] = operand


def clear_near(buffers):
    empty = jnp.zeros((64, lanes), bf16)
    for near in buffers:
        for k in range(8):
            near[0:64, (2 * k + 1) * lanes : (2 * k + 2) * lanes] = empty
            near[64:128, 2 * k * lanes : (2 * k + 1) * lanes] = empty


def pair_dots(left, near, block, k):
    at = pl.ds(pl.multiple_of(block * lanes, lanes), lanes)
    part = slice(2 * k * lanes, 2 * (k + 1) * lanes)
    both = jnp.dot(left[at, :], near[:, part], preferred_element_type=f32)
    return both[:, 0:lanes], both[:, lanes:]


def signal_kernel(
    plan, left, columns, self_signal, own, m0, m1, m2, m3,
    allowed, smallest, distance, rates, table, *near
):
    clear_near(near)
    fill_table(own, (m0, m1, m2, m3), table, rows)

    def prepare(block, buf):
        centre = centre_of(tile_at(table, block))
        for k in range(1, 8):
            put_near(near[buf], k, tile_at(table, plan[k, block]) - centre)

    def finish(block, buf):
        at = pl.ds(pl.multiple_of(block * lanes, lanes), lanes)
        best = self_signal[at, :]
        sounds = tile_at(table, block)[7:8]
        for k in range(1, 8):
            tile = tile_at(table, plan[k, block])
            len_row, sound_row = tile[3:4] * 0.05, tile[7:8]
            sounds = jnp.maximum(sounds, sound_row)
            part = slice(k * lanes, (k + 1) * lanes)
            dist_sq, closing = pair_dots(left, near[buf], block, k)
            dist_sq = jnp.maximum(dist_sq, tiny)
            distance[at, part] = dist_sq * lax.rsqrt(dist_sq)
            mean_len = columns[at, 0:lanes] + len_row
            rate = closing * mean_len / (dist_sq + mean_len * mean_len)
            rates[at, part] = rate
            signal = sound_row - rate
            best = jnp.maximum(best, signal)
        top = jnp.max(best.T, axis=0, keepdims=True)
        top = jnp.maximum(top, jnp.max(sounds, axis=1, keepdims=True))
        own_tile = tile_at(table, block)
        allowed[pl.ds(block, 1), :] = courant * own_tile[3:4] / (own_tile[7:8] + top)

    two_deep(prepare, finish)
    least = jnp.min(allowed[...], axis=(0, 1), keepdims=True)
    smallest[...] = jnp.broadcast_to(least, (rows, lanes))


def density_kernel(
    plan, offsets, counts, columns, distance, self_kernel, own, m0, m1, m2, m3, second, *rest
):
    outgoing = rest[0:4]
    table, masses, sums, *scratch = rest[4:]
    feats, weights = scratch[0:2], scratch[2:4]
    fill_table(own, (m0, m1, m2, m3), table, rows)
    fill_mass(own, (m0, m1, m2, m3), masses)

    def prepare(block, buf):
        centre = centre_of(tile_at(table, block))
        ids = row_ids()
        for k in range(8):
            entry = plan[k, block]
            part = slice(k * lanes, (k + 1) * lanes)
            tile = tile_at(table, entry) - centre
            weighed = jnp.where(ids == 3, 1.0, tile) * masses[pl.ds(entry, 1), :]
            stacked = jnp.concatenate(
                [weighed, weighed * tile[0:1], weighed * tile[1:2], weighed * tile[2:3]], axis=0
            )
            high, low = split2(stacked)
            feats[buf][0:32, part] = high
            feats[buf][32:64, part] = low

    def finish(block, buf):
        both = pl.ds(pl.multiple_of(block * 2 * lanes, lanes), 2 * lanes)
        weights[buf][:, 0:lanes] = self_kernel[both, :]
        for start in range(0, lanes, 2 * chunk):
            at = pl.ds(pl.multiple_of(block * lanes + start, 2 * chunk), 2 * chunk)
            scale = columns[at, 2 * lanes :]
            for k in range(1, 8):
                part = slice(k * lanes, (k + 1) * lanes)
                high, low = split2(spline(distance[at, part] * scale))
                weights[buf][start : start + 2 * chunk, part] = high
                weights[buf][lanes + start : lanes + start + 2 * chunk, part] = low
        out = lax.dot_general(
            feats[buf][...], weights[buf][...], (((1,), (1,)), ((), ())), preferred_element_type=f32
        )
        out = out[0:32] + out[32:64]
        sums[pl.ds(block, 32, stride=8), :] = out[:, 0:lanes] + out[:, lanes:]

    two_deep(prepare, finish)

    def total(field):
        return sums[field * 8 : (field + 1) * 8, :]

    def mine(field):
        return own[pl.ds(field, 8, stride=rows), :]

    length = mine(3)
    place = [mine(a) for a in range(3)]
    place = [value - (jnp.floor(value[:, 0:1]) + 0.5) for value in place]
    whole = total(3)
    dens = whole * (2.0 / math.pi) / (length * length * length)
    first = [total(a) for a in range(3)]
    inverse = 1.0 / whole
    floor = 0.05 * length * length

    def moment(a, b):
        raw = total(8 + 8 * a + b) - place[a] * first[b] - place[b] * first[a]
        return (raw + place[a] * place[b] * whole) * inverse

    axx = moment(0, 0) + floor
    ayy = moment(1, 1) + floor
    azz = moment(2, 2) + floor
    axy, axz, ayz = moment(0, 1), moment(0, 2), moment(1, 2)
    cof_xx = ayy * azz - ayz * ayz
    cof_yy = axx * azz - axz * axz
    cof_zz = axx * ayy - axy * axy
    cof_xy = axz * ayz - axy * azz
    cof_xz = axy * ayz - ayy * axz
    cof_yz = axy * axz - axx * ayz
    inv_det = 1.0 / (axx * cof_xx + axy * cof_xy + axz * cof_xz)
    pressure = (gas_gamma - 1.0) * own[72:80, :] / dens
    fields = [dens, pressure, cof_xx * inv_det, cof_yy * inv_det, cof_zz * inv_det]
    fields += [cof_xy * inv_det, cof_xz * inv_det, cof_yz * inv_det]
    for field in range(8):
        second[pl.ds(field, 8, stride=rows), :] = fields[field]
    cut_windows(lambda r: offsets[0, r], lambda r: counts[0, r], second, outgoing, False)


def weight_kernel(
    first, plan, columns, distance, rates, self_weight, self_damping, second, own, m0, m1, m2, m3,
    weights, damping, dens_col, table
):
    fill_table(own, (m0, m1, m2, m3), table, rows)

    def step(place, _):
        block = first + place
        turned = jnp.broadcast_to(second[pl.ds(block * rows, 1), :], (lanes, lanes)).T
        dens_col[pl.ds(pl.multiple_of(place * lanes, lanes), lanes), :] = turned
        tiles = [tile_at(table, plan[k, block]) for k in range(8)]
        for start in range(0, lanes, narrow_rows):
            at = pl.ds(pl.multiple_of(block * lanes + start, narrow_rows), narrow_rows)
            to = pl.ds(pl.multiple_of(place * lanes + start, narrow_rows), narrow_rows)
            len_own = columns[at, 0:lanes]
            sound_own = columns[at, lanes : 2 * lanes]
            damping[to, 0:lanes] = self_damping[at, :]
            for k in range(1, 8):
                part = slice(k * lanes, (k + 1) * lanes)
                weight, damped = pair_weight(
                    distance[at, part],
                    rates[at, part],
                    len_own + tiles[k][3:4] * 0.05,
                    sound_own + tiles[k][7:8] * 0.75,
                )
                damping[to, part] = damped
                high, low = split2(weight)
                base = pl.multiple_of(place * 2 * lanes + start, narrow_rows)
                weights[pl.ds(base, narrow_rows), part] = high
                weights[pl.ds(base + lanes, narrow_rows), part] = low
        both = pl.ds(pl.multiple_of(place * 2 * lanes, lanes), 2 * lanes)
        weights[both, 0:lanes] = self_weight[both, :]
        return 0

    lax.fori_loop(0, 8, step, 0, unroll=2)


def momentum_kernel(
    plan, weights, damping, dens_col,
    own, m0, m1, m2, m3, second, s0, s1, s2, s3, accel, heating, density, *scratch
):
    table, masses, table2, sums, *scratch = scratch
    feats, damped = scratch[0:2], scratch[2:4]
    fill_table(own, (m0, m1, m2, m3), table, rows)
    fill_mass(own, (m0, m1, m2, m3), masses)
    fill_table(second, (s0, s1, s2, s3), table2, rows)
    ids = row_ids()
    picks = []
    for picked in ((2, 5, 6, 2), (5, 3, 7, 3), (6, 7, 4, 4)):
        places = jnp.full((rows, lanes), picked[3], jnp.int32)
        for at in range(3):
            places = jnp.where(lax.rem(ids, 4) == at, picked[at], places)
        picks.append(places)

    def features(tile, extra, mass):
        cols = [jnp.take_along_axis(extra, places, axis=0) for places in picks]
        heavy = tile * mass
        applied = None
        for axis in range(3):
            operand = jnp.where(ids < 4, tile[axis : axis + 1], tile[4 + axis : 5 + axis])
            term = cols[axis] * operand
            applied = term if applied is None else applied + term
        swirl = (
            applied[0:1] * tile[4:5] + applied[1:2] * tile[5:6] + applied[2:3] * tile[6:7]
        )
        applied = placed(applied, 3, swirl)
        press = extra[1:2] * mass
        parts = [jnp.where(ids == 3, mass, heavy)]
        parts += [heavy * tile[4 + axis : 5 + axis] for axis in range(3)]
        parts += [extra * mass, extra * press, applied * mass, applied * press]
        return jnp.concatenate(parts, axis=0)

    def prepare(block, buf):
        centre = centre_of(tile_at(table, block))
        for k in range(8):
            entry = plan[k, block]
            part = slice(k * lanes, (k + 1) * lanes)
            tile = tile_at(table, entry) - centre
            high, low = split2(
                features(tile, tile_at(table2, entry), masses[pl.ds(entry, 1), :])
            )
            feats[buf][0:64, part] = high
            feats[buf][64:128, part] = low

    def finish_part(weights, damping, dens_col, first, block, buf):
        place = block - first
        for start in range(0, lanes, chunk):
            at = pl.ds(pl.multiple_of(place * lanes + start, chunk), chunk)
            for k in range(8):
                dens_row = tile_at(table2, plan[k, block])[0:1]
                part = slice(k * lanes, (k + 1) * lanes)
                high, low = split2(damping[at, part] / (dens_col[at, :] + dens_row))
                damped[buf][start : start + chunk, part] = high
                damped[buf][lanes + start : lanes + start + chunk, part] = low
        own_weights = weights[pl.ds(pl.multiple_of(place * 2 * lanes, lanes), 2 * lanes), :]
        for base, value in ((0, own_weights), (64, damped[buf][...])):
            out = lax.dot_general(
                feats[buf][...], value, (((1,), (1,)), ((), ())), preferred_element_type=f32
            )
            out = out[0:64] + out[64:128]
            sums[pl.ds(base * 8 + block, 64, stride=8), :] = out[:, 0:lanes] + out[:, lanes:]

    two_deep(prepare, functools.partial(finish_part, weights, damping, dens_col, 0))

    def mine(ref, field):
        return ref[pl.ds(field, 8, stride=rows), :]

    place = [mine(own, a) for a in range(3)]
    place = [value - (jnp.floor(value[:, 0:1]) + 0.5) for value in place]
    speed = [mine(own, 4 + a) for a in range(3)]
    density[...] = mine(second, 0)
    pressure = mine(second, 1)
    order = ((2, 5, 6), (5, 3, 7), (6, 7, 4))
    matrix = [[mine(second, order[a][b]) for b in range(3)] for a in range(3)]

    def pieces(base):
        def total(field):
            return sums[(base + field) * 8 : (base + field + 1) * 8, :]

        mass = total(3)
        offset = [total(a) - place[a] * mass for a in range(3)]
        mass_v = [total(4 + a) for a in range(3)]
        applied = [
            matrix[a][0] * offset[0] + matrix[a][1] * offset[1] + matrix[a][2] * offset[2]
            for a in range(3)
        ]
        work = None
        for a in range(3):
            for b in range(3):
                cross = speed[a] * offset[b] - total(8 + 8 * a + b) + mass_v[a] * place[b]
                term = matrix[a][b] * cross
                work = term if work is None else work + term
        return total, applied, work

    def near_force(total, matrices, vectors):
        return [
            total(vectors + a)
            - total(matrices + order[a][0]) * place[0]
            - total(matrices + order[a][1]) * place[1]
            - total(matrices + order[a][2]) * place[2]
            for a in range(3)
        ]

    norm = 16.0 / math.pi / 20.0**6
    total, applied, work = pieces(0)
    pushed = near_force(total, 40, 56)
    total2, applied2, work2 = pieces(64)
    pushed2 = near_force(total2, 32, 48)
    for a in range(3):
        value = -norm * (
            pressure * applied[a] + pushed[a] + (2.0 / 9.0) * (applied2[a] + pushed2[a])
        )
        for block in range(8):
            part = slice(block * lanes, (block + 1) * lanes)
            accel[a : a + 1, part] = value[block : block + 1, :]
    near_work = (
        speed[0] * pushed2[0]
        + speed[1] * pushed2[1]
        + speed[2] * pushed2[2]
        - total2(51)
        + place[0] * total2(52)
        + place[1] * total2(53)
        + place[2] * total2(54)
    )
    heating[...] = norm * (pressure * work + (1.0 / 9.0) * (work2 + near_work))


def call(kernel, outs, scratch, smem, args, flops, limit):
    return pl.pallas_call(
        kernel,
        out_shape=[jax.ShapeDtypeStruct(shape, kind) for shape, kind in outs],
        in_specs=[smem_spec] * smem + [vmem_spec] * (len(args) - smem),
        out_specs=[vmem_spec] * len(outs),
        scratch_shapes=[pltpu.VMEM(shape, kind) for shape, kind in scratch],
        compiler_params=pltpu.CompilerParams(vmem_limit_bytes=limit * 1024 * 1024),
        cost_estimate=pl.CostEstimate(flops=flops, bytes_accessed=200000, transcendentals=0),
    )(*args)


def fold(value, axis, step):
    size = lax.axis_size(axis)
    return jnp.minimum(value, lax.ppermute(value, axis, [(i, i ^ step) for i in range(size)]))


def body(positions, velocities, mass, smoothing, energy, send_offsets, send_counts, pair_blocks):
    points = positions.shape[1]
    send_offsets, send_counts = send_offsets.reshape(1, 4), send_counts.reshape(1, 4)
    tile = ((rows, lanes), f32)
    packed = ((72, lanes), f32)
    own, *outgoing = pl.pallas_call(
        pack_kernel,
        out_shape=[jax.ShapeDtypeStruct((80, lanes), f32)] + [jax.ShapeDtypeStruct(*packed)] * 4,
        in_specs=[vmem_spec] * 5 + [smem_spec] * 2,
        out_specs=[vmem_spec] * 5,
    )(
        positions,
        velocities,
        mass.reshape(8, lanes),
        smoothing.reshape(8, lanes),
        energy.reshape(8, lanes),
        send_offsets,
        send_counts,
    )
    received = [swap(value, axis, odd) for value, (axis, odd, _) in zip(outgoing, swaps)]
    last = (1, 2, 3)
    steps = [("dom", 1 << bit) for bit in range(2, lax.axis_size("dom").bit_length() - 1)]
    steps += [("slab", 1 << bit) for bit in reversed(range(lax.axis_size("slab").bit_length() - 1))]
    left, columns, own, plan, self_kernel, self_signal, self_weight, self_damping = pl.pallas_call(
        own_kernel,
        out_shape=[
            jax.ShapeDtypeStruct((8 * lanes, lanes), bf16),
            jax.ShapeDtypeStruct((8 * lanes, 3 * lanes), f32),
            jax.ShapeDtypeStruct((80, lanes), f32),
            jax.ShapeDtypeStruct(pair_blocks.shape, jnp.int32),
            jax.ShapeDtypeStruct((16 * lanes, lanes), bf16),
            jax.ShapeDtypeStruct((8 * lanes, lanes), f32),
            jax.ShapeDtypeStruct((16 * lanes, lanes), bf16),
            jax.ShapeDtypeStruct((8 * lanes, lanes), f32),
        ],
        in_specs=[vmem_spec] * 2,
        out_specs=[vmem_spec] * 8,
        compiler_params=pltpu.CompilerParams(vmem_limit_bytes=8 * 1024 * 1024),
    )(pair_blocks, own)
    table = ((328, lanes), f32)
    masses = ((48, lanes), f32)
    near = ((lanes, 16 * lanes), bf16)
    feats = ((64, 8 * lanes), bf16)
    halves = ((2 * lanes, 8 * lanes), bf16)
    square = ((8 * lanes, 8 * lanes), f32)
    allowed, smallest, distance, rates = call(
        signal_kernel,
        [tile, tile, square, square],
        [table, near, near],
        1,
        (plan, left, columns, self_signal, own, *received),
        3 * 10**9,
        20,
    )
    smallest = fold(smallest, *steps[0])
    second, *outgoing2 = call(
        density_kernel,
        [packed] + [((64, lanes), f32)] * 4,
        [table, masses, ((9 * 32, lanes), f32)] + [feats] * 2 + [halves] * 2,
        3,
        (plan, send_offsets, send_counts, columns, distance, self_kernel, own, *received),
        5 * 10**9,
        20,
    )
    smallest, outgoing2 = lax.optimization_barrier((smallest, outgoing2))
    received2 = [swap(value, axis, odd) for value, (axis, odd, _) in zip(outgoing2, swaps)]
    parts = []
    smallest = fold(smallest, *steps[1])
    for first in (0,):
        smallest = fold(smallest, *steps[2])
        weights, damping, dens_col = call(
            functools.partial(weight_kernel, first),
            [((16 * lanes, 8 * lanes), bf16), ((8 * lanes, 8 * lanes), f32), ((8 * lanes, lanes), f32)],
            [table],
            1,
            (plan, columns, distance, rates, self_weight, self_damping, second, own, *received),
            10**9,
            20,
        )
        smallest, distance, weights = lax.optimization_barrier((smallest, distance, weights))
        parts += [weights, damping, dens_col]
    for step in steps[3:]:
        smallest = fold(smallest, *step)
    smallest, received2 = lax.optimization_barrier((smallest, received2))
    accel, heating, density = call(
        momentum_kernel,
        [((3, points), f32), tile, tile],
        [table, masses, table, ((9 * lanes, lanes), f32)]
        + [((lanes, 8 * lanes), bf16)] * 2
        + [halves] * 2,
        1,
        (plan, *parts, own, *received, second, *received2),
        5 * 10**9,
        20,
    )
    size = lax.axis_size("dom")
    moved = [
        lax.ppermute(smallest, "dom", [(i, i ^ step) for i in range(size)]) for step in last
    ]
    for value in moved:
        smallest = jnp.minimum(smallest, value)
    share = smallest / allowed
    return (density.reshape(points), accel, heating.reshape(points), share.reshape(points))


def solution(mesh):
    both = ("slab", "dom")
    wide, flat = P(None, both), P(both)
    in_specs = (wide, wide, flat, flat, flat, wide, wide, wide)
    out_specs = (flat, wide, flat, flat)
    return jax.shard_map(body, mesh=mesh, in_specs=in_specs, out_specs=out_specs, check_vma=False)
```

```python
import functools
import math

import jax
import jax.numpy as jnp
from jax import lax
from jax.experimental import pallas as pl
from jax.experimental.pallas import tpu as pltpu
from jax.sharding import PartitionSpec as P

gas_gamma = 5.0 / 3.0
courant = 0.4
f32 = jnp.float32
bf16 = jnp.bfloat16
rows = 8
lanes = 128
tiny = 1e-12
chunk = 32
narrow_rows = 16
swaps = (("dom", 0, 2), ("slab", 0, 0), ("dom", 1, 2), ("slab", 1, 0))
vmem_spec = pl.BlockSpec(memory_space=pltpu.VMEM)
smem_spec = pl.BlockSpec(memory_space=pltpu.SMEM)


def partner(axis, odd, base):
    place = lax.axis_index(axis)
    size = lax.axis_size(axis)
    upward = lax.rem(place + odd, 2) == 0
    direction = base + jnp.where(upward, 1, 0)
    exists = jnp.where(upward, place < size - 1, place > 0)
    return direction, exists


def swap(value, axis, odd):
    size = lax.axis_size(axis)
    pairs = [
        (i, (i + 1) % size if (i - odd) % 2 == 0 else (i - 1) % size) for i in range(size)
    ]
    return lax.ppermute(value, axis, pairs)


def split2(value):
    high = value.astype(bf16)
    low = (value - high.astype(f32)).astype(bf16)
    return high, low


def split3(value):
    first = value.astype(bf16).astype(f32)
    rest = value - first
    second = rest.astype(bf16).astype(f32)
    return first, second, rest - second


def row_ids():
    return lax.broadcasted_iota(jnp.int32, (rows, lanes), 0)


def centre_of(tile):
    corner = jnp.floor(tile[:, 0:1]) + 0.5
    return jnp.where(row_ids() < 3, jnp.broadcast_to(corner, tile.shape), 0.0)


def sum_xyz(tile, start):
    return tile[start : start + 1] + tile[start + 1 : start + 2] + tile[start + 2 : start + 3]


def placed(tile, at, row):
    return jnp.where(row_ids() == at, jnp.broadcast_to(row, tile.shape), tile)


def near_operand(tile):
    norm = sum_xyz(tile * tile, 0)
    drift = (
        tile[0:1] * tile[4:5] + tile[1:2] * tile[5:6] + tile[2:3] * tile[6:7]
    )
    first, second, third = split3(placed(placed(tile, 3, norm), 7, drift))
    ones = jnp.where(row_ids() < 3, 1.0, 0.0)
    stacked = [first, second, third, first, second, first, ones, jnp.zeros_like(ones)]
    return jnp.concatenate(stacked, axis=0).astype(bf16)


def own_operand(tile, own_term):
    first, second, third = split3(tile)
    parts = split3(own_term)
    ones = jnp.zeros((rows, lanes), f32)
    for at in range(3):
        ones = placed(ones, at, parts[at])
    stacked = [first, first, first, second, second, third, ones, jnp.zeros_like(ones)]
    return jnp.concatenate(stacked, axis=0)


def own_distance(tile):
    norm = sum_xyz(tile * tile, 0)
    ids = row_ids()
    left = jnp.where(ids < 3, -2.0 * tile, jnp.where(ids == 3, 1.0, 0.0))
    return own_operand(left, norm)


def own_closing(tile, scale):
    drift = (
        tile[0:1] * tile[4:5] + tile[1:2] * tile[5:6] + tile[2:3] * tile[6:7]
    )
    ids = row_ids()
    left = jnp.concatenate([-tile[4:8], -tile[0:4]], axis=0)
    left = jnp.where(ids == 3, 0.0, jnp.where(ids == 7, 1.0, left))
    return own_operand(left * scale, drift * scale)


def fill_table(own, received, table, width):
    table[0 : 8 * width, :] = own[0 : 8 * width, :]
    for message, (axis, odd, base) in zip(received, swaps):
        direction, _ = partner(axis, odd, base)
        start = pl.multiple_of((direction + 1) * (8 * width), 8 * width)
        table[pl.ds(start, 8 * width), :] = message[0 : 8 * width, :]
    table[40 * width : 40 * width + 8, :] = jnp.zeros((8, lanes), f32)


def fill_mass(own, received, masses):
    masses[0:8, :] = own[64:72, :]
    for message, (axis, odd, base) in zip(received, swaps):
        direction, _ = partner(axis, odd, base)
        start = pl.multiple_of((direction + 1) * 8, 8)
        masses[pl.ds(start, 8), :] = message[64:72, :]
    masses[40:48, :] = jnp.zeros((8, lanes), f32)


def tile_at(table, entry):
    return table[pl.ds(pl.multiple_of(entry * rows, rows), rows), :]


def cut_windows(offset_of, count_of, source, outgoing, masses):
    for target, (axis, odd, base) in zip(outgoing, swaps):
        direction, exists = partner(axis, odd, base)
        offset = offset_of(direction)
        count = jnp.where(exists, count_of(direction), 0)
        for slot in range(8):
            block = jnp.minimum(offset + slot, 7)
            keep = slot < count
            tile = tile_at(source, block)
            target[slot * rows : (slot + 1) * rows, :] = jnp.where(keep, tile, 0.0)
            if masses:
                row = source[pl.ds(64 + block, 1), :]
                target[64 + slot : 65 + slot, :] = jnp.where(keep, row, 0.0)


def pack_kernel(positions, velocities, mass, smoothing, energy, offsets, counts, own, *outgoing):
    sound = jnp.sqrt(gas_gamma * (gas_gamma - 1.0) * energy[...])
    for block in range(8):
        part = slice(block * lanes, (block + 1) * lanes)
        at = block * rows
        own[at : at + 3, :] = positions[:, part]
        own[at + 4 : at + 7, :] = velocities[:, part]
    own[pl.ds(3, 8, stride=rows), :] = smoothing[...]
    own[pl.ds(7, 8, stride=rows), :] = sound
    own[64:72, :] = mass[...]
    own[72:80, :] = energy[...]
    cut_windows(lambda r: offsets[0, r], lambda r: counts[0, r], own, outgoing, True)


def two_deep(prepare, finish, first=0, last=8):
    prepare(first, 0)

    def step(half, _):
        block = first + half * 2
        prepare(block + 1, 1)
        finish(block, 0)
        prepare(jnp.minimum(block + 2, last - 1), 0)
        finish(block + 1, 1)
        return 0

    lax.fori_loop(0, (last - first) // 2, step, 0, unroll=True)


def spline(ratio):
    wide = jnp.maximum(1.0 - ratio, 0.0)
    narrow = jnp.maximum(0.5 - ratio, 0.0)
    twice = narrow + narrow
    return wide * wide * wide - twice * twice * narrow


def pair_weight(dist, rate, mean_len, sounds):
    inv_len = 1.0 / mean_len
    ratio = dist * inv_len
    wide = jnp.maximum(20.0 - ratio, 0.0) * inv_len
    narrow = jnp.maximum(10.0 - ratio, 0.0) * inv_len
    twice = narrow + narrow
    weight = wide * wide * wide - twice * twice * narrow
    rate = jnp.minimum(rate, 0.0)
    return weight, weight * rate * (rate - sounds)


def own_kernel(
    pairs, own, left, columns, table, plan, self_kernel, self_signal, self_weight, self_damping
):
    table[...] = own[...]
    plan[...] = pairs[...]

    def step(block, _):
        tile = tile_at(own, block)
        centred = tile - centre_of(tile)
        stacked = jnp.concatenate([own_distance(centred), own_closing(centred, 30.0)], axis=0)
        at = pl.ds(pl.multiple_of(block * lanes, lanes), lanes)
        operand = stacked.T.astype(bf16)
        left[at, :] = operand
        turned = tile.T
        length = turned[:, 3:4]
        columns[at, 0:lanes] = jnp.broadcast_to(length * 0.05, (lanes, lanes))
        columns[at, lanes : 2 * lanes] = jnp.broadcast_to(turned[:, 7:8] * 0.75, (lanes, lanes))
        columns[at, 2 * lanes :] = jnp.broadcast_to(0.5 / length, (lanes, lanes))
        near = near_operand(centred)
        empty = jnp.zeros_like(near)
        near = jnp.concatenate(
            [jnp.concatenate([near, empty], axis=1), jnp.concatenate([empty, near], axis=1)], axis=0
        )
        both = jnp.dot(operand, near, preferred_element_type=f32)
        dist_sq = jnp.maximum(both[:, 0:lanes], tiny)
        dist = dist_sq * lax.rsqrt(dist_sq)
        mean_len = columns[at, 0:lanes] + tile[3:4] * 0.05
        rate = both[:, lanes:] * mean_len / (dist_sq + mean_len * mean_len)
        to = pl.multiple_of(block * 2 * lanes, lanes)
        high, low = split2(spline(dist * columns[at, 2 * lanes :]))
        self_kernel[pl.ds(to, lanes), :] = high
        self_kernel[pl.ds(to + lanes, lanes), :] = low
        self_signal[at, :] = tile[7:8] - rate
        weight, damping = pair_weight(
            dist, rate, mean_len, columns[at, lanes : 2 * lanes] + tile[7:8] * 0.75
        )
        self_damping[at, :] = damping
        high, low = split2(weight)
        self_weight[pl.ds(to, lanes), :] = high
        self_weight[pl.ds(to + lanes, lanes), :] = low
        return 0

    lax.fori_loop(0, 8, step, 0, unroll=True)


def put_near(near, k, tile):
    operand = near_operand(tile)
    at = 2 * k * lanes
    near[0:64, at : at + lanes] = operand
    near[64:128, at + lanes : at + 2 * lanes] = operand


def clear_near(buffers):
    empty = jnp.zeros((64, lanes), bf16)
    for near in buffers:
        for k in range(8):
            near[0:64, (2 * k + 1) * lanes : (2 * k + 2) * lanes] = empty
            near[64:128, 2 * k * lanes : (2 * k + 1) * lanes] = empty


def pair_dots(left, near, block, k):
    at = pl.ds(pl.multiple_of(block * lanes, lanes), lanes)
    part = slice(2 * k * lanes, 2 * (k + 1) * lanes)
    both = jnp.dot(left[at, :], near[:, part], preferred_element_type=f32)
    return both[:, 0:lanes], both[:, lanes:]


def signal_kernel(
    plan, left, columns, self_signal, own, m0, m1, m2, m3,
    allowed, smallest, distance, rates, table, *near
):
    clear_near(near)
    fill_table(own, (m0, m1, m2, m3), table, rows)

    def prepare(block, buf):
        centre = centre_of(tile_at(table, block))
        for k in range(1, 8):
            put_near(near[buf], k, tile_at(table, plan[k, block]) - centre)

    def finish(block, buf):
        at = pl.ds(pl.multiple_of(block * lanes, lanes), lanes)
        best = self_signal[at, :]
        sounds = tile_at(table, block)[7:8]
        for k in range(1, 8):
            tile = tile_at(table, plan[k, block])
            len_row, sound_row = tile[3:4] * 0.05, tile[7:8]
            sounds = jnp.maximum(sounds, sound_row)
            part = slice(k * lanes, (k + 1) * lanes)
            dist_sq, closing = pair_dots(left, near[buf], block, k)
            dist_sq = jnp.maximum(dist_sq, tiny)
            distance[at, part] = dist_sq * lax.rsqrt(dist_sq)
            mean_len = columns[at, 0:lanes] + len_row
            rate = closing * mean_len / (dist_sq + mean_len * mean_len)
            rates[at, part] = rate
            signal = sound_row - rate
            best = jnp.maximum(best, signal)
        top = jnp.max(best.T, axis=0, keepdims=True)
        top = jnp.maximum(top, jnp.max(sounds, axis=1, keepdims=True))
        own_tile = tile_at(table, block)
        allowed[pl.ds(block, 1), :] = courant * own_tile[3:4] / (own_tile[7:8] + top)

    two_deep(prepare, finish)
    least = jnp.min(allowed[...], axis=(0, 1), keepdims=True)
    smallest[...] = jnp.broadcast_to(least, (rows, lanes))


def density_kernel(
    plan, offsets, counts, columns, distance, self_kernel, own, m0, m1, m2, m3, second, *rest
):
    outgoing = rest[0:4]
    table, masses, sums, *scratch = rest[4:]
    feats, weights = scratch[0:2], scratch[2:4]
    fill_table(own, (m0, m1, m2, m3), table, rows)
    fill_mass(own, (m0, m1, m2, m3), masses)

    def prepare(block, buf):
        centre = centre_of(tile_at(table, block))
        ids = row_ids()
        for k in range(8):
            entry = plan[k, block]
            part = slice(k * lanes, (k + 1) * lanes)
            tile = tile_at(table, entry) - centre
            weighed = jnp.where(ids == 3, 1.0, tile) * masses[pl.ds(entry, 1), :]
            stacked = jnp.concatenate(
                [weighed, weighed * tile[0:1], weighed * tile[1:2], weighed * tile[2:3]], axis=0
            )
            high, low = split2(stacked)
            feats[buf][0:32, part] = high
            feats[buf][32:64, part] = low

    def finish(block, buf):
        both = pl.ds(pl.multiple_of(block * 2 * lanes, lanes), 2 * lanes)
        weights[buf][:, 0:lanes] = self_kernel[both, :]
        for start in range(0, lanes, 2 * chunk):
            at = pl.ds(pl.multiple_of(block * lanes + start, 2 * chunk), 2 * chunk)
            scale = columns[at, 2 * lanes :]
            for k in range(1, 8):
                part = slice(k * lanes, (k + 1) * lanes)
                high, low = split2(spline(distance[at, part] * scale))
                weights[buf][start : start + 2 * chunk, part] = high
                weights[buf][lanes + start : lanes + start + 2 * chunk, part] = low
        out = lax.dot_general(
            feats[buf][...], weights[buf][...], (((1,), (1,)), ((), ())), preferred_element_type=f32
        )
        out = out[0:32] + out[32:64]
        sums[pl.ds(block, 32, stride=8), :] = out[:, 0:lanes] + out[:, lanes:]

    two_deep(prepare, finish)

    def total(field):
        return sums[field * 8 : (field + 1) * 8, :]

    def mine(field):
        return own[pl.ds(field, 8, stride=rows), :]

    length = mine(3)
    place = [mine(a) for a in range(3)]
    place = [value - (jnp.floor(value[:, 0:1]) + 0.5) for value in place]
    whole = total(3)
    dens = whole * (2.0 / math.pi) / (length * length * length)
    first = [total(a) for a in range(3)]
    inverse = 1.0 / whole
    floor = 0.05 * length * length

    def moment(a, b):
        raw = total(8 + 8 * a + b) - place[a] * first[b] - place[b] * first[a]
        return (raw + place[a] * place[b] * whole) * inverse

    axx = moment(0, 0) + floor
    ayy = moment(1, 1) + floor
    azz = moment(2, 2) + floor
    axy, axz, ayz = moment(0, 1), moment(0, 2), moment(1, 2)
    cof_xx = ayy * azz - ayz * ayz
    cof_yy = axx * azz - axz * axz
    cof_zz = axx * ayy - axy * axy
    cof_xy = axz * ayz - axy * azz
    cof_xz = axy * ayz - ayy * axz
    cof_yz = axy * axz - axx * ayz
    inv_det = 1.0 / (axx * cof_xx + axy * cof_xy + axz * cof_xz)
    pressure = (gas_gamma - 1.0) * own[72:80, :] / dens
    fields = [dens, pressure, cof_xx * inv_det, cof_yy * inv_det, cof_zz * inv_det]
    fields += [cof_xy * inv_det, cof_xz * inv_det, cof_yz * inv_det]
    for field in range(8):
        second[pl.ds(field, 8, stride=rows), :] = fields[field]
    cut_windows(lambda r: offsets[0, r], lambda r: counts[0, r], second, outgoing, False)


def weight_kernel(
    first, plan, columns, distance, rates, self_weight, self_damping, second, own, m0, m1, m2, m3,
    weights, damping, dens_col, table
):
    fill_table(own, (m0, m1, m2, m3), table, rows)

    def step(place, _):
        block = first + place
        turned = jnp.broadcast_to(second[pl.ds(block * rows, 1), :], (lanes, lanes)).T
        dens_col[pl.ds(pl.multiple_of(place * lanes, lanes), lanes), :] = turned
        tiles = [tile_at(table, plan[k, block]) for k in range(8)]
        for start in range(0, lanes, narrow_rows):
            at = pl.ds(pl.multiple_of(block * lanes + start, narrow_rows), narrow_rows)
            to = pl.ds(pl.multiple_of(place * lanes + start, narrow_rows), narrow_rows)
            len_own = columns[at, 0:lanes]
            sound_own = columns[at, lanes : 2 * lanes]
            damping[to, 0:lanes] = self_damping[at, :]
            for k in range(1, 8):
                part = slice(k * lanes, (k + 1) * lanes)
                weight, damped = pair_weight(
                    distance[at, part],
                    rates[at, part],
                    len_own + tiles[k][3:4] * 0.05,
                    sound_own + tiles[k][7:8] * 0.75,
                )
                damping[to, part] = damped
                high, low = split2(weight)
                base = pl.multiple_of(place * 2 * lanes + start, narrow_rows)
                weights[pl.ds(base, narrow_rows), part] = high
                weights[pl.ds(base + lanes, narrow_rows), part] = low
        both = pl.ds(pl.multiple_of(place * 2 * lanes, lanes), 2 * lanes)
        weights[both, 0:lanes] = self_weight[both, :]
        return 0

    lax.fori_loop(0, 8, step, 0, unroll=2)


def momentum_kernel(
    plan, weights, damping, dens_col,
    own, m0, m1, m2, m3, second, s0, s1, s2, s3, accel, heating, density, *scratch
):
    table, masses, table2, sums, *scratch = scratch
    feats, damped = scratch[0:2], scratch[2:4]
    fill_table(own, (m0, m1, m2, m3), table, rows)
    fill_mass(own, (m0, m1, m2, m3), masses)
    fill_table(second, (s0, s1, s2, s3), table2, rows)
    ids = row_ids()
    picks = []
    for picked in ((2, 5, 6, 2), (5, 3, 7, 3), (6, 7, 4, 4)):
        places = jnp.full((rows, lanes), picked[3], jnp.int32)
        for at in range(3):
            places = jnp.where(lax.rem(ids, 4) == at, picked[at], places)
        picks.append(places)

    def features(tile, extra, mass):
        cols = [jnp.take_along_axis(extra, places, axis=0) for places in picks]
        heavy = tile * mass
        applied = None
        for axis in range(3):
            operand = jnp.where(ids < 4, tile[axis : axis + 1], tile[4 + axis : 5 + axis])
            term = cols[axis] * operand
            applied = term if applied is None else applied + term
        swirl = (
            applied[0:1] * tile[4:5] + applied[1:2] * tile[5:6] + applied[2:3] * tile[6:7]
        )
        applied = placed(applied, 3, swirl)
        press = extra[1:2] * mass
        parts = [jnp.where(ids == 3, mass, heavy)]
        parts += [heavy * tile[4 + axis : 5 + axis] for axis in range(3)]
        parts += [extra * mass, extra * press, applied * mass, applied * press]
        return jnp.concatenate(parts, axis=0)

    def prepare(block, buf):
        centre = centre_of(tile_at(table, block))
        for k in range(8):
            entry = plan[k, block]
            part = slice(k * lanes, (k + 1) * lanes)
            tile = tile_at(table, entry) - centre
            high, low = split2(
                features(tile, tile_at(table2, entry), masses[pl.ds(entry, 1), :])
            )
            feats[buf][0:64, part] = high
            feats[buf][64:128, part] = low

    def finish_part(weights, damping, dens_col, first, block, buf):
        place = block - first
        for start in range(0, lanes, chunk):
            at = pl.ds(pl.multiple_of(place * lanes + start, chunk), chunk)
            for k in range(8):
                dens_row = tile_at(table2, plan[k, block])[0:1]
                part = slice(k * lanes, (k + 1) * lanes)
                high, low = split2(damping[at, part] / (dens_col[at, :] + dens_row))
                damped[buf][start : start + chunk, part] = high
                damped[buf][lanes + start : lanes + start + chunk, part] = low
        own_weights = weights[pl.ds(pl.multiple_of(place * 2 * lanes, lanes), 2 * lanes), :]
        for base, value in ((0, own_weights), (64, damped[buf][...])):
            out = lax.dot_general(
                feats[buf][...], value, (((1,), (1,)), ((), ())), preferred_element_type=f32
            )
            out = out[0:64] + out[64:128]
            sums[pl.ds(base * 8 + block, 64, stride=8), :] = out[:, 0:lanes] + out[:, lanes:]

    two_deep(prepare, functools.partial(finish_part, weights, damping, dens_col, 0))

    def mine(ref, field):
        return ref[pl.ds(field, 8, stride=rows), :]

    place = [mine(own, a) for a in range(3)]
    place = [value - (jnp.floor(value[:, 0:1]) + 0.5) for value in place]
    speed = [mine(own, 4 + a) for a in range(3)]
    density[...] = mine(second, 0)
    pressure = mine(second, 1)
    order = ((2, 5, 6), (5, 3, 7), (6, 7, 4))
    matrix = [[mine(second, order[a][b]) for b in range(3)] for a in range(3)]

    def pieces(base):
        def total(field):
            return sums[(base + field) * 8 : (base + field + 1) * 8, :]

        mass = total(3)
        offset = [total(a) - place[a] * mass for a in range(3)]
        mass_v = [total(4 + a) for a in range(3)]
        applied = [
            matrix[a][0] * offset[0] + matrix[a][1] * offset[1] + matrix[a][2] * offset[2]
            for a in range(3)
        ]
        work = None
        for a in range(3):
            for b in range(3):
                cross = speed[a] * offset[b] - total(8 + 8 * a + b) + mass_v[a] * place[b]
                term = matrix[a][b] * cross
                work = term if work is None else work + term
        return total, applied, work

    def near_force(total, matrices, vectors):
        return [
            total(vectors + a)
            - total(matrices + order[a][0]) * place[0]
            - total(matrices + order[a][1]) * place[1]
            - total(matrices + order[a][2]) * place[2]
            for a in range(3)
        ]

    norm = 16.0 / math.pi / 20.0**6
    total, applied, work = pieces(0)
    pushed = near_force(total, 40, 56)
    total2, applied2, work2 = pieces(64)
    pushed2 = near_force(total2, 32, 48)
    for a in range(3):
        value = -norm * (
            pressure * applied[a] + pushed[a] + (2.0 / 9.0) * (applied2[a] + pushed2[a])
        )
        for block in range(8):
            part = slice(block * lanes, (block + 1) * lanes)
            accel[a : a + 1, part] = value[block : block + 1, :]
    near_work = (
        speed[0] * pushed2[0]
        + speed[1] * pushed2[1]
        + speed[2] * pushed2[2]
        - total2(51)
        + place[0] * total2(52)
        + place[1] * total2(53)
        + place[2] * total2(54)
    )
    heating[...] = norm * (pressure * work + (1.0 / 9.0) * (work2 + near_work))


def call(kernel, outs, scratch, smem, args, flops, limit):
    return pl.pallas_call(
        kernel,
        out_shape=[jax.ShapeDtypeStruct(shape, kind) for shape, kind in outs],
        in_specs=[smem_spec] * smem + [vmem_spec] * (len(args) - smem),
        out_specs=[vmem_spec] * len(outs),
        scratch_shapes=[pltpu.VMEM(shape, kind) for shape, kind in scratch],
        compiler_params=pltpu.CompilerParams(vmem_limit_bytes=limit * 1024 * 1024),
        cost_estimate=pl.CostEstimate(flops=flops, bytes_accessed=200000, transcendentals=0),
    )(*args)


def fold(value, axis, step):
    size = lax.axis_size(axis)
    return jnp.minimum(value, lax.ppermute(value, axis, [(i, i ^ step) for i in range(size)]))


def body(positions, velocities, mass, smoothing, energy, send_offsets, send_counts, pair_blocks):
    points = positions.shape[1]
    send_offsets, send_counts = send_offsets.reshape(1, 4), send_counts.reshape(1, 4)
    tile = ((rows, lanes), f32)
    packed = ((72, lanes), f32)
    own, *outgoing = pl.pallas_call(
        pack_kernel,
        out_shape=[jax.ShapeDtypeStruct((80, lanes), f32)] + [jax.ShapeDtypeStruct(*packed)] * 4,
        in_specs=[vmem_spec] * 5 + [smem_spec] * 2,
        out_specs=[vmem_spec] * 5,
    )(
        positions,
        velocities,
        mass.reshape(8, lanes),
        smoothing.reshape(8, lanes),
        energy.reshape(8, lanes),
        send_offsets,
        send_counts,
    )
    received = [swap(value, axis, odd) for value, (axis, odd, _) in zip(outgoing, swaps)]
    last = (2, 3, 1)
    steps = [("dom", 1 << bit) for bit in range(2, lax.axis_size("dom").bit_length() - 1)]
    steps += [("slab", 1 << bit) for bit in reversed(range(lax.axis_size("slab").bit_length() - 1))]
    left, columns, own, plan, self_kernel, self_signal, self_weight, self_damping = pl.pallas_call(
        own_kernel,
        out_shape=[
            jax.ShapeDtypeStruct((8 * lanes, lanes), bf16),
            jax.ShapeDtypeStruct((8 * lanes, 3 * lanes), f32),
            jax.ShapeDtypeStruct((80, lanes), f32),
            jax.ShapeDtypeStruct(pair_blocks.shape, jnp.int32),
            jax.ShapeDtypeStruct((16 * lanes, lanes), bf16),
            jax.ShapeDtypeStruct((8 * lanes, lanes), f32),
            jax.ShapeDtypeStruct((16 * lanes, lanes), bf16),
            jax.ShapeDtypeStruct((8 * lanes, lanes), f32),
        ],
        in_specs=[vmem_spec] * 2,
        out_specs=[vmem_spec] * 8,
        compiler_params=pltpu.CompilerParams(vmem_limit_bytes=8 * 1024 * 1024),
    )(pair_blocks, own)
    table = ((328, lanes), f32)
    masses = ((48, lanes), f32)
    near = ((lanes, 16 * lanes), bf16)
    feats = ((64, 8 * lanes), bf16)
    halves = ((2 * lanes, 8 * lanes), bf16)
    square = ((8 * lanes, 8 * lanes), f32)
    allowed, smallest, distance, rates = call(
        signal_kernel,
        [tile, tile, square, square],
        [table, near, near],
        1,
        (plan, left, columns, self_signal, own, *received),
        3 * 10**9,
        20,
    )
    smallest = fold(smallest, *steps[0])
    second, *outgoing2 = call(
        density_kernel,
        [packed] + [((64, lanes), f32)] * 4,
        [table, masses, ((9 * 32, lanes), f32)] + [feats] * 2 + [halves] * 2,
        3,
        (plan, send_offsets, send_counts, columns, distance, self_kernel, own, *received),
        5 * 10**9,
        20,
    )
    smallest, outgoing2 = lax.optimization_barrier((smallest, outgoing2))
    received2 = [swap(value, axis, odd) for value, (axis, odd, _) in zip(outgoing2, swaps)]
    parts = []
    smallest = fold(smallest, *steps[1])
    for first in (0,):
        smallest = fold(smallest, *steps[2])
        weights, damping, dens_col = call(
            functools.partial(weight_kernel, first),
            [((16 * lanes, 8 * lanes), bf16), ((8 * lanes, 8 * lanes), f32), ((8 * lanes, lanes), f32)],
            [table],
            1,
            (plan, columns, distance, rates, self_weight, self_damping, second, own, *received),
            10**9,
            20,
        )
        smallest, distance, weights = lax.optimization_barrier((smallest, distance, weights))
        parts += [weights, damping, dens_col]
    for step in steps[3:]:
        smallest = fold(smallest, *step)
    smallest, received2 = lax.optimization_barrier((smallest, received2))
    accel, heating, density = call(
        momentum_kernel,
        [((3, points), f32), tile, tile],
        [table, masses, table, ((9 * lanes, lanes), f32)]
        + [((lanes, 8 * lanes), bf16)] * 2
        + [halves] * 2,
        1,
        (plan, *parts, own, *received, second, *received2),
        5 * 10**9,
        20,
    )
    size = lax.axis_size("dom")
    moved = [
        lax.ppermute(smallest, "dom", [(i, i ^ step) for i in range(size)]) for step in last
    ]
    for value in moved:
        smallest = jnp.minimum(smallest, value)
    share = smallest / allowed
    return (density.reshape(points), accel, heating.reshape(points), share.reshape(points))


def solution(mesh):
    both = ("slab", "dom")
    wide, flat = P(None, both), P(both)
    in_specs = (wide, wide, flat, flat, flat, wide, wide, wide)
    out_specs = (flat, wide, flat, flat)
    return jax.shard_map(body, mesh=mesh, in_specs=in_specs, out_specs=out_specs, check_vma=False)
```
